32 devices in a mesh: section: 2 (over x), dp: 16 (over z, y, core).
Axes of the slice: x: 2, y: 2, z: 4, core: 2. Of those that a mesh axis runs over, the one named last changes fastest.
Arguments:
- boundary: bfloat16 [2, 64, 13, 13, 512], P('section', 'dp'), may hold values from -6 to 6
- weights: bfloat16 [2, 4608, 512], P('section'), may hold values from -0.09375 to 0.09375
- biases: float32 [2, 512], P('section'), may hold values from -3 to 3
- frame_video: int32 [64], P('dp'), may hold values from 0 to 63
- video_clips: int32 [64], replicated, may hold values from 1 to 25, as said below
Outputs:
- section_results: bfloat16 [2, 64, 13, 13, 512], P('section', 'dp')
- weight_grads: float32 [2, 4608, 512], P('section', 'dp')
- bias_grads: float32 [2, 512], P('section', 'dp')
The draws below stay inside these ranges and needn't reach their ends.
Inputs may be any that keep to these rules, and one draw needn't show every extreme that they name: `video_clips`: each video's clip count.
All inputs are finite; a program needn't handle non-finite values.
Results may differ from the reference program's by a relative error of at most 0.006.
Values may be sent and summed in bfloat16 or wider, within the bound.
A program may use at most 128 MiB of HBM per device.

```python
import math
import jax
import jax.numpy as jnp
import numpy as np
from jax import lax

C = 512
SIDE = 13
FRAMES = 64
VIDEOS = 64


def draw_video_clips(key, part):
    key = jax.random.fold_in(key, 7)
    keys = jax.random.split(key, 4)
    first = jax.random.randint(keys[0], (VIDEOS,), 1, 26)
    second = jax.random.randint(keys[1], (VIDEOS,), 1, 26)
    counts = jnp.minimum(first, second)
    place = jax.random.randint(keys[2], (), 0, VIDEOS)
    other = (place + 1 + jax.random.randint(keys[3], (), 0, VIDEOS - 1)) % VIDEOS
    counts = counts.at[place].set(25)
    counts = counts.at[other].set(1)
    return counts.astype(jnp.int32)


def touch_ends(array, key, low, largest):
    longest = array.shape.index(max(array.shape))
    spots = []
    for shift in (0, 1):
        where = [jax.random.randint(jax.random.fold_in(key, axis), (), 0, length) for axis, length in enumerate(array.shape)]
        where[longest] = (where[longest] + shift) % array.shape[longest]
        spots.append(tuple(where))
    return array.at[spots[0]].set(low).at[spots[1]].set(largest)


def shard_levels(rng, extent, cuts, least, largest):
    def one(position, shards_of):
        draws = jax.random.uniform(jax.random.fold_in(jax.random.fold_in(rng, 6), position), (shards_of,), jnp.float32, least / len(cuts), largest / len(cuts))
        return jnp.repeat(jnp.exp(draws), extent[position] // shards_of).reshape((-1,) + (1,) * (len(extent) - position - 1))

    gain = one(*cuts[0])
    for cut in cuts[1:]:
        gain = gain * one(*cut)
    return gain


def rank_table(number_of, lean):
    loads = [(1 << 20) // math.isqrt(grade ** lean) + 1 for grade in range(1, number_of + 1)]
    deviation = 1 + sum(loads) // (1 << 30)
    return np.cumsum(np.array([max(1, weight // deviation) for weight in loads]))


def ranked(stream_key, dims, count, lean):
    table = rank_table(count, lean)
    ticket = jax.random.randint(jax.random.fold_in(stream_key, 1), dims, 0, int(table[count - 1]))
    standing = jnp.searchsorted(jnp.asarray(table, jnp.int32), ticket, side="right")
    return jax.random.permutation(jax.random.fold_in(stream_key, 2), count)[standing].astype(jnp.int32)


def gaussian(own_key, dims, deviation, reach, cuts=(), kind=jnp.bfloat16):
    array = jax.random.normal(own_key, dims, jnp.float32) * deviation
    if len(cuts) > 0:
        array = shard_levels(own_key, dims, cuts, -0.22, 0.18) * array
    return jnp.clip(array, min=-reach, max=reach).astype(kind)


def setup_inputs(seed: int = 0) -> dict:
    streams_of = jax.random.split(jax.random.key(seed), 6)
    return {
        "boundary": gaussian(streams_of[0], (2, FRAMES, SIDE, SIDE, C), 1.0, 6.0, ((0, 2), (1, 16))),
        "weights": gaussian(streams_of[1], (2, 9 * C, C), (9 * C) ** -0.5, 0.09375, ((0, 2),)),
        "biases": gaussian(streams_of[2], (2, C), 0.5, 3.0, ((0, 2),), jnp.float32),
        "frame_video": touch_ends(ranked(streams_of[3], (FRAMES,), VIDEOS, 2), jax.random.fold_in(streams_of[3], 3), 0, VIDEOS - 1).astype(jnp.int32),
        "video_clips": draw_video_clips(jax.random.fold_in(streams_of[5], 71), 0),
    }


@jax.custom_vjp
def low(v):
    return lax.optimization_barrier(v.astype(jnp.bfloat16)).astype(jnp.float32)

@jax.custom_vjp
def low_back(v):
    return v

def low_keep(v):
    return (low(v), None)

def low_pass(kept, grad):
    return (grad,)

def back_keep(v):
    return (v, None)

def back_low(kept, grad):
    return (low(grad),)
low.defvjp(low_keep, low_pass)
low_back.defvjp(back_keep, back_low)

def convolve(frames, kernel):
    channels = kernel.shape[1]
    shaped = kernel.reshape(3, 3, channels, channels)
    return lax.conv_general_dilated(frames, shaped, (1, 1), 'SAME', dimension_numbers=('NHWC', 'HWIO', 'NHWC'), precision=lax.Precision.HIGHEST)

def forward(frames, kernel_four, offset_four, kernel_five, offset_five):
    preact_four = low_back(convolve(frames, kernel_four) + offset_four)
    hidden = low_back(low(jax.nn.silu(preact_four)))
    preact_five = low_back(convolve(hidden, kernel_five) + offset_five)
    return jax.nn.silu(preact_five)

def reference(boundary, weights, biases, frame_video, video_clips):
    frames = boundary[0].astype(jnp.float32)
    cotangent = boundary[1].astype(jnp.float32)
    kernels = weights.astype(jnp.float32)
    clip_count = video_clips[frame_video].astype(jnp.float32)
    weighting = 1.0 / clip_count
    output, pullback = jax.vjp(forward, frames, kernels[0], biases[0], kernels[1], biases[1])
    grads = pullback(cotangent * weighting[:, None, None, None])
    section_results = jnp.stack([grads[0], output]).astype(jnp.bfloat16)
    weight_grads = jnp.stack([grads[1], grads[3]])
    bias_grads = jnp.stack([grads[2], grads[4]])
    return (section_results, weight_grads, bias_grads)
```

```python
import functools

import jax
import jax.numpy as jnp
from jax import lax
from jax.experimental import pallas as pl
from jax.experimental.pallas import tpu as pltpu
from jax.sharding import PartitionSpec as P

MESH = pl.DeviceIdType.MESH
F32 = jnp.float32
BF16 = jnp.bfloat16
ROW = 16
STEP = 256


def line_sizes(chips):
    sizes = []
    while chips > 1:
        size = 4 if chips % 4 == 0 else 2 if chips % 2 == 0 else chips
        sizes.append(size)
        chips //= size
    return tuple(sizes)


def dest_at(own, step, size):
    rights = size - 1 - own
    low = jnp.where(step < rights, size - 1 - step, step - rights)
    high = jnp.where(step < own, step, size - 1 - (step - own))
    return jnp.where(own < (size + 1) // 2, low, high)


class Plan:
    def __init__(self, frames, side, channels, dp_count, videos):
        self.frames, self.side, self.channels = frames, side, channels
        self.dp_count, self.videos = dp_count, videos
        self.cells = side * side
        self.padded = side * ROW
        self.packed = -(-self.cells // 16) * 16
        self.half = channels // 2
        self.chips = dp_count // 2
        self.lines = line_sizes(self.chips)
        self.rows = 9 * channels // self.chips
        pieces = 2 if self.rows % 32 == 0 else 1
        step = self.rows // pieces
        self.pieces = [(i * step, step) for i in range(pieces)]
        self.last = pieces - 1
        self.wire = self.rows + 16


def kernel(plan, *refs):
    (x_hbm, w_hbm, bias_ref, video_ref, clips_ref, res_hbm, wout, bout,
     w, wt, xin, xs, ds, wd, xt, xo, do, grad, pre, pad32, pack32, stage,
     sent, arrived, bsum, hold, tmp, fin, finb) = refs[:29]
    rest = list(refs[29:])
    lines = plan.lines
    levels = len(lines)
    sendbufs = [rest.pop(0) for _ in range(levels)]
    recvbufs = [rest.pop(0) for _ in range(levels)]
    holds = [rest.pop(0) for _ in range(levels)]
    line_send = [rest.pop(0) for _ in range(levels)]
    line_recv = [rest.pop(0) for _ in range(levels)]
    (load_sem, wload_sem, store_sem, hop_send, hop_recv, xo_send, xo_recv, do_send, do_recv,
     fin_send, fin_recv) = rest

    frames, side, ch, half = plan.frames, plan.side, plan.channels, plan.half
    padded, packed = plan.padded, plan.packed
    sec = lax.axis_index("section")
    me = lax.axis_index("dp")
    core = lax.rem(me, 2)
    chip = lax.div(me, 2)
    coords, strides = [], []
    stride = plan.dp_count
    for size in lines:
        stride //= size
        strides.append(stride)
        coords.append(lax.rem(lax.div(me, stride), size))
    first = sec == 0
    across = (1 - sec, me)
    twin = (sec, me + 1 - 2 * core)

    def load_frame(f):
        return pltpu.make_async_copy(x_hbm.at[0, f], xin.at[f], load_sem.at[f])

    def load_w(a):
        part = pl.ds(3 * ch * a, 3 * ch)
        return pltpu.make_async_copy(w_hbm.at[0, part], w.at[part], wload_sem.at[a])

    load_frame(0).start()
    for a in range(3):
        load_w(a).start()
    for f in range(1, frames):
        load_frame(f).start()

    barrier = pltpu.get_barrier_semaphore()
    pl.semaphore_signal(barrier, inc=1, device_id=across, device_id_type=MESH)
    pl.semaphore_signal(barrier, inc=1, device_id=twin, device_id_type=MESH)
    expected = 2
    for size, own, stride in zip(lines, coords, strides):
        @pl.when(own > 0)
        def _():
            pl.semaphore_signal(barrier, inc=1, device_id=(sec, me - stride), device_id_type=MESH)

        @pl.when(own < size - 1)
        def _():
            pl.semaphore_signal(barrier, inc=1, device_id=(sec, me + stride), device_id_type=MESH)

        expected = expected + (own > 0).astype(jnp.int32) + (own < size - 1).astype(jnp.int32)

    xs[...] = jnp.zeros_like(xs)
    pad32[...] = jnp.zeros_like(pad32)
    pack32[...] = jnp.zeros_like(pack32)
    bsum[...] = jnp.zeros_like(bsum)
    pl.semaphore_wait(barrier, expected)

    row_ids = lax.broadcasted_iota(jnp.int32, (padded, ch), 0)
    real = lax.rem(row_ids, ROW) < side

    def base_of(f):
        return pl.multiple_of(ROW + STEP * f, 16)

    def spread_frame(f):
        for i in range(side):
            pad32[i * ROW : i * ROW + side, :] = xin[f, i].astype(F32)
        return pad32[...]

    def unpack(f):
        pack32[...] = arrived[f].astype(F32)
        for i in range(side):
            pad32[i * ROW : i * ROW + side, :] = pack32[i * side : (i + 1) * side, :]
        return pad32[...]

    def pack(f, value):
        pad32[...] = value
        for i in range(side):
            pack32[i * side : (i + 1) * side, :] = pad32[i * ROW : i * ROW + side, :]
        sent[f] = pack32[...].astype(BF16)
        for i in range(side):
            pad32[i * ROW + side : (i + 1) * ROW, :] = jnp.zeros((ROW - side, ch), F32)

    def shifted(v, distance):
        return pltpu.roll(v, distance % padded, 0).astype(BF16)

    def put_inputs(f, v):
        at = pl.ds(base_of(f), padded)
        xs[at, 0:ch] = shifted(v, 1)
        xs[at, ch : 2 * ch] = v.astype(BF16)
        xs[at, 2 * ch : 3 * ch] = shifted(v, -1)

    def put_deltas(f, v):
        at = pl.ds(base_of(f), padded)
        ds[at, 0:ch] = shifted(v, -1)
        ds[at, ch : 2 * ch] = v.astype(BF16)
        ds[at, 2 * ch : 3 * ch] = shifted(v, 1)

    def put_wd(slot, v):
        at = pl.ds(base_of(slot), padded)
        wd[at, 0:half] = shifted(v, -1)
        wd[at, half : 2 * half] = v.astype(BF16)
        wd[at, 2 * half : 3 * half] = shifted(v, 1)
        bsum[0:1, :] += jnp.sum(v, axis=0, keepdims=True)

    def conv(f):
        total = jnp.zeros((padded, ch), F32)
        for a in range(3):
            at = pl.ds(pl.multiple_of(base_of(f) + ROW * (a - 1), 16), padded)
            total += jnp.dot(xs[at, :], w[3 * ch * a : 3 * ch * (a + 1), :], preferred_element_type=F32)
        return total

    def conv_back(f):
        total = jnp.zeros((padded, ch), F32)
        for a in range(3):
            at = pl.ds(pl.multiple_of(base_of(f) - ROW * (a - 1), 16), padded)
            total += jnp.dot(ds[at, :], wt[3 * ch * a : 3 * ch * (a + 1), :], preferred_element_type=F32)
        return total

    def transpose_w():
        for k in range(9):
            at = slice(ch * k, ch * (k + 1))
            wt[at, :] = w[at, :].T

    def hop(f):
        return pltpu.make_async_remote_copy(
            src_ref=sent.at[f], dst_ref=arrived.at[f], send_sem=hop_send.at[f], recv_sem=hop_recv.at[f],
            device_id=across, device_id_type=MESH)

    def share_input(f):
        return pltpu.make_async_remote_copy(
            src_ref=xs.at[pl.ds(base_of(f), STEP), pl.ds(ch, ch)], dst_ref=xo.at[f],
            send_sem=xo_send.at[f], recv_sem=xo_recv.at[f], device_id=twin, device_id_type=MESH)

    def share_delta(f):
        lane = pl.multiple_of(ch + half * (1 - core), 128)
        return pltpu.make_async_remote_copy(
            src_ref=ds.at[pl.ds(base_of(f), padded), pl.ds(lane, half)], dst_ref=do.at[f],
            send_sem=do_send.at[f], recv_sem=do_recv.at[f], device_id=twin, device_id_type=MESH)

    def store_result(f):
        return pltpu.make_async_copy(stage.at[f], res_hbm.at[0, f], store_sem.at[f])

    def put_result(f, v):
        for i in range(side):
            stage[f, i] = v[i * ROW : i * ROW + side, :].astype(BF16)
        store_result(f).start()

    def own_half(f):
        lane = pl.multiple_of(ch + half * core, 128)
        return ds[pl.ds(base_of(f), padded), pl.ds(lane, half)].astype(F32)

    def delta_ready(f, v):
        put_deltas(f, v)
        share_delta(f).start()
        put_wd(2 * f, own_half(f))

    def other_delta(f):
        share_delta(f).wait_recv()
        put_wd(2 * f + 1, do[f].astype(F32))

    def transpose_own(f):
        xt[2 * f] = xs[pl.ds(base_of(f), STEP), ch : 2 * ch].T

    def transpose_other(f):
        share_input(f).wait_recv()
        xt[2 * f + 1] = xo[f].T

    def weight_term(slot, a):
        at = pl.ds(pl.multiple_of(base_of(slot) - ROW * (a - 1), 16), STEP)
        return jnp.dot(xt[slot], wd[at, :], preferred_element_type=F32)

    def weight_terms(slot):
        for a in range(3):
            term = weight_term(slot, a)
            for b in range(3):
                at = slice(ch * (3 * a + b), ch * (3 * a + b + 1))
                grad[at, :] += term[:, half * b : half * (b + 1)]

    def each(body):
        lax.fori_loop(0, frames, lambda f, c: (body(f), c)[1], 0)

    def clear():
        ds[...] = jnp.zeros_like(ds)
        wd[...] = jnp.zeros_like(wd)
        grad[...] = jnp.zeros_like(grad)

    @pl.when(first)
    def _():
        for a in range(3):
            load_w(a).wait()

        def forward(f):
            load_frame(f).wait()
            put_inputs(f, spread_frame(f))
            value = conv(f) + bias_ref[...]
            pre[f] = value
            pack(f, value / (1.0 + jnp.exp(-value)))
            hop(f).start()
            share_input(f).start()

        each(forward)
        clear()
        transpose_w()
        each(transpose_own)
        each(transpose_other)

        def backward(f):
            hop(f).wait_recv()
            v = pre[f]
            s = 1.0 / (1.0 + jnp.exp(-v))
            d = unpack(f) * (s * (1.0 + v * (1.0 - s)))
            d = jnp.where(real, d, 0.0).astype(BF16).astype(F32)
            delta_ready(f, d)
            weight_terms(2 * f)
            other_delta(f)
            weight_terms(2 * f + 1)

        each(backward)

    @pl.when(jnp.logical_not(first))
    def _():
        for a in range(3):
            load_w(a).wait()
        transpose_w()
        clear()

        def both(f):
            load_frame(f).wait()
            hop(f).wait_recv()
            put_inputs(f, unpack(f))
            share_input(f).start()
            v = conv(f) + bias_ref[...]
            s = 1.0 / (1.0 + jnp.exp(-v))
            put_result(f, v * s)
            clip = clips_ref[video_ref[f]].astype(F32)
            weighting = 1.0 / jnp.full((1, ch), clip, F32)
            d = (spread_frame(f) * weighting) * (s * (1.0 + v * (1.0 - s)))
            d = jnp.where(real, d, 0.0).astype(BF16).astype(F32)
            delta_ready(f, d)
            pack(f, conv_back(f))
            hop(f).start()
            transpose_own(f)

        each(both)

        def terms(f):
            transpose_other(f)
            other_delta(f)
            weight_terms(2 * f)
            weight_terms(2 * f + 1)

        each(terms)

    wire = plan.wire

    def to_wire(value, bias):
        if bias is None:
            return value.astype(BF16)
        high = bias.astype(BF16).astype(F32)
        ids = lax.broadcasted_iota(jnp.int32, (16, half), 0)
        more = jnp.where(ids == 0, high, jnp.where(ids == 1, bias - high, 0.0))
        return jnp.concatenate([value, more], axis=0).astype(BF16)

    def piece_of(ref, index, piece):
        start, size = plan.pieces[piece]
        value = ref[index, start : start + size, :].astype(F32)
        if piece != plan.last:
            return value, None
        return value, jnp.sum(ref[index, plan.rows : plan.rows + 16, :].astype(F32), axis=0, keepdims=True)

    def extent(piece):
        start, size = plan.pieces[piece]
        return pl.ds(start, size + (16 if piece == plan.last else 0))

    def line_copy(level, flat, piece, right):
        side_at = jnp.where(right, 0, 1)
        to = jnp.where(right, me + strides[level], me - strides[level])
        return pltpu.make_async_remote_copy(
            src_ref=sendbufs[level].at[flat, extent(piece)],
            dst_ref=recvbufs[level].at[side_at, flat, extent(piece)],
            send_sem=line_send[level].at[flat, piece], recv_sem=line_recv[level].at[side_at, flat, piece],
            device_id=(sec, to), device_id_type=MESH)

    def line_wait(level, flat, piece, side_at):
        pltpu.make_async_remote_copy(
            src_ref=sendbufs[level].at[flat, extent(piece)],
            dst_ref=recvbufs[level].at[side_at, flat, extent(piece)],
            send_sem=line_send[level].at[flat, piece], recv_sem=line_recv[level].at[side_at, flat, piece],
            device_id=twin, device_id_type=MESH).wait_recv()

    def put_acc(ref, piece, value, bias):
        start, size = plan.pieces[piece]
        ref[start : start + size, :] = value
        if bias is not None:
            ref[plan.rows : plan.rows + 1, :] = bias

    def get_acc(ref, piece):
        start, size = plan.pieces[piece]
        bias = ref[plan.rows : plan.rows + 1, :] if piece == plan.last else None
        return ref[start : start + size, :], bias

    def add_arrived(ref, level, flat, piece, side_at):
        line_wait(level, flat, piece, side_at)
        start, size = plan.pieces[piece]
        value, bias = piece_of(recvbufs[level].at[side_at], flat, piece)
        ref[start : start + size, :] += value
        if bias is not None:
            ref[plan.rows : plan.rows + 1, :] += bias

    def leaf(flat, piece):
        start, size = plan.pieces[piece]
        at = pl.ds(pl.multiple_of(flat * plan.rows + start, 16), size)
        return grad[at, :], (bsum[0:1, :] if piece == plan.last else None)

    def send(level, flat, piece, value, bias, right):
        sendbufs[level][flat, extent(piece), :] = to_wire(value, bias)
        line_copy(level, flat, piece, right).start()

    def reduced(level, before, piece):
        size, own = lines[level], coords[level]
        leafy = level == levels - 1
        early = leafy and size == 2
        for step in range(size):
            dest = dest_at(own, step, size)
            flat = before * size + dest
            if step < size - 1 and early:
                continue
            if leafy:
                value, bias = leaf(flat, piece)
            else:
                reduced(level + 1, flat, piece)
                value, bias = get_acc(holds[level + 1], piece)
            if step < size - 1:
                put_acc(tmp, piece, value, bias)
                right = dest > own

                @pl.when(jnp.logical_and(right, own > 0))
                def _():
                    add_arrived(tmp, level, flat, piece, 0)

                @pl.when(jnp.logical_and(jnp.logical_not(right), own < size - 1))
                def _():
                    add_arrived(tmp, level, flat, piece, 1)

                value, bias = get_acc(tmp, piece)
                send(level, flat, piece, value, bias, right)
            else:
                put_acc(holds[level], piece, value, bias)

                @pl.when(own > 0)
                def _():
                    add_arrived(holds[level], level, flat, piece, 0)

                @pl.when(own < size - 1)
                def _():
                    add_arrived(holds[level], level, flat, piece, 1)

    def early_sends(level, before, piece):
        size, own = lines[level], coords[level]
        if level == levels - 1:
            if size == 2:
                dest = 1 - own
                flat = before * size + dest
                value, bias = leaf(flat, piece)
                send(level, flat, piece, value, bias, dest > own)
            return
        for step in range(size):
            early_sends(level + 1, before * size + dest_at(own, step, size), piece)

    def top_steps(body):
        size, own = lines[0], coords[0]
        for step in range(size):
            for piece in range(len(plan.pieces)):
                body(step, dest_at(own, step, size), piece)

    if levels == 1:
        for piece in range(len(plan.pieces)):
            early_sends(0, 0, piece)
    else:
        top_steps(lambda step, dest, piece: early_sends(1, dest, piece))

    @pl.when(first)
    def _():
        def back(f):
            put_result(f, conv_back(f))

        each(back)

    def top(step, dest, piece):
        size, own = lines[0], coords[0]
        reduced(1, dest, piece)
        value, bias = get_acc(holds[1], piece)
        if step < size - 1:
            put_acc(tmp, piece, value, bias)
            right = dest > own

            @pl.when(jnp.logical_and(right, own > 0))
            def _():
                add_arrived(tmp, 0, dest, piece, 0)

            @pl.when(jnp.logical_and(jnp.logical_not(right), own < size - 1))
            def _():
                add_arrived(tmp, 0, dest, piece, 1)

            value, bias = get_acc(tmp, piece)
            send(0, dest, piece, value, bias, right)
        else:
            put_acc(holds[0], piece, value, bias)

    if levels == 1:
        for piece in range(len(plan.pieces)):
            reduced(0, 0, piece)
    else:
        top_steps(top)
        size, own = lines[0], coords[0]
        for piece in range(len(plan.pieces)):
            @pl.when(own > 0)
            def _():
                add_arrived(holds[0], 0, own, piece, 0)

            @pl.when(own < size - 1)
            def _():
                add_arrived(holds[0], 0, own, piece, 1)

    mine = plan.rows // 2
    total = holds[0]
    fin[...] = total[pl.ds(pl.multiple_of((1 - core) * mine, 8), mine), :]
    finb[0, 0:1, :] = total[plan.rows : plan.rows + 1, :]
    lane = pl.multiple_of(half * core, 128)
    swap = pltpu.make_async_remote_copy(
        src_ref=fin, dst_ref=wout.at[0, :, pl.ds(lane, half)], send_sem=fin_send.at[0], recv_sem=fin_recv.at[0],
        device_id=twin, device_id_type=MESH)
    swapb = pltpu.make_async_remote_copy(
        src_ref=finb.at[0], dst_ref=finb.at[1], send_sem=fin_send.at[1], recv_sem=fin_recv.at[1],
        device_id=twin, device_id_type=MESH)
    swap.start()
    swapb.start()
    wout[0, :, pl.ds(lane, half)] = total[pl.ds(pl.multiple_of(core * mine, 8), mine), :]
    swapb.wait_recv()
    share = ch // plan.dp_count
    begin = me * share
    mine_has = (begin >= half) == (core == 1)
    row = jnp.where(mine_has, finb[0, 0:8, :], finb[1, 0:8, :])
    place = lax.rem(begin, half)
    bout[...] = pltpu.roll(row, lax.rem(half - place, half), 1)[0:1, 0:share]
    swap.wait_recv()

    swap.wait_send()
    swapb.wait_send()

    def finish(f):
        hop(f).wait_send()
        share_input(f).wait_send()
        share_delta(f).wait_send()
        store_result(f).wait()

    each(finish)

    @pl.when(first)
    def _():
        pass

    def drain(level, before, piece):
        size, own = lines[level], coords[level]
        for step in range(size):
            dest = dest_at(own, step, size)
            flat = before * size + dest
            if level < levels - 1:
                drain(level + 1, flat, piece)
            if step < size - 1:
                line_copy(level, flat, piece, dest > own).wait_send()

    for piece in range(len(plan.pieces)):
        drain(0, 0, piece)


def body(boundary, weights, biases, frame_video, video_clips):
    frames, side, ch = boundary.shape[1], boundary.shape[2], boundary.shape[4]
    dp_count = lax.axis_size("dp")
    plan = Plan(frames, side, ch, dp_count, video_clips.shape[0])
    half, padded, packed = plan.half, plan.padded, plan.packed
    rows = STEP * frames + 2 * ROW
    wide = STEP * 2 * frames + 2 * ROW
    vmem = lambda *shape, dtype=BF16: pltpu.VMEM(shape, dtype)
    counts = []
    count = 1
    for size in plan.lines:
        count *= size
        counts.append(count)
    pieces = len(plan.pieces)
    dma = pltpu.SemaphoreType.DMA
    acc_rows = plan.rows + 8
    scratch = [
        vmem(9 * ch, ch),
        vmem(9 * ch, ch),
        vmem(frames, side, side, ch),
        vmem(rows, 3 * ch),
        vmem(rows, 3 * ch),
        vmem(wide, 3 * half),
        vmem(2 * frames, ch, STEP),
        vmem(frames, STEP, ch),
        vmem(frames, padded, half),
        vmem(9 * ch, half, dtype=F32),
        vmem(frames, padded, ch, dtype=F32),
        vmem(padded, ch, dtype=F32),
        vmem(packed, ch, dtype=F32),
        vmem(frames, side, side, ch),
        vmem(frames, packed, ch),
        vmem(frames, packed, ch),
        vmem(8, half, dtype=F32),
        vmem(8, 128, dtype=F32),
        vmem(acc_rows, half, dtype=F32),
        vmem(plan.rows // 2, half, dtype=F32),
        vmem(2, 8, half, dtype=F32),
    ]
    scratch += [vmem(n, plan.wire, half) for n in counts]
    scratch += [vmem(2, n, plan.wire, half) for n in counts]
    scratch += [vmem(acc_rows, half, dtype=F32) for n in counts]
    scratch += [dma((n, pieces)) for n in counts]
    scratch += [dma((2, n, pieces)) for n in counts]
    scratch += [dma((frames,)), dma((3,)), dma((frames,))]
    scratch += [dma((frames,)) for _ in range(6)]
    scratch += [dma((2,)), dma((2,))]
    any_space = pl.BlockSpec(memory_space=pl.ANY)
    whole = pl.BlockSpec(memory_space=pltpu.VMEM)
    scalars = pl.BlockSpec(memory_space=pltpu.SMEM)
    share = 9 * ch // dp_count
    return pl.pallas_call(
        functools.partial(kernel, plan),
        out_shape=(
            jax.ShapeDtypeStruct(boundary.shape, BF16),
            jax.ShapeDtypeStruct((1, share, ch), F32),
            jax.ShapeDtypeStruct((1, ch // dp_count), F32),
        ),
        in_specs=[any_space, any_space, whole, scalars, scalars],
        out_specs=(any_space, whole, whole),
        scratch_shapes=scratch,
        compiler_params=pltpu.CompilerParams(
            collective_id=0, has_side_effects=True, vmem_limit_bytes=58 * 1024 * 1024
        ),
    )(boundary, weights, biases, frame_video, video_clips)


def solution(mesh):
    return jax.shard_map(
        body,
        mesh=mesh,
        in_specs=(
            P("section", "dp", None, None, None),
            P("section", None, None),
            P("section", None),
            P("dp"),
            P(),
        ),
        out_specs=(
            P("section", "dp", None, None, None),
            P("section", "dp", None),
            P("section", "dp"),
        ),
        check_vma=False,
    )
```

```python
import functools

import jax
import jax.numpy as jnp
from jax import lax
from jax.experimental import pallas as pl
from jax.experimental.pallas import tpu as pltpu
from jax.sharding import PartitionSpec as P

VMEM_LIMIT = 48 * 1024 * 1024
MESH = pl.DeviceIdType.MESH
F32 = jnp.float32
BF16 = jnp.bfloat16
SLOTS = 16
AHEAD = (0, 2, 5, 8, 11, 13)
BACK = (0, 3, 6, 9, 11, 13)
LATE = 8


def line_sizes(chips):
    sizes = []
    while chips > 1:
        size = 4 if chips % 4 == 0 else 2 if chips % 2 == 0 else chips
        sizes.append(size)
        chips //= size
    return tuple(sizes)


def dest_at(own, step, size):
    rights = size - 1 - own
    low = jnp.where(step < rights, size - 1 - step, step - rights)
    high = jnp.where(step < own, step, size - 1 - (step - own))
    return jnp.where(own < (size + 1) // 2, low, high)


class Plan:
    def __init__(self, frames, side, channels, dp_count):
        self.frames, self.side, self.channels, self.dp_count = frames, side, channels, dp_count
        self.group = SLOTS * frames
        self.cells = side * frames
        self.half = channels // 2
        self.chips = dp_count // 2
        self.lines = line_sizes(self.chips)
        self.rows = 9 * channels // self.chips
        self.mine = self.rows // 2
        levels = len(self.lines)
        inner_first = tuple(reversed(range(levels)))
        outer_first = tuple(range(levels))
        self.pieces = []
        for keeper in range(2):
            if self.mine % 96 == 0 and levels == 2:
                sixteenths = self.mine // 16
                turned = sixteenths // 6
                part = (sixteenths - turned) // 2
                cuts = [(part, inner_first), (sixteenths - turned - part, inner_first), (turned, outer_first)]
                begin = 0
                for size, order in cuts:
                    self.pieces.append((keeper, begin, 16 * size, order))
                    begin += 16 * size
            else:
                self.pieces.append((keeper, 0, self.mine, inner_first))
        self.wire = BF16 if all(size % 16 == 0 and begin % 16 == 0 for _, begin, size, _ in self.pieces) else F32

    def slots(self, piece, stage):
        order = self.pieces[piece][3]
        count = 1
        for line in order[stage:]:
            count *= self.lines[line]
        return count

    def arrivals(self, piece, stage):
        size = self.lines[self.pieces[piece][3][stage]]
        after = self.slots(piece, stage) // size
        return after if size == 2 else (size + 1) * after


def kernel(plan, *refs):
    (x_hbm, w_hbm, bias_hbm, video_hbm, clips_hbm, res, wout, bout,
     w, wt, xin, xs, ds, wd, xt, xc, do, grad, pre, pad,
     sent, arrived, bsum, scale, bias_ref, video_ref, clips_ref, bias_in) = refs[:28]
    rest = list(refs[28:])
    lines, pieces = plan.lines, plan.pieces
    levels = len(lines)

    def take(count):
        taken = rest[:count]
        del rest[:count]
        return taken

    out_bufs = [take(levels) for _ in pieces]
    in_bufs = [take(levels) for _ in pieces]
    sums = [take(levels) for _ in pieces]
    last_in = take(len(pieces))
    line_send = take(len(pieces))
    line_recv = [take(levels) for _ in pieces]
    last_recv = take(len(pieces))
    (load_sem, wload_sem, small_sem, ahead_send, ahead_recv, back_send, back_recv, xc_send, xc_recv, do_send, do_recv,
     keep_send, keep_recv, bias_send, bias_recv) = rest

    frames, side, ch, half = plan.frames, plan.side, plan.channels, plan.half
    group, cells = plan.group, plan.cells
    sec = lax.axis_index("section")
    me = lax.axis_index("dp")
    core = lax.rem(me, 2)
    coords, strides = [], []
    stride = plan.dp_count
    for size in lines:
        stride //= size
        strides.append(stride)
        coords.append(lax.rem(lax.div(me, stride), size))
    first = sec == 0
    across = (1 - sec, me)
    twin = (sec, me + 1 - 2 * core)

    def load_rows(k):
        begin, end = ((0, 3), (3, side))[k]
        return pltpu.make_async_copy(x_hbm.at[0, begin:end], xin.at[begin:end], load_sem.at[k])

    def load_w(a):
        part = pl.ds(3 * ch * a, 3 * ch)
        return pltpu.make_async_copy(w_hbm.at[0, part], w.at[part], wload_sem.at[a])

    def load_small(k):
        source, to = ((bias_hbm, bias_ref), (video_hbm, video_ref), (clips_hbm, clips_ref))[k]
        return pltpu.make_async_copy(source, to, small_sem.at[k])

    load_rows(0).start()
    for a in range(3):
        load_w(a).start()
    load_rows(1).start()
    for k in range(3):
        load_small(k).start()

    barrier = pltpu.get_barrier_semaphore()
    for device in (across, twin):
        pl.semaphore_signal(barrier, inc=1, device_id=device, device_id_type=MESH)
    greeted = 2
    for own, size, stride in zip(coords, lines, strides):
        for there, exists in ((me - stride, own > 0), (me + stride, own < size - 1)):
            @pl.when(exists)
            def _():
                for device in (there, there + 1 - 2 * core):
                    pl.semaphore_signal(barrier, inc=1, device_id=(sec, device), device_id_type=MESH)

            greeted = greeted + 2 * exists.astype(jnp.int32)

    for ref in (xs, ds):
        ref[0:group, :] = jnp.zeros((group, 3 * ch), BF16)
        ref[(side + 1) * group : (side + 2) * group, :] = jnp.zeros((group, 3 * ch), BF16)
    xt[:, 0 : 2 * group] = jnp.zeros((ch, 2 * group), BF16)
    xt[:, (side + 1) * 2 * group : (side + 2) * 2 * group] = jnp.zeros((ch, 2 * group), BF16)
    pad[...] = jnp.zeros_like(pad)
    bsum[...] = jnp.zeros_like(bsum)

    def spread(ref, begin, end):
        for i in range(begin, end):
            pad[i * group : i * group + cells, :] = ref[i].astype(F32).reshape(cells, ch)
        return pad[begin * group : end * group, :]

    def gather(ref, begin, end, value):
        for i in range(begin, end):
            at = (i - begin) * group
            ref[i] = value[at : at + cells, :].reshape(side, frames, ch).astype(BF16)

    def real(rows):
        ids = lax.broadcasted_iota(jnp.int32, (rows * group, ch), 0)
        return lax.rem(ids, group) < cells

    def moved(v, slots):
        return pltpu.roll(v, slots * frames % v.shape[0], 0).astype(BF16)

    def put_inputs(begin, end, v):
        at = slice((begin + 1) * group, (end + 1) * group)
        middle = v.astype(BF16)
        xs[at, 0:ch] = moved(v, 1)
        xs[at, ch : 2 * ch] = middle
        xs[at, 2 * ch : 3 * ch] = moved(v, -1)
        xc[begin:end, 0] = middle.reshape(end - begin, group, ch)

    def put_deltas(begin, end, v):
        at = slice((begin + 1) * group, (end + 1) * group)
        ds[at, 0:ch] = moved(v, -1)
        ds[at, ch : 2 * ch] = v.astype(BF16)
        ds[at, 2 * ch : 3 * ch] = moved(v, 1)

    def put_halves(begin, end, which, v):
        parts = (moved(v, -1), v.astype(BF16), moved(v, 1))
        for i in range(begin, end):
            at = slice((2 * i + which) * group, (2 * i + which + 1) * group)
            for b in range(3):
                wd[at, half * b : half * (b + 1)] = parts[b][(i - begin) * group : (i - begin + 1) * group, :]
        bsum[0:1, :] += jnp.sum(v, axis=0, keepdims=True)

    def product(source, factor, begin, end, sign):
        total = jnp.zeros(((end - begin) * group, ch), F32)
        for a in range(3):
            at = (begin + 1 + sign * (a - 1)) * group
            total += jnp.dot(source[at : at + (end - begin) * group, :], factor[3 * ch * a : 3 * ch * (a + 1), :],
                             preferred_element_type=F32)
        return total

    def conv(begin, end):
        return product(xs, w, begin, end, 1) + bias_ref[...]

    def conv_back(begin, end):
        return product(ds, wt, begin, end, -1)

    def transpose_w():
        for k in range(9):
            at = slice(ch * k, ch * (k + 1))
            wt[at, :] = w[at, :].T

    def hop(bounds, sems, k):
        rows = pl.ds(bounds[k], bounds[k + 1] - bounds[k])
        return pltpu.make_async_remote_copy(
            src_ref=sent.at[rows], dst_ref=arrived.at[rows], send_sem=sems[0].at[0], recv_sem=sems[1].at[k],
            device_id=across, device_id_type=MESH)

    def ahead(k):
        return hop(AHEAD, (ahead_send, ahead_recv), k)

    def back(k):
        return hop(BACK, (back_send, back_recv), k)

    def share_inputs(k):
        rows = pl.ds(AHEAD[k], AHEAD[k + 1] - AHEAD[k])
        return pltpu.make_async_remote_copy(
            src_ref=xc.at[rows, 0], dst_ref=xc.at[rows, 1], send_sem=xc_send.at[0], recv_sem=xc_recv.at[k],
            device_id=twin, device_id_type=MESH)

    def share_deltas(k, begin, end):
        lane = pl.multiple_of(ch + half * (1 - core), 128)
        return pltpu.make_async_remote_copy(
            src_ref=ds.at[pl.ds((begin + 1) * group, (end - begin) * group), pl.ds(lane, half)],
            dst_ref=do.at[pl.ds(begin * group, (end - begin) * group)],
            send_sem=do_send.at[0], recv_sem=do_recv.at[k], device_id=twin, device_id_type=MESH)

    def own_deltas(begin, end):
        lane = pl.multiple_of(ch + half * core, 128)
        own = ds[(begin + 1) * group : (end + 1) * group, pl.ds(lane, half)]
        put_halves(begin, end, 0, own.astype(F32))

    def other_deltas(k, begin, end):
        share_deltas(k, begin, end).wait_recv()
        put_halves(begin, end, 1, do[begin * group : end * group, :].astype(F32))

    def transpose_inputs():
        for k in range(len(AHEAD) - 1):
            share_inputs(k).wait_recv()
        for begin in range(0, side, 2):
            end = min(begin + 2, side)
            part = xc[begin:end].reshape((end - begin) * 2 * group, ch)
            xt[:, (begin + 1) * 2 * group : (end + 1) * 2 * group] = part.T

    def weight_terms(begin, end, fresh):
        wide = 2 * group
        for a in range(3):
            term = jnp.dot(xt[:, (begin + a) * wide : (end + a) * wide], wd[begin * wide : end * wide, :],
                           preferred_element_type=F32)
            for b in range(3):
                at = slice(ch * (3 * a + b), ch * (3 * a + b + 1))
                part = term[:, half * b : half * (b + 1)]
                grad[at, :] = part if fresh else grad[at, :] + part

    def sigmoid(v):
        return 1.0 / (1.0 + jnp.exp(-v))

    for k in range(3):
        load_small(k).wait()

    def ahead_rows(k):
        begin, end = AHEAD[k], AHEAD[k + 1]
        v = conv(begin, end)
        pre[begin * group : end * group, :] = v
        gather(sent, begin, end, v * sigmoid(v))

    @pl.when(first)
    def _():
        load_rows(0).wait()
        put_inputs(0, 3, spread(xin, 0, 3))
        for a in range(3):
            load_w(a).wait()
        ahead_rows(0)

    @pl.when(jnp.logical_not(first))
    def _():
        ids = lax.rem(lax.broadcasted_iota(jnp.int32, (group, ch), 0), frames)
        per_row = jnp.zeros((group, ch), F32)
        for f in range(frames):
            clip = clips_ref[video_ref[f]].astype(F32)
            per_row = jnp.where(ids == f, 1.0 / jnp.full((1, ch), clip, F32), per_row)
        scale[...] = per_row
        for a in range(3):
            load_w(a).wait()
        transpose_w()
        load_rows(0).wait()

    load_rows(1).wait()
    pl.semaphore_wait(barrier, greeted)

    @pl.when(first)
    def _():
        ahead(0).start()
        put_inputs(3, side, spread(xin, 3, side))
        share_inputs(0).start()
        for k in range(1, len(AHEAD) - 1):
            ahead_rows(k)
            ahead(k).start()
            share_inputs(k).start()
        transpose_w()
        transpose_inputs()

        done = 0
        for k, (begin, end) in enumerate(zip(BACK, BACK[1:])):
            back(k).wait_recv()
            v = pre[begin * group : end * group, :]
            s = sigmoid(v)
            d = spread(arrived, begin, end) * (s * (1.0 + v * (1.0 - s)))
            d = jnp.where(real(end - begin), d, 0.0).astype(BF16).astype(F32)
            put_deltas(begin, end, d)
            share_deltas(k, begin, end).start()
            own_deltas(begin, end)
            if end - 1 <= LATE:
                gather(res.at[0], done, end - 1, conv_back(done, end - 1))
                done = end - 1
            other_deltas(k, begin, end)
            weight_terms(begin, end, k == 0)

    @pl.when(jnp.logical_not(first))
    def _():
        rows_of = []
        done, next_back = 0, 0
        for k, (begin, end) in enumerate(zip(AHEAD, AHEAD[1:])):
            ahead(k).wait_recv()
            put_inputs(begin, end, spread(arrived, begin, end))
            share_inputs(k).start()
            top = side if end == side else end - 1
            v = conv(done, top)
            s = sigmoid(v)
            g = spread(xin, done, top).reshape(top - done, group, ch) * scale[...]
            d = g.reshape((top - done) * group, ch) * (s * (1.0 + v * (1.0 - s)))
            d = jnp.where(real(top - done), d, 0.0).astype(BF16).astype(F32)
            put_deltas(done, top, d)
            rows_of.append((done, top))
            begin, done = done, top
            while next_back < len(BACK) - 1 and (BACK[next_back + 1] < done or done == side):
                low, high = BACK[next_back], BACK[next_back + 1]
                gather(sent, low, high, conv_back(low, high))
                back(next_back).start()
                next_back += 1
            share_deltas(k, begin, done).start()
            own_deltas(begin, done)
            gather(res.at[0], begin, done, v * s)
        transpose_inputs()
        for k, (begin, end) in enumerate(rows_of):
            other_deltas(k, begin, end)
        weight_terms(0, side, True)

    def arrival_at(piece, stage, slot, side_at):
        size = lines[pieces[piece][3][stage]]
        after = plan.slots(piece, stage) // size
        if size == 2:
            return lax.rem(slot, after)
        own = lax.div(slot, after) == coords[pieces[piece][3][stage]]
        return jnp.where(jnp.logical_and(own, side_at == 1), size * after + lax.rem(slot, after), slot)

    def line_copy(piece, stage, slot, dest, final=False):
        keeper, _, size, order = pieces[piece]
        line = order[stage]
        right = dest > coords[line]
        side_at = jnp.where(right, 0, 1)
        to = me + jnp.where(right, strides[line], -strides[line])
        if final:
            to = to - core + keeper
            at = 0 if lines[line] == 2 else side_at
            target, sem = last_in[piece].at[at, core], last_recv[piece].at[at, core]
        else:
            there = dest == coords[line] + jnp.where(right, 1, -1)
            after = plan.slots(piece, stage) // lines[line]
            if lines[line] == 2:
                at = lax.rem(slot, after)
            else:
                second = jnp.logical_and(there, jnp.logical_not(right))
                at = jnp.where(second, lines[line] * after + lax.rem(slot, after), slot)
            target, sem = in_bufs[piece][stage].at[at], line_recv[piece][stage].at[at]
        return pltpu.make_async_remote_copy(
            src_ref=out_bufs[piece][stage].at[slot], dst_ref=target,
            send_sem=line_send[piece].at[stage], recv_sem=sem, device_id=(sec, to), device_id_type=MESH)

    def arrival(piece, stage, slot, side_at):
        at = arrival_at(piece, stage, slot, side_at)
        pltpu.make_async_remote_copy(
            src_ref=out_bufs[piece][stage].at[slot], dst_ref=in_bufs[piece][stage].at[at],
            send_sem=line_send[piece].at[stage], recv_sem=line_recv[piece][stage].at[at],
            device_id=twin, device_id_type=MESH).wait_recv()
        return in_bufs[piece][stage][at].astype(F32)

    def last_arrival(piece, side_at, columns):
        at = 0 if lines[pieces[piece][3][levels - 1]] == 2 else side_at
        pltpu.make_async_remote_copy(
            src_ref=out_bufs[piece][levels - 1].at[0], dst_ref=last_in[piece].at[at, columns],
            send_sem=line_send[piece].at[levels - 1], recv_sem=last_recv[piece].at[at, columns],
            device_id=twin, device_id_type=MESH).wait_recv()
        return last_in[piece][at, columns].astype(F32)

    def send_on(piece, stage, slot, dest):
        line = pieces[piece][3][stage]
        if stage < levels - 1:
            line_copy(piece, stage, slot, dest).start()
            return
        next_to = jnp.abs(dest - coords[line]) == 1

        @pl.when(next_to)
        def _():
            line_copy(piece, stage, slot, dest, True).start()

        @pl.when(jnp.logical_not(next_to))
        def _():
            line_copy(piece, stage, slot, dest).start()

    def leaf(piece, slot):
        keeper, begin, size, order = pieces[piece]
        left, chip = slot, 0
        for line in reversed(order):
            chip = chip + lax.rem(left, lines[line]) * (strides[line] // 2)
            left = lax.div(left, lines[line])
        at = chip * plan.rows + keeper * plan.mine + begin
        return grad[pl.ds(pl.multiple_of(at, 8), size), :]

    def dest_slot(piece, stage, rest_slot, step):
        line = pieces[piece][3][stage]
        dest = dest_at(coords[line], step, lines[line])
        after = plan.slots(piece, stage) // lines[line]
        return dest, dest * after + rest_slot

    def is_early(piece, stage):
        return stage == 0 and lines[pieces[piece][3][0]] == 2

    def early_send(piece, rest_slot):
        dest, slot = dest_slot(piece, 0, rest_slot, 0)
        out_bufs[piece][0][slot] = leaf(piece, slot).astype(plan.wire)
        send_on(piece, 0, slot, dest)

    def line_step(piece, stage, rest_slot, step):
        line = pieces[piece][3][stage]
        size, own = lines[line], coords[line]
        if step < size - 1 and is_early(piece, stage):
            return
        dest, slot = dest_slot(piece, stage, rest_slot, step)
        if stage == 0:
            value = leaf(piece, slot)
        else:
            value = summed(piece, stage - 1, slot)
        total = sums[piece][stage]
        if step < size - 1:
            right = dest > own
            upstream = jnp.logical_or(jnp.logical_and(right, own > 0), jnp.logical_and(jnp.logical_not(right), own < size - 1))

            @pl.when(upstream)
            def _():
                both = value + arrival(piece, stage, slot, jnp.where(right, 0, 1))
                out_bufs[piece][stage][slot] = both.astype(plan.wire)

            @pl.when(jnp.logical_not(upstream))
            def _():
                out_bufs[piece][stage][slot] = value.astype(plan.wire)

            send_on(piece, stage, slot, dest)
        else:
            total[...] = value
            if stage < levels - 1:
                @pl.when(own > 0)
                def _():
                    total[...] += arrival(piece, stage, slot, 0)

                @pl.when(own < size - 1)
                def _():
                    total[...] += arrival(piece, stage, slot, 1)

    pending = set()

    def summed(piece, stage, rest_slot):
        if (piece, stage) not in pending:
            for step in range(lines[pieces[piece][3][stage]]):
                line_step(piece, stage, rest_slot, step)
        return sums[piece][stage][...]

    def keep_copy(piece):
        keeper, begin, size, _ = pieces[piece]
        return pltpu.make_async_remote_copy(
            src_ref=sums[piece][levels - 1],
            dst_ref=wout.at[0, begin : begin + size, half * (1 - keeper) : half * (2 - keeper)],
            send_sem=keep_send.at[0], recv_sem=keep_recv.at[piece % (len(pieces) // 2)], device_id=twin, device_id_type=MESH)

    def keep(piece):
        keeper, begin, size, _ = pieces[piece]

        @pl.when(core == keeper)
        def _():
            wout[0, begin : begin + size, half * keeper : half * (keeper + 1)] = sums[piece][levels - 1][...]

        @pl.when(core != keeper)
        def _():
            keep_copy(piece).start()

    def finish(piece):
        keeper, begin, size, order = pieces[piece]
        line = order[levels - 1]
        own = coords[line]

        @pl.when(core == keeper)
        def _():
            keep_copy(piece).wait_recv()

            def add(side_at):
                for columns in range(2):
                    wout[0, begin : begin + size, half * columns : half * (columns + 1)] += last_arrival(piece, side_at, columns)

            pl.when(own > 0)(lambda: add(0))
            pl.when(own < lines[line] - 1)(lambda: add(1))

    def bias_copy(line, right):
        way = 0 if right else 1
        return pltpu.make_async_remote_copy(
            src_ref=bias_in.at[line, 1 + way], dst_ref=bias_in.at[line, 3 + way],
            send_sem=bias_send.at[line, way], recv_sem=bias_recv.at[line, way],
            device_id=(sec, me + strides[line] * (1 if right else -1)), device_id_type=MESH)

    def bias_step(line, step):
        own, size = coords[line], lines[line]
        for right in (True, False):
            way = 0 if right else 1

            @pl.when(own == (step if right else size - 1 - step))
            def _():
                if step > 0:
                    bias_copy(line, right).wait_recv()
                    bias_in[line, 1 + way] = bias_in[line, 0] + bias_in[line, 3 + way]
                else:
                    bias_in[line, 1 + way] = bias_in[line, 0]
                bias_copy(line, right).start()

    def bias_end(line):
        own, size = coords[line], lines[line]
        total = bias_in.at[line - 1 if line > 0 else levels, 0]
        total[...] = bias_in[line, 0]
        for right in (True, False):
            way = 0 if right else 1
            exists = own > 0 if right else own < size - 1
            waited = jnp.logical_and(own > 0, own < size - 1)

            @pl.when(exists)
            def _():
                pl.when(jnp.logical_not(waited))(lambda: bias_copy(line, right).wait_recv())
                total[...] += bias_in[line, 3 + way]

        if line == 0:
            bias_swap().start()

    def bias_swap():
        return pltpu.make_async_remote_copy(
            src_ref=bias_in.at[levels, 0], dst_ref=bias_in.at[levels, 1],
            send_sem=bias_send.at[levels, 0], recv_sem=bias_recv.at[levels, 0],
            device_id=twin, device_id_type=MESH)

    bias_work = []
    for line in reversed(range(levels)):
        for step in range(lines[line] - 1):
            bias_work.append(functools.partial(bias_step, line, step))
        bias_work.append(functools.partial(bias_end, line))

    def some_bias(count=1):
        for work in bias_work[:count]:
            work()
        del bias_work[:count]

    straight = [p for p, piece in enumerate(pieces) if piece[3][0] == levels - 1]
    turned = [p for p in range(len(pieces)) if p not in straight]
    top = levels - 1
    steps = lines[pieces[0][3][top]]

    def early(step):
        def down(piece, stage, slot):
            if stage == 0:
                if is_early(piece, 0):
                    early_send(piece, slot)
                return
            for inner in range(lines[pieces[piece][3][stage]]):
                down(piece, stage - 1, dest_slot(piece, stage, slot, inner)[1])

        for piece in straight:
            if levels == 1:
                if step == 0:
                    down(piece, 0, 0)
            else:
                down(piece, top - 1, dest_slot(piece, top, 0, step)[1])

    def turn(step):
        for piece in turned:
            order = pieces[piece][3]
            for outer in range(lines[order[1]]):
                dest, rest_slot = dest_slot(piece, 1, 0, outer)
                line_step(piece, 0, rest_slot, step)
                if step == lines[order[0]] - 1:
                    pending.add((piece, 0))
                    line_step(piece, 1, 0, outer)
                    pending.discard((piece, 0))
            if step == lines[order[0]] - 1:
                keep(piece)

    def go(step):
        for piece in straight:
            line_step(piece, top, 0, step)
            if step == steps - 1:
                keep(piece)

    turns = lines[pieces[turned[0]][3][0]] if turned else 0
    bias_in[levels - 1, 0] = bsum[...]
    some_bias()
    for step in range(steps):
        early(step)
        if step == 1 and turned:
            turn(0)

    @pl.when(first)
    def _():
        gather(res.at[0], LATE, side, conv_back(LATE, side))

    for step in range(max(steps, turns - 1)):
        if 1 <= step + 1 < turns:
            turn(step + 1)
        some_bias(2 if step == 0 else 1)
        if step < steps:
            go(step)
    some_bias(len(bias_work))

    bias_swap().wait_recv()
    share = ch // plan.dp_count
    place = me * share
    own_half = (place >= half) == (core == 1)
    row = jnp.where(own_half, bias_in[levels, 0], bias_in[levels, 1])
    bout[...] = pltpu.roll(row, lax.rem(half - lax.rem(place, half), half), 1)[0:1, 0:share]

    for piece in turned + straight:
        finish(piece)

    def sent_all(ref, sem):
        pltpu.make_async_copy(ref, ref, sem).wait()

    bias_swap().wait_send()
    for line, size in enumerate(lines):
        pl.when(coords[line] < size - 1)(lambda: bias_copy(line, True).wait_send())
        pl.when(coords[line] > 0)(lambda: bias_copy(line, False).wait_send())
    sent_all(wout.at[0, :, 0:half], keep_send.at[0])
    for piece, (_, _, _, order) in enumerate(pieces):
        for stage in range(levels):
            count = plan.slots(piece, stage)
            count -= count // lines[order[stage]]
            sent_all(out_bufs[piece][stage].at[pl.ds(0, count)], line_send[piece].at[stage])
    sent_all(xc.at[:, 0], xc_send.at[0])
    sent_all(do, do_send.at[0])
    pl.when(first)(lambda: sent_all(sent, ahead_send.at[0]))
    pl.when(jnp.logical_not(first))(lambda: sent_all(sent, back_send.at[0]))


def body(boundary, weights, biases, frame_video, video_clips):
    boundary = jnp.transpose(boundary, (0, 2, 3, 1, 4))
    _, side, _, frames, ch = boundary.shape
    dp_count = lax.axis_size("dp")
    plan = Plan(frames, side, ch, dp_count)
    half, group = plan.half, plan.group
    vmem = lambda *shape, dtype=BF16: pltpu.VMEM(shape, dtype)
    dma = pltpu.SemaphoreType.DMA
    scratch = [
        vmem(9 * ch, ch),
        vmem(9 * ch, ch),
        vmem(side, side, frames, ch),
        vmem((side + 2) * group, 3 * ch),
        vmem((side + 2) * group, 3 * ch),
        vmem(side * 2 * group, 3 * half),
        vmem(ch, (side + 2) * 2 * group),
        vmem(side, 2, group, ch),
        vmem(side * group, half),
        vmem(9 * ch, half, dtype=F32),
        vmem(side * group, ch, dtype=F32),
        vmem(side * group, ch, dtype=F32),
        vmem(side, side, frames, ch),
        vmem(side, side, frames, ch),
        vmem(8, half, dtype=F32),
        vmem(group, ch, dtype=F32),
        vmem(1, ch, dtype=F32),
        pltpu.SMEM(frame_video.shape, jnp.int32),
        pltpu.SMEM(video_clips.shape, jnp.int32),
        vmem(len(plan.lines) + 1, 5, 8, half, dtype=F32),
    ]
    levels = len(plan.lines)
    wire = plan.wire
    every = [(p, stage) for p in range(len(plan.pieces)) for stage in range(levels)]
    height = lambda p: plan.pieces[p][2]
    scratch += [vmem(plan.slots(p, stage), height(p), half, dtype=wire) for p, stage in every]
    scratch += [vmem(plan.arrivals(p, stage), height(p), half, dtype=wire) for p, stage in every]
    scratch += [vmem(height(p), half, dtype=F32) for p, _ in every]
    ends = [1 if plan.lines[order[-1]] == 2 else 2 for _, _, _, order in plan.pieces]
    scratch += [vmem(end, 2, height(p), half, dtype=wire) for p, end in enumerate(ends)]
    scratch += [dma((levels,)) for _ in plan.pieces]
    scratch += [dma((plan.arrivals(p, stage),)) for p, stage in every]
    scratch += [dma((end, 2)) for end in ends]
    steps, backs = len(AHEAD) - 1, len(BACK) - 1
    most = max(steps, backs)
    keeps = len(plan.pieces) // 2
    scratch += [dma((n,)) for n in (2, 3, 3, 1, steps, 1, backs, 1, steps, 1, most, 1, keeps)]
    scratch += [dma((levels + 1, 2)) for _ in range(2)]
    whole = pl.BlockSpec(memory_space=pltpu.VMEM)
    share = 9 * ch // dp_count
    operands = [
        pltpu.with_memory_space_constraint(operand, pltpu.HBM)
        for operand in (boundary, weights, biases, frame_video, video_clips)
    ]
    results, kernel_grad, bias_grad = pl.pallas_call(
        functools.partial(kernel, plan),
        out_shape=(
            pltpu.VMEM(boundary.shape, BF16),
            pltpu.VMEM((1, share, ch), F32),
            pltpu.VMEM((1, ch // dp_count), F32),
        ),
        in_specs=[pl.BlockSpec(memory_space=pltpu.HBM)] * 5,
        out_specs=(whole, whole, whole),
        scratch_shapes=scratch,
        compiler_params=pltpu.CompilerParams(
            collective_id=0, has_side_effects=True, vmem_limit_bytes=VMEM_LIMIT
        ),
    )(*operands)
    return jnp.transpose(results, (0, 3, 1, 2, 4)), kernel_grad, bias_grad


def solution(mesh):
    return jax.shard_map(
        body,
        mesh=mesh,
        in_specs=(
            P("section", "dp", None, None, None),
            P("section", None, None),
            P("section", None),
            P("dp"),
            P(),
        ),
        out_specs=(
            P("section", "dp", None, None, None),
            P("section", "dp", None),
            P("section", "dp"),
        ),
        check_vma=False,
    )
```

```python
import functools

import jax
import jax.numpy as jnp
from jax import lax
from jax.experimental import pallas as pl
from jax.experimental.pallas import tpu as pltpu
from jax.sharding import PartitionSpec as P

VMEM_LIMIT = 54 * 1024 * 1024
MESH = pl.DeviceIdType.MESH
F32 = jnp.float32
BF16 = jnp.bfloat16
SLOTS = 16
AHEAD = (0, 2, 4, 6, 8, 10, 12, 13)
BACK = (0, 2, 4, 6, 8, 10, 12, 13)
TERMS = {1: (0, 4), 3: (4, 8), 4: (8, 10)}
REST = 10
EARLY = {2: (0, 3, (0, 1))}
LATE = ((3, 8, (2, 3, 4)), (8, 13, (5, 6)))


def line_sizes(chips):
    sizes = []
    while chips > 1:
        size = 4 if chips % 4 == 0 else 2 if chips % 2 == 0 else chips
        sizes.append(size)
        chips //= size
    return tuple(sizes)


def dest_at(own, step, size):
    rights = size - 1 - own
    low = jnp.where(step < rights, size - 1 - step, step - rights)
    high = jnp.where(step < own, step, size - 1 - (step - own))
    return jnp.where(own < (size + 1) // 2, low, high)


class Plan:
    def __init__(self, frames, side, channels, dp_count):
        self.frames, self.side, self.channels, self.dp_count = frames, side, channels, dp_count
        self.group = SLOTS * frames
        self.cells = side * frames
        self.half = channels // 2
        self.chips = dp_count // 2
        self.lines = line_sizes(self.chips)
        self.rows = 9 * channels // self.chips
        self.mine = self.rows // 2
        levels = len(self.lines)
        inner_first = tuple(reversed(range(levels)))
        outer_first = tuple(range(levels))
        self.pieces = []
        for keeper in range(2):
            if self.mine % 96 == 0 and levels == 2:
                sixteenths = self.mine // 16
                turned = sixteenths // 6
                part = (sixteenths - turned) // 2
                cuts = [(part, inner_first), (sixteenths - turned - part, inner_first), (turned, outer_first)]
                begin = 0
                for size, order in cuts:
                    self.pieces.append((keeper, begin, 16 * size, order))
                    begin += 16 * size
            else:
                self.pieces.append((keeper, 0, self.mine, inner_first))
        self.wire = BF16 if all(size % 16 == 0 and begin % 16 == 0 for _, begin, size, _ in self.pieces) else F32

    def slots(self, piece, stage):
        order = self.pieces[piece][3]
        count = 1
        for line in order[stage:]:
            count *= self.lines[line]
        return count

    def arrivals(self, piece, stage):
        size = self.lines[self.pieces[piece][3][stage]]
        after = self.slots(piece, stage) // size
        return after if size == 2 else (size + 1) * after


def kernel(plan, *refs):
    (x_hbm, w_hbm, bias_hbm, video_hbm, clips_hbm, res, wout, bout,
     w, wt, xin, xs, ds, wd, xt, xc, do, grad, pre, other_pre, pad,
     sent, arrived, returned, bsum, scale, bias_ref, video_ref, clips_ref, bias_in) = refs[:30]
    rest = list(refs[30:])
    lines, pieces = plan.lines, plan.pieces
    levels = len(lines)

    def take(count):
        taken = rest[:count]
        del rest[:count]
        return taken

    out_bufs = [take(levels) for _ in pieces]
    in_bufs = [take(levels) for _ in pieces]
    sums = [take(levels) for _ in pieces]
    last_in = take(len(pieces))
    line_send = take(len(pieces))
    line_recv = [take(levels) for _ in pieces]
    last_recv = take(len(pieces))
    (load_sem, wload_sem, small_sem, ahead_send, ahead_recv, back_send, back_recv, xc_send, xc_recv, do_send, do_recv,
     pre_sem,
     keep_send, keep_recv, bias_send, bias_recv) = rest

    frames, side, ch, half = plan.frames, plan.side, plan.channels, plan.half
    group, cells = plan.group, plan.cells
    sec = lax.axis_index("section")
    me = lax.axis_index("dp")
    core = lax.rem(me, 2)
    coords, strides = [], []
    stride = plan.dp_count
    for size in lines:
        stride //= size
        strides.append(stride)
        coords.append(lax.rem(lax.div(me, stride), size))
    first = sec == 0
    across = (1 - sec, me)
    twin = (sec, me + 1 - 2 * core)
    aslant = (1 - sec, me + 1 - 2 * core)

    upside = coords[0] >= (lines[0] + 1) // 2

    def row(i):
        return jnp.where(upside, side - 1 - i, i)

    def tap(a):
        return jnp.where(upside, 2 - a, a)

    first_rows = 3

    def load_row(i):
        return pltpu.make_async_copy(x_hbm.at[0, row(i)], xin.at[i], load_sem.at[0 if i < first_rows else 1])

    def wait_rows(k):
        rows = xin.at[0:first_rows] if k == 0 else xin.at[first_rows:side]
        pltpu.make_async_copy(rows, rows, load_sem.at[k]).wait()

    def load_w(a):
        part = pl.ds(pl.multiple_of(3 * ch * tap(a), 3 * ch), 3 * ch)
        return pltpu.make_async_copy(w_hbm.at[0, part], w.at[3 * ch * a : 3 * ch * (a + 1)], wload_sem.at[a])

    def load_small(k):
        source, to = ((bias_hbm, bias_ref), (video_hbm, video_ref), (clips_hbm, clips_ref))[k]
        return pltpu.make_async_copy(source, to, small_sem.at[k])

    for i in range(first_rows):
        load_row(i).start()
    for a in range(3):
        load_w(a).start()
    for i in range(first_rows, side):
        load_row(i).start()
    for k in range(3):
        load_small(k).start()

    barrier = pltpu.get_barrier_semaphore()
    for device in (across, aslant, twin):
        pl.semaphore_signal(barrier, inc=1, device_id=device, device_id_type=MESH)
    greeted = 3
    for own, size, stride in zip(coords, lines, strides):
        for there, exists in ((me - stride, own > 0), (me + stride, own < size - 1)):
            @pl.when(exists)
            def _():
                for device in (there, there + 1 - 2 * core):
                    pl.semaphore_signal(barrier, inc=1, device_id=(sec, device), device_id_type=MESH)

            greeted = greeted + 2 * exists.astype(jnp.int32)

    for ref in (xs, ds):
        for i in (0, side + 1):
            ref[i] = jnp.zeros((group, 3 * ch), BF16)
    xt[:, 0 : 2 * group] = jnp.zeros((ch, 2 * group), BF16)
    xt[:, (side + 1) * 2 * group : (side + 2) * 2 * group] = jnp.zeros((ch, 2 * group), BF16)
    pad[...] = jnp.zeros_like(pad)
    bsum[...] = jnp.zeros_like(bsum)

    def spread(ref, begin, end, lane=0):
        lanes = slice(lane, lane + ref.shape[-1])
        for i in range(begin, end):
            pad[i * group : i * group + cells, lanes] = ref[i].astype(F32).reshape(cells, ref.shape[-1])
        return pad[begin * group : end * group, lanes]

    def gather(ref, begin, end, value, order=lambda i: i):
        for i in range(begin, end):
            at = (i - begin) * group
            ref[order(i)] = value[at : at + cells, :].reshape(side, frames, ch).astype(BF16)

    def rounded(v):
        ids = lax.broadcasted_iota(jnp.int32, v.shape, 0)
        return jnp.where(lax.rem(ids, group) < cells, v, 0.0).astype(BF16).astype(F32)

    def moved(v, slots):
        if slots:
            v = pltpu.roll(v, slots * frames % v.shape[0], 0)
        return v.astype(BF16).reshape(v.shape[0] // group, group, v.shape[1])

    def put_inputs(begin, end, v):
        for b in range(3):
            xs[begin + 1 : end + 1, :, b * ch : (b + 1) * ch] = moved(v, 1 - b)
        xc[begin:end, 0] = moved(v, 0)

    def put_deltas(begin, end, v, lane=0):
        for b in range(3):
            at = pl.multiple_of(b * ch + lane, 128)
            ds[begin + 1 : end + 1, :, pl.ds(at, v.shape[1])] = moved(v, b - 1)

    def put_halves(begin, end, which, v):
        for b in range(3):
            wd[begin:end, which, :, half * b : half * (b + 1)] = moved(v, b - 1)
        bsum[0:1, :] += jnp.sum(v, axis=0, keepdims=True)

    def product(source, factor, begin, end, sign, ready=lambda a: None):
        count = (end - begin) * group
        total = jnp.zeros((count, ch), F32)
        for a in range(3):
            ready(a)
            at = begin + 1 + sign * (a - 1)
            total += jnp.dot(source[at : at + end - begin].reshape(count, 3 * ch), factor[3 * ch * a : 3 * ch * (a + 1), :],
                             preferred_element_type=F32)
        return total

    def conv(begin, end, ready=lambda a: None):
        return product(xs, w, begin, end, 1, ready) + bias_ref[...]

    def conv_back(begin, end):
        return product(ds, wt, begin, end, -1)

    def transpose_w(a):
        for k in range(3 * a, 3 * a + 3):
            at = slice(ch * k, ch * (k + 1))
            wt[at, :] = w[at, :].T

    def ahead(k):
        rows = pl.ds(AHEAD[k], AHEAD[k + 1] - AHEAD[k])
        return pltpu.make_async_remote_copy(
            src_ref=sent.at[rows], dst_ref=arrived.at[rows], send_sem=ahead_send.at[0], recv_sem=ahead_recv.at[k],
            device_id=across, device_id_type=MESH)

    def back(k, which):
        rows = pl.ds(BACK[k], BACK[k + 1] - BACK[k])
        lane = pl.multiple_of(half * (core if which == 0 else 1 - core), 128)
        return pltpu.make_async_remote_copy(
            src_ref=sent.at[rows, :, :, pl.ds(lane, half)], dst_ref=returned.at[which, rows],
            send_sem=back_send.at[0], recv_sem=back_recv.at[which, k],
            device_id=(across, aslant)[which], device_id_type=MESH)

    def share_inputs(k):
        rows = pl.ds(AHEAD[k], AHEAD[k + 1] - AHEAD[k])
        return pltpu.make_async_remote_copy(
            src_ref=xc.at[rows, 0], dst_ref=xc.at[rows, 1], send_sem=xc_send.at[0], recv_sem=xc_recv.at[k],
            device_id=twin, device_id_type=MESH)

    def share_pre():
        lane = pl.multiple_of(half * (1 - core), 128)
        return pltpu.make_async_remote_copy(
            src_ref=pre.at[:, pl.ds(lane, half)], dst_ref=other_pre, send_sem=pre_sem.at[0], recv_sem=pre_sem.at[1],
            device_id=twin, device_id_type=MESH)

    def share_deltas(k, begin, end, source):
        return pltpu.make_async_remote_copy(
            src_ref=source, dst_ref=do.at[begin:end],
            send_sem=do_send.at[0], recv_sem=do_recv.at[k], device_id=twin, device_id_type=MESH)

    def other_deltas(k, begin, end):
        share_deltas(k, begin, end, do.at[begin:end]).wait_recv()
        return do[begin:end].reshape((end - begin) * group, half).astype(F32)

    def transpose_inputs():
        for k in range(len(AHEAD) - 1):
            share_inputs(k).wait_recv()
        for begin in range(0, side, 2):
            end = min(begin + 2, side)
            part = xc[begin:end].reshape((end - begin) * 2 * group, ch)
            xt[:, (begin + 1) * 2 * group : (end + 1) * 2 * group] = part.T

    def weight_term(a, begin, end, fresh=False):
        wide = 2 * group
        term = jnp.dot(xt[:, (begin + a) * wide : (end + a) * wide], wd[begin:end].reshape((end - begin) * wide, 3 * half),
                       preferred_element_type=F32)
        for b in range(3):
            at = pl.ds(pl.multiple_of(ch * (3 * tap(a) + b), ch), ch)
            part = term[:, half * b : half * (b + 1)]
            grad[at, :] = part if fresh else grad[at, :] + part

    def sigmoid(v):
        return 1.0 / (1.0 + jnp.exp(-v))

    for k in range(3):
        load_small(k).wait()

    def ahead_rows(k, ready=lambda a: None):
        begin, end = AHEAD[k], AHEAD[k + 1]
        v = conv(begin, end, ready)
        s = sigmoid(v)
        gather(sent, begin, end, v * s)
        pre[begin * group : end * group, :] = s * (1.0 + v * (1.0 - s))

    @pl.when(first)
    def _():
        wait_rows(0)
        put_inputs(0, first_rows, spread(xin, 0, first_rows))
        ahead_rows(0, lambda a: load_w(a).wait())

    @pl.when(jnp.logical_not(first))
    def _():
        ids = lax.rem(lax.broadcasted_iota(jnp.int32, (group, ch), 0), frames)
        per_row = jnp.zeros((group, ch), F32)
        for f in range(frames):
            clip = clips_ref[video_ref[f]].astype(F32)
            per_row = jnp.where(ids == f, 1.0 / jnp.full((1, ch), clip, F32), per_row)
        scale[...] = per_row
        for a in range(3):
            load_w(a).wait()
            transpose_w(a)
        wait_rows(0)

    wait_rows(1)
    pl.semaphore_wait(barrier, greeted)

    back_rows = list(zip(BACK, BACK[1:]))
    final = len(back_rows) - 1

    def returned_deltas(k):
        begin, end = back_rows[k]
        rows = slice(begin * group, end * group)
        for which in range(2):
            back(k, which).wait_recv()
            if which == 0:
                factor = pre[rows, pl.ds(pl.multiple_of(half * core, 128), half)]
            else:
                factor = other_pre[rows, :]
            d = rounded(spread(returned.at[which], begin, end, half * which) * factor)
            put_halves(begin, end, which, d)
            if which == 0:
                put_deltas(begin, end, d, half * core)
        share_deltas(k, begin, end, wd.at[begin:end, 1, :, half : 2 * half]).start()

    def input_grad(begin, end, chunks):
        for k in chunks:
            put_deltas(*back_rows[k], other_deltas(k, *back_rows[k]), half * (1 - core))
        gather(res.at[0], begin, end, conv_back(begin, end), row)

    @pl.when(first)
    def _():
        ahead(0).start()
        put_inputs(first_rows, side, spread(xin, first_rows, side))
        share_inputs(0).start()
        for k in range(1, len(AHEAD) - 1):
            ahead_rows(k)
            ahead(k).start()
            share_inputs(k).start()
        share_pre().start()
        for a in range(3):
            transpose_w(a)
        transpose_inputs()
        share_pre().wait_recv()

        for k in range(final):
            returned_deltas(k)
            if k in TERMS:
                for a in range(3):
                    weight_term(a, *TERMS[k], TERMS[k][0] == 0)
            if k in EARLY:
                input_grad(*EARLY[k])
        weight_term(2, REST, BACK[final])

    @pl.when(jnp.logical_not(first))
    def _():
        rows_of = []
        done, next_back = 0, 0
        for k, (begin, end) in enumerate(zip(AHEAD, AHEAD[1:])):
            ahead(k).wait_recv()
            put_inputs(begin, end, spread(arrived, begin, end))
            share_inputs(k).start()
            top = side if end == side else end - 1
            v = conv(done, top)
            s = sigmoid(v)
            g = spread(xin, done, top).reshape(top - done, group, ch) * scale[...]
            d = rounded(g.reshape((top - done) * group, ch) * (s * (1.0 + v * (1.0 - s))))
            put_deltas(done, top, d)
            rows_of.append((done, top))
            begin, done = done, top
            while next_back < len(BACK) - 1 and (BACK[next_back + 1] < done or done == side):
                low, high = BACK[next_back], BACK[next_back + 1]
                gather(sent, low, high, conv_back(low, high))
                for which in range(2):
                    back(next_back, which).start()
                next_back += 1
            lane = pl.multiple_of(ch + half * (1 - core), 128)
            share_deltas(k, begin, done, ds.at[begin + 1 : done + 1, :, pl.ds(lane, half)]).start()
            lane = pl.multiple_of(ch + half * core, 128)
            own = ds[begin + 1 : done + 1, :, pl.ds(lane, half)]
            put_halves(begin, done, 0, own.reshape((done - begin) * group, half).astype(F32))
            gather(res.at[0], begin, done, v * s, row)
        transpose_inputs()
        for k, (begin, end) in enumerate(rows_of):
            put_halves(begin, end, 1, other_deltas(k, begin, end))
        weight_term(2, 0, side, True)

    def rest_of_gradient(a):
        @pl.when(first)
        def _():
            if a == 1:
                returned_deltas(final)
            weight_term(a, REST, side)

        pl.when(jnp.logical_not(first))(lambda: weight_term(a, 0, side, True))

    def arrival_at(piece, stage, slot, side_at):
        size = lines[pieces[piece][3][stage]]
        after = plan.slots(piece, stage) // size
        if size == 2:
            return lax.rem(slot, after)
        own = lax.div(slot, after) == coords[pieces[piece][3][stage]]
        return jnp.where(jnp.logical_and(own, side_at == 1), size * after + lax.rem(slot, after), slot)

    def line_copy(piece, stage, slot, dest, final=False):
        keeper, _, size, order = pieces[piece]
        line = order[stage]
        right = dest > coords[line]
        side_at = jnp.where(right, 0, 1)
        to = me + jnp.where(right, strides[line], -strides[line])
        if final:
            to = to - core + keeper
            at = 0 if lines[line] == 2 else side_at
            target, sem = last_in[piece].at[at, core], last_recv[piece].at[at, core]
        else:
            there = dest == coords[line] + jnp.where(right, 1, -1)
            after = plan.slots(piece, stage) // lines[line]
            if lines[line] == 2:
                at = lax.rem(slot, after)
            else:
                second = jnp.logical_and(there, jnp.logical_not(right))
                at = jnp.where(second, lines[line] * after + lax.rem(slot, after), slot)
            target, sem = in_bufs[piece][stage].at[at], line_recv[piece][stage].at[at]
        return pltpu.make_async_remote_copy(
            src_ref=out_bufs[piece][stage].at[slot], dst_ref=target,
            send_sem=line_send[piece].at[stage], recv_sem=sem, device_id=(sec, to), device_id_type=MESH)

    def arrival(piece, stage, slot, side_at):
        at = arrival_at(piece, stage, slot, side_at)
        pltpu.make_async_remote_copy(
            src_ref=out_bufs[piece][stage].at[slot], dst_ref=in_bufs[piece][stage].at[at],
            send_sem=line_send[piece].at[stage], recv_sem=line_recv[piece][stage].at[at],
            device_id=twin, device_id_type=MESH).wait_recv()
        return in_bufs[piece][stage][at].astype(F32)

    def last_arrival(piece, side_at, columns):
        at = 0 if lines[pieces[piece][3][levels - 1]] == 2 else side_at
        pltpu.make_async_remote_copy(
            src_ref=out_bufs[piece][levels - 1].at[0], dst_ref=last_in[piece].at[at, columns],
            send_sem=line_send[piece].at[levels - 1], recv_sem=last_recv[piece].at[at, columns],
            device_id=twin, device_id_type=MESH).wait_recv()
        return last_in[piece][at, columns].astype(F32)

    def send_on(piece, stage, slot, dest):
        line = pieces[piece][3][stage]
        if stage < levels - 1:
            line_copy(piece, stage, slot, dest).start()
            return
        next_to = jnp.abs(dest - coords[line]) == 1

        @pl.when(next_to)
        def _():
            line_copy(piece, stage, slot, dest, True).start()

        @pl.when(jnp.logical_not(next_to))
        def _():
            line_copy(piece, stage, slot, dest).start()

    def leaf(piece, slot):
        keeper, begin, size, order = pieces[piece]
        left, chip = slot, 0
        for line in reversed(order):
            chip = chip + lax.rem(left, lines[line]) * (strides[line] // 2)
            left = lax.div(left, lines[line])
        at = chip * plan.rows + keeper * plan.mine + begin
        return grad[pl.ds(pl.multiple_of(at, 8), size), :]

    def dest_slot(piece, stage, rest_slot, step):
        line = pieces[piece][3][stage]
        dest = dest_at(coords[line], step, lines[line])
        after = plan.slots(piece, stage) // lines[line]
        return dest, dest * after + rest_slot

    def is_early(piece, stage):
        return stage == 0 and lines[pieces[piece][3][0]] == 2

    def early_send(piece, rest_slot):
        dest, slot = dest_slot(piece, 0, rest_slot, 0)
        out_bufs[piece][0][slot] = leaf(piece, slot).astype(plan.wire)
        send_on(piece, 0, slot, dest)

    def line_step(piece, stage, rest_slot, step):
        line = pieces[piece][3][stage]
        size, own = lines[line], coords[line]
        if step < size - 1 and is_early(piece, stage):
            return
        dest, slot = dest_slot(piece, stage, rest_slot, step)
        if stage == 0:
            value = leaf(piece, slot)
        else:
            value = summed(piece, stage - 1, slot)
        total = sums[piece][stage]
        if step < size - 1:
            right = dest > own
            upstream = jnp.logical_or(jnp.logical_and(right, own > 0), jnp.logical_and(jnp.logical_not(right), own < size - 1))

            @pl.when(upstream)
            def _():
                both = value + arrival(piece, stage, slot, jnp.where(right, 0, 1))
                out_bufs[piece][stage][slot] = both.astype(plan.wire)

            @pl.when(jnp.logical_not(upstream))
            def _():
                out_bufs[piece][stage][slot] = value.astype(plan.wire)

            send_on(piece, stage, slot, dest)
        else:
            total[...] = value
            if stage < levels - 1:
                @pl.when(own > 0)
                def _():
                    total[...] += arrival(piece, stage, slot, 0)

                @pl.when(own < size - 1)
                def _():
                    total[...] += arrival(piece, stage, slot, 1)

    pending = set()

    def summed(piece, stage, rest_slot):
        if (piece, stage) not in pending:
            for step in range(lines[pieces[piece][3][stage]]):
                line_step(piece, stage, rest_slot, step)
        return sums[piece][stage][...]

    def keep_copy(piece):
        keeper, begin, size, _ = pieces[piece]
        return pltpu.make_async_remote_copy(
            src_ref=sums[piece][levels - 1],
            dst_ref=wout.at[0, begin : begin + size, half * (1 - keeper) : half * (2 - keeper)],
            send_sem=keep_send.at[0], recv_sem=keep_recv.at[piece % (len(pieces) // 2)], device_id=twin, device_id_type=MESH)

    def keep(piece):
        keeper, begin, size, _ = pieces[piece]

        @pl.when(core == keeper)
        def _():
            wout[0, begin : begin + size, half * keeper : half * (keeper + 1)] = sums[piece][levels - 1][...]

        @pl.when(core != keeper)
        def _():
            keep_copy(piece).start()

    def finish(piece):
        keeper, begin, size, order = pieces[piece]
        line = order[levels - 1]
        own = coords[line]

        @pl.when(core == keeper)
        def _():
            keep_copy(piece).wait_recv()

            def add(side_at):
                for columns in range(2):
                    wout[0, begin : begin + size, half * columns : half * (columns + 1)] += last_arrival(piece, side_at, columns)

            pl.when(own > 0)(lambda: add(0))
            pl.when(own < lines[line] - 1)(lambda: add(1))

    def bias_copy(line, right):
        way = 0 if right else 1
        return pltpu.make_async_remote_copy(
            src_ref=bias_in.at[line, 1 + way], dst_ref=bias_in.at[line, 3 + way],
            send_sem=bias_send.at[line, way], recv_sem=bias_recv.at[line, way],
            device_id=(sec, me + strides[line] * (1 if right else -1)), device_id_type=MESH)

    def bias_step(line, step):
        own, size = coords[line], lines[line]
        for right in (True, False):
            way = 0 if right else 1

            @pl.when(own == (step if right else size - 1 - step))
            def _():
                if step > 0:
                    bias_copy(line, right).wait_recv()
                    bias_in[line, 1 + way] = bias_in[line, 0] + bias_in[line, 3 + way]
                else:
                    bias_in[line, 1 + way] = bias_in[line, 0]
                bias_copy(line, right).start()

    def bias_end(line):
        own, size = coords[line], lines[line]
        total = bias_in.at[line + 1, 0]
        total[...] = bias_in[line, 0]
        for right in (True, False):
            way = 0 if right else 1
            exists = own > 0 if right else own < size - 1
            waited = jnp.logical_and(own > 0, own < size - 1)

            @pl.when(exists)
            def _():
                pl.when(jnp.logical_not(waited))(lambda: bias_copy(line, right).wait_recv())
                total[...] += bias_in[line, 3 + way]

        if line == levels - 1:
            bias_swap().start()

    def bias_swap():
        return pltpu.make_async_remote_copy(
            src_ref=bias_in.at[levels, 0], dst_ref=bias_in.at[levels, 1],
            send_sem=bias_send.at[levels, 0], recv_sem=bias_recv.at[levels, 0],
            device_id=twin, device_id_type=MESH)

    bias_work = []
    for line in range(levels):
        for step in range(lines[line] - 1):
            bias_work.append(functools.partial(bias_step, line, step))
        bias_work.append(functools.partial(bias_end, line))

    def some_bias(count=1):
        for work in bias_work[:count]:
            work()
        del bias_work[:count]

    straight = [p for p, piece in enumerate(pieces) if piece[3][0] == levels - 1]
    turned = [p for p in range(len(pieces)) if p not in straight]
    top = levels - 1
    steps = lines[pieces[0][3][top]]

    def early(step):
        def down(piece, stage, slot):
            if stage == 0:
                if is_early(piece, 0):
                    early_send(piece, slot)
                return
            for inner in range(lines[pieces[piece][3][stage]]):
                down(piece, stage - 1, dest_slot(piece, stage, slot, inner)[1])

        for piece in straight:
            if levels == 1:
                if step == 0:
                    down(piece, 0, 0)
            else:
                down(piece, top - 1, dest_slot(piece, top, 0, step)[1])

    def turn(step):
        for piece in turned:
            order = pieces[piece][3]
            for outer in range(lines[order[1]]):
                dest, rest_slot = dest_slot(piece, 1, 0, outer)
                line_step(piece, 0, rest_slot, step)
                if step == lines[order[0]] - 1:
                    pending.add((piece, 0))
                    line_step(piece, 1, 0, outer)
                    pending.discard((piece, 0))
            if step == lines[order[0]] - 1:
                keep(piece)

    def go(step):
        for piece in straight:
            line_step(piece, top, 0, step)
            if step == steps - 1:
                keep(piece)

    turns = lines[pieces[turned[0]][3][0]] if turned else 0
    staged = levels > 1 and lines[0] >= 4
    ends = jnp.logical_or(coords[0] == 0, coords[0] == lines[0] - 1)
    if staged:
        early(0)
        if turned:
            pl.when(ends)(lambda: turn(0))
    rest_of_gradient(1)
    bias_in[0, 0] = bsum[...]
    some_bias()
    if staged:
        early(1)
    rest_of_gradient(0)
    for step in range(2 if staged else 0, steps - 1):
        early(step)
    if turned:
        if staged:
            pl.when(jnp.logical_not(ends))(lambda: turn(0))
        else:
            turn(0)
    some_bias()

    def late(k):
        if k < len(LATE):
            pl.when(first)(lambda: input_grad(*LATE[k]))

    late(0)
    for step in range(max(steps, turns - 1)):
        if 1 <= step + 1 < turns:
            turn(step + 1)
        some_bias((1, 2)[step] if step < 2 else 0)
        if step == min(1, steps - 2):
            early(steps - 1)
        if step < steps:
            go(step)
        late(step + 1)

    for n, piece in enumerate(turned + straight):
        if n == len(pieces) // 2:
            some_bias(len(bias_work))
        finish(piece)

    bias_swap().wait_recv()
    share = ch // plan.dp_count
    place = me * share
    own_half = (place >= half) == (core == 1)
    bias_row = jnp.where(own_half, bias_in[levels, 0], bias_in[levels, 1])
    bout[...] = pltpu.roll(bias_row, lax.rem(half - lax.rem(place, half), half), 1)[0:1, 0:share]

    def sent_all(ref, sem):
        pltpu.make_async_copy(ref, ref, sem).wait()

    bias_swap().wait_send()
    for line, size in enumerate(lines):
        pl.when(coords[line] < size - 1)(lambda: bias_copy(line, True).wait_send())
        pl.when(coords[line] > 0)(lambda: bias_copy(line, False).wait_send())
    sent_all(wout.at[0, :, 0:half], keep_send.at[0])
    for piece, (_, _, _, order) in enumerate(pieces):
        for stage in range(levels):
            count = plan.slots(piece, stage)
            count -= count // lines[order[stage]]
            sent_all(out_bufs[piece][stage].at[pl.ds(0, count)], line_send[piece].at[stage])
    sent_all(xc.at[:, 0], xc_send.at[0])
    sent_all(do, do_send.at[0])
    pl.when(first)(lambda: share_pre().wait_send())
    pl.when(first)(lambda: sent_all(sent, ahead_send.at[0]))
    pl.when(jnp.logical_not(first))(lambda: sent_all(sent, back_send.at[0]))


def body(boundary, weights, biases, frame_video, video_clips):
    boundary = jnp.transpose(boundary, (0, 2, 3, 1, 4))
    _, side, _, frames, ch = boundary.shape
    dp_count = lax.axis_size("dp")
    plan = Plan(frames, side, ch, dp_count)
    half, group = plan.half, plan.group
    vmem = lambda *shape, dtype=BF16: pltpu.VMEM(shape, dtype)
    dma = pltpu.SemaphoreType.DMA
    scratch = [
        vmem(9 * ch, ch),
        vmem(9 * ch, ch),
        vmem(side, side, frames, ch),
        vmem(side + 2, group, 3 * ch),
        vmem(side + 2, group, 3 * ch),
        vmem(side, 2, group, 3 * half),
        vmem(ch, (side + 2) * 2 * group),
        vmem(side, 2, group, ch),
        vmem(side, group, half),
        vmem(9 * ch, half, dtype=F32),
        vmem(side * group, ch, dtype=F32),
        vmem(side * group, half, dtype=F32),
        vmem(side * group, ch, dtype=F32),
        vmem(side, side, frames, ch),
        vmem(side, side, frames, ch),
        vmem(2, side, side, frames, half),
        vmem(8, half, dtype=F32),
        vmem(group, ch, dtype=F32),
        vmem(1, ch, dtype=F32),
        pltpu.SMEM(frame_video.shape, jnp.int32),
        pltpu.SMEM(video_clips.shape, jnp.int32),
        vmem(len(plan.lines) + 1, 5, 8, half, dtype=F32),
    ]
    levels = len(plan.lines)
    wire = plan.wire
    every = [(p, stage) for p in range(len(plan.pieces)) for stage in range(levels)]
    height = lambda p: plan.pieces[p][2]
    scratch += [vmem(plan.slots(p, stage), height(p), half, dtype=wire) for p, stage in every]
    scratch += [vmem(plan.arrivals(p, stage), height(p), half, dtype=wire) for p, stage in every]
    scratch += [vmem(height(p), half, dtype=F32) for p, _ in every]
    ends = [1 if plan.lines[order[-1]] == 2 else 2 for _, _, _, order in plan.pieces]
    scratch += [vmem(end, 2, height(p), half, dtype=wire) for p, end in enumerate(ends)]
    scratch += [dma((levels,)) for _ in plan.pieces]
    scratch += [dma((plan.arrivals(p, stage),)) for p, stage in every]
    scratch += [dma((end, 2)) for end in ends]
    steps, backs = len(AHEAD) - 1, len(BACK) - 1
    most = max(steps, backs)
    keeps = len(plan.pieces) // 2
    shapes = [(2,), (3,), (3,), (1,), (steps,), (1,), (2, backs), (1,), (steps,), (1,), (most,), (2,), (1,), (keeps,)]
    scratch += [dma(shape) for shape in shapes]
    scratch += [dma((levels + 1, 2)) for _ in range(2)]
    whole = pl.BlockSpec(memory_space=pltpu.VMEM)
    share = 9 * ch // dp_count
    operands = [
        pltpu.with_memory_space_constraint(operand, pltpu.HBM)
        for operand in (boundary, weights, biases, frame_video, video_clips)
    ]
    results, kernel_grad, bias_grad = pl.pallas_call(
        functools.partial(kernel, plan),
        out_shape=(
            pltpu.VMEM(boundary.shape, BF16),
            pltpu.VMEM((1, share, ch), F32),
            pltpu.VMEM((1, ch // dp_count), F32),
        ),
        in_specs=[pl.BlockSpec(memory_space=pltpu.HBM)] * 5,
        out_specs=(whole, whole, whole),
        scratch_shapes=scratch,
        compiler_params=pltpu.CompilerParams(
            collective_id=0, has_side_effects=True, vmem_limit_bytes=VMEM_LIMIT
        ),
    )(*operands)
    return jnp.transpose(results, (0, 3, 1, 2, 4)), kernel_grad, bias_grad


def solution(mesh):
    return jax.shard_map(
        body,
        mesh=mesh,
        in_specs=(
            P("section", "dp", None, None, None),
            P("section", None, None),
            P("section", None),
            P("dp"),
            P(),
        ),
        out_specs=(
            P("section", "dp", None, None, None),
            P("section", "dp", None),
            P("section", "dp"),
        ),
        check_vma=False,
    )
```

```python
import functools

import jax
import jax.numpy as jnp
from jax import lax
from jax.experimental import pallas as pl
from jax.experimental.pallas import tpu as pltpu
from jax.sharding import PartitionSpec as P

VMEM_LIMIT = 54 * 1024 * 1024
MESH = pl.DeviceIdType.MESH
F32 = jnp.float32
BF16 = jnp.bfloat16
SLOTS = 16
AHEAD = (0, 2, 4, 6, 8, 10, 12, 13)
BACK = (0, 2, 4, 6, 8, 10, 12, 13)
TERMS = {1: (0, 4), 3: (4, 8), 4: (8, 10)}
REST = 10
EARLY = {2: (0, 3, (0, 1))}
LATE = ((3, 8, (2, 3, 4)), (8, 13, (5, 6)))


def line_sizes(chips):
    sizes = []
    while chips > 1:
        size = 4 if chips % 4 == 0 else 2 if chips % 2 == 0 else chips
        sizes.append(size)
        chips //= size
    return tuple(sizes)


def dest_at(own, step, size):
    rights = size - 1 - own
    low = jnp.where(step < rights, size - 1 - step, step - rights)
    high = jnp.where(step < own, step, size - 1 - (step - own))
    return jnp.where(own < (size + 1) // 2, low, high)


class Plan:
    def __init__(self, frames, side, channels, dp_count):
        self.frames, self.side, self.channels, self.dp_count = frames, side, channels, dp_count
        self.group = SLOTS * frames
        self.cells = side * frames
        self.half = channels // 2
        self.chips = dp_count // 2
        self.lines = line_sizes(self.chips)
        self.rows = 9 * channels // self.chips
        self.mine = self.rows // 2
        levels = len(self.lines)
        inner_first = tuple(reversed(range(levels)))
        outer_first = tuple(range(levels))
        self.pieces = []
        for keeper in range(2):
            if self.mine % 96 == 0 and levels == 2:
                sixteenths = self.mine // 16
                turned = sixteenths // 6
                part = (sixteenths - turned) // 2
                cuts = [(part, inner_first), (sixteenths - turned - part, inner_first), (turned, outer_first)]
                begin = 0
                for size, order in cuts:
                    self.pieces.append((keeper, begin, 16 * size, order))
                    begin += 16 * size
            else:
                self.pieces.append((keeper, 0, self.mine, inner_first))
        self.wire = BF16 if all(size % 16 == 0 and begin % 16 == 0 for _, begin, size, _ in self.pieces) else F32

    def slots(self, piece, stage):
        order = self.pieces[piece][3]
        count = 1
        for line in order[stage:]:
            count *= self.lines[line]
        return count

    def arrivals(self, piece, stage):
        size = self.lines[self.pieces[piece][3][stage]]
        after = self.slots(piece, stage) // size
        return after if size == 2 else (size + 1) * after


def kernel(plan, *refs):
    (x_hbm, w_hbm, bias_hbm, video_hbm, clips_hbm, res, wout, bout,
     w, wt, xin, xs, ds, wd, xt, xc, do, grad, pre, other_pre, pad,
     sent, arrived, returned, bsum, scale, bias_ref, video_ref, clips_ref, bias_in) = refs[:30]
    rest = list(refs[30:])
    lines, pieces = plan.lines, plan.pieces
    levels = len(lines)

    def take(count):
        taken = rest[:count]
        del rest[:count]
        return taken

    out_bufs = [take(levels) for _ in pieces]
    in_bufs = [take(levels) for _ in pieces]
    sums = [take(levels) for _ in pieces]
    last_in = take(len(pieces))
    own_in = take(len(pieces))
    line_send = take(len(pieces))
    line_recv = [take(levels) for _ in pieces]
    last_recv = take(len(pieces))
    (load_sem, wload_sem, small_sem, ahead_send, ahead_recv, back_send, back_recv, xc_send, xc_recv, do_send, do_recv,
     pre_sem,
     keep_send, keep_recv, bias_send, bias_recv, own_recv) = rest

    frames, side, ch, half = plan.frames, plan.side, plan.channels, plan.half
    group, cells = plan.group, plan.cells
    sec = lax.axis_index("section")
    me = lax.axis_index("dp")
    core = lax.rem(me, 2)
    coords, strides = [], []
    stride = plan.dp_count
    for size in lines:
        stride //= size
        strides.append(stride)
        coords.append(lax.rem(lax.div(me, stride), size))
    first = sec == 0
    across = (1 - sec, me)
    twin = (sec, me + 1 - 2 * core)
    aslant = (1 - sec, me + 1 - 2 * core)

    upside = coords[0] >= (lines[0] + 1) // 2

    def row(i):
        return jnp.where(upside, side - 1 - i, i)

    def tap(a):
        return jnp.where(upside, 2 - a, a)

    first_rows = 3

    def load_row(i):
        return pltpu.make_async_copy(x_hbm.at[0, row(i)], xin.at[i], load_sem.at[0 if i < first_rows else 1])

    def wait_rows(k):
        rows = xin.at[0:first_rows] if k == 0 else xin.at[first_rows:side]
        pltpu.make_async_copy(rows, rows, load_sem.at[k]).wait()

    def load_w(n, a):
        part = pl.ds(pl.multiple_of(3 * ch * tap(a), 3 * ch), 3 * ch)
        columns = slice(half * n, half * (n + 1))
        return pltpu.make_async_copy(
            w_hbm.at[0, part, columns], w.at[3 * ch * a : 3 * ch * (a + 1), columns], wload_sem.at[n, a])

    def load_small(k):
        source, to = ((bias_hbm, bias_ref), (video_hbm, video_ref), (clips_hbm, clips_ref))[k]
        return pltpu.make_async_copy(source, to, small_sem.at[k])

    for i in range(first_rows):
        load_row(i).start()
    for n in range(2):
        for a in range(3):
            load_w(n, a).start()
    for i in range(first_rows, side):
        load_row(i).start()
    for k in range(3):
        load_small(k).start()

    barrier = pltpu.get_barrier_semaphore()
    for device in (across, aslant, twin):
        pl.semaphore_signal(barrier, inc=1, device_id=device, device_id_type=MESH)
    greeted = 3
    for own, size, stride in zip(coords, lines, strides):
        for there, exists in ((me - stride, own > 0), (me + stride, own < size - 1)):
            @pl.when(exists)
            def _():
                for device in (there, there + 1 - 2 * core):
                    pl.semaphore_signal(barrier, inc=1, device_id=(sec, device), device_id_type=MESH)

            greeted = greeted + 2 * exists.astype(jnp.int32)

    for ref in (xs, ds):
        for i in (0, side + 1):
            ref[i] = jnp.zeros((group, 3 * ch), BF16)
    xt[:, 0 : 2 * group] = jnp.zeros((ch, 2 * group), BF16)
    xt[:, (side + 1) * 2 * group : (side + 2) * 2 * group] = jnp.zeros((ch, 2 * group), BF16)
    pad[...] = jnp.zeros_like(pad)
    bsum[...] = jnp.zeros_like(bsum)

    def spread(ref, begin, end, lane=0):
        lanes = slice(lane, lane + ref.shape[-1])
        for i in range(begin, end):
            pad[i * group : i * group + cells, lanes] = ref[i].astype(F32).reshape(cells, ref.shape[-1])
        return pad[begin * group : end * group, lanes]

    def gather(ref, begin, end, value, order=lambda i: i, columns=slice(0, ch)):
        for i in range(begin, end):
            at = (i - begin) * group
            part = value[at : at + cells, :].reshape(side, frames, value.shape[1])
            ref[order(i), :, :, columns] = part.astype(BF16)

    def rounded(v):
        ids = lax.broadcasted_iota(jnp.int32, v.shape, 0)
        return jnp.where(lax.rem(ids, group) < cells, v, 0.0).astype(BF16).astype(F32)

    def moved(v, slots):
        if slots:
            v = pltpu.roll(v, slots * frames % v.shape[0], 0)
        return v.astype(BF16).reshape(v.shape[0] // group, group, v.shape[1])

    def put_inputs(begin, end, v):
        for b in range(3):
            xs[begin + 1 : end + 1, :, b * ch : (b + 1) * ch] = moved(v, 1 - b)
        xc[begin:end, 0] = moved(v, 0)

    def put_deltas(begin, end, v, lane=0):
        for b in range(3):
            at = pl.multiple_of(b * ch + lane, 128)
            ds[begin + 1 : end + 1, :, pl.ds(at, v.shape[1])] = moved(v, b - 1)

    def put_halves(begin, end, which, v):
        for b in range(3):
            wd[begin:end, which, :, half * b : half * (b + 1)] = moved(v, b - 1)
        bsum[0:1, :] += jnp.sum(v, axis=0, keepdims=True)

    def product(source, factor, begin, end, sign, columns=slice(0, ch), ready=lambda a: None):
        count = (end - begin) * group
        total = jnp.zeros((count, columns.stop - columns.start), F32)
        for a in range(3):
            ready(a)
            at = begin + 1 + sign * (a - 1)
            total += jnp.dot(source[at : at + end - begin].reshape(count, 3 * ch), factor[3 * ch * a : 3 * ch * (a + 1), columns],
                             preferred_element_type=F32)
        return total

    def conv(begin, end, columns=slice(0, ch), ready=lambda a: None):
        return product(xs, w, begin, end, 1, columns, ready) + bias_ref[:, columns]

    def conv_back(begin, end):
        return product(ds, wt, begin, end, -1)

    def transpose_w(a):
        for k in range(3 * a, 3 * a + 3):
            at = slice(ch * k, ch * (k + 1))
            wt[at, :] = w[at, :].T

    def ahead(k, columns=slice(0, ch)):
        rows = pl.ds(AHEAD[k], AHEAD[k + 1] - AHEAD[k])
        return pltpu.make_async_remote_copy(
            src_ref=sent.at[rows, :, :, columns], dst_ref=arrived.at[rows, :, :, columns],
            send_sem=ahead_send.at[0], recv_sem=ahead_recv.at[k], device_id=across, device_id_type=MESH)

    def back(k, which):
        rows = pl.ds(BACK[k], BACK[k + 1] - BACK[k])
        lane = pl.multiple_of(half * (core if which == 0 else 1 - core), 128)
        return pltpu.make_async_remote_copy(
            src_ref=sent.at[rows, :, :, pl.ds(lane, half)], dst_ref=returned.at[which, rows],
            send_sem=back_send.at[0], recv_sem=back_recv.at[k],
            device_id=(across, aslant)[which], device_id_type=MESH)

    def share_inputs(k):
        rows = pl.ds(AHEAD[k], AHEAD[k + 1] - AHEAD[k])
        return pltpu.make_async_remote_copy(
            src_ref=xc.at[rows, 0], dst_ref=xc.at[rows, 1], send_sem=xc_send.at[0], recv_sem=xc_recv.at[k],
            device_id=twin, device_id_type=MESH)

    def share_pre():
        lane = pl.multiple_of(half * (1 - core), 128)
        return pltpu.make_async_remote_copy(
            src_ref=pre.at[:, pl.ds(lane, half)], dst_ref=other_pre, send_sem=pre_sem.at[0], recv_sem=pre_sem.at[1],
            device_id=twin, device_id_type=MESH)

    def share_deltas(k, begin, end, source):
        return pltpu.make_async_remote_copy(
            src_ref=source, dst_ref=do.at[begin:end],
            send_sem=do_send.at[0], recv_sem=do_recv.at[k], device_id=twin, device_id_type=MESH)

    def other_deltas(k, begin, end):
        share_deltas(k, begin, end, do.at[begin:end]).wait_recv()
        return do[begin:end].reshape((end - begin) * group, half).astype(F32)

    def transpose_inputs():
        for k in range(len(AHEAD) - 1):
            share_inputs(k).wait_recv()
        for begin in range(0, side, 2):
            end = min(begin + 2, side)
            part = xc[begin:end].reshape((end - begin) * 2 * group, ch)
            xt[:, (begin + 1) * 2 * group : (end + 1) * 2 * group] = part.T

    def weight_term(a, begin, end, fresh=False):
        wide = 2 * group
        term = jnp.dot(xt[:, (begin + a) * wide : (end + a) * wide], wd[begin:end].reshape((end - begin) * wide, 3 * half),
                       preferred_element_type=F32)
        for b in range(3):
            at = pl.ds(pl.multiple_of(ch * (3 * tap(a) + b), ch), ch)
            part = term[:, half * b : half * (b + 1)]
            grad[at, :] = part if fresh else grad[at, :] + part

    def sigmoid(v):
        return 1.0 / (1.0 + jnp.exp(-v))

    for k in range(3):
        load_small(k).wait()

    def ahead_rows(k, columns=slice(0, ch), ready=lambda a: None):
        begin, end = AHEAD[k], AHEAD[k + 1]
        v = conv(begin, end, columns, ready)
        s = sigmoid(v)
        gather(sent, begin, end, v * s, columns=columns)
        pre[begin * group : end * group, columns] = s * (1.0 + v * (1.0 - s))

    @pl.when(first)
    def _():
        wait_rows(0)
        put_inputs(0, first_rows, spread(xin, 0, first_rows))
        ahead_rows(0, slice(0, half), lambda a: load_w(0, a).wait())

    @pl.when(jnp.logical_not(first))
    def _():
        ids = lax.rem(lax.broadcasted_iota(jnp.int32, (group, ch), 0), frames)
        per_row = jnp.zeros((group, ch), F32)
        for f in range(frames):
            clip = clips_ref[video_ref[f]].astype(F32)
            per_row = jnp.where(ids == f, 1.0 / jnp.full((1, ch), clip, F32), per_row)
        scale[...] = per_row
        wait_rows(0)

    wait_rows(1)
    pl.semaphore_wait(barrier, greeted)

    back_rows = list(zip(BACK, BACK[1:]))
    final = len(back_rows) - 1

    def returned_deltas(k):
        begin, end = back_rows[k]
        rows = slice(begin * group, end * group)
        both = returned.at[:, begin:end]
        pltpu.make_async_copy(both, both, back_recv.at[k]).wait()
        for which in range(2):
            if which == 0:
                factor = pre[rows, pl.ds(pl.multiple_of(half * core, 128), half)]
            else:
                factor = other_pre[rows, :]
            d = rounded(spread(returned.at[which], begin, end, half * which) * factor)
            put_halves(begin, end, which, d)
        share_deltas(k, begin, end, wd.at[begin:end, 1, :, half : 2 * half]).start()

    def own_deltas(k):
        begin, end = back_rows[k]
        own = wd[begin:end, 0, :, half : 2 * half].reshape((end - begin) * group, half)
        put_deltas(begin, end, own.astype(F32), half * core)

    def input_grad(begin, end, chunks):
        for k in chunks:
            own_deltas(k)
            put_deltas(*back_rows[k], other_deltas(k, *back_rows[k]), half * (1 - core))
        gather(res.at[0], begin, end, conv_back(begin, end), row)

    @pl.when(first)
    def _():
        ahead(0, slice(0, half)).start()
        ahead_rows(0, slice(half, ch), lambda a: load_w(1, a).wait())
        ahead(0, slice(half, ch)).start()
        put_inputs(first_rows, side, spread(xin, first_rows, side))
        share_inputs(0).start()
        for k in range(1, len(AHEAD) - 1):
            ahead_rows(k)
            ahead(k).start()
            share_inputs(k).start()
        share_pre().start()
        for a in range(3):
            transpose_w(a)
        transpose_inputs()
        share_pre().wait_recv()

        for k in range(final):
            returned_deltas(k)
            if k in TERMS:
                for a in range(3):
                    weight_term(a, *TERMS[k], TERMS[k][0] == 0)
            if k in EARLY:
                input_grad(*EARLY[k])
        weight_term(2, REST, BACK[final])

    @pl.when(jnp.logical_not(first))
    def _():
        for a in range(3):
            load_w(0, a).wait()
            load_w(1, a).wait()
            transpose_w(a)
        rows_of = []
        done, next_back = 0, 0
        for k, (begin, end) in enumerate(zip(AHEAD, AHEAD[1:])):
            ahead(k).wait_recv()
            put_inputs(begin, end, spread(arrived, begin, end))
            share_inputs(k).start()
            top = side if end == side else end - 1
            v = conv(done, top)
            s = sigmoid(v)
            g = spread(xin, done, top).reshape(top - done, group, ch) * scale[...]
            d = rounded(g.reshape((top - done) * group, ch) * (s * (1.0 + v * (1.0 - s))))
            put_deltas(done, top, d)
            rows_of.append((done, top))
            begin, done = done, top
            while next_back < len(BACK) - 1 and (BACK[next_back + 1] < done or done == side):
                low, high = BACK[next_back], BACK[next_back + 1]
                gather(sent, low, high, conv_back(low, high))
                for which in range(2):
                    back(next_back, which).start()
                next_back += 1
            lane = pl.multiple_of(ch + half * (1 - core), 128)
            share_deltas(k, begin, done, ds.at[begin + 1 : done + 1, :, pl.ds(lane, half)]).start()
            lane = pl.multiple_of(ch + half * core, 128)
            own = ds[begin + 1 : done + 1, :, pl.ds(lane, half)]
            put_halves(begin, done, 0, own.reshape((done - begin) * group, half).astype(F32))
            gather(res.at[0], begin, done, v * s, row)
        transpose_inputs()
        for k, (begin, end) in enumerate(rows_of):
            put_halves(begin, end, 1, other_deltas(k, begin, end))
        weight_term(2, 0, side, True)

    def rest_of_gradient(a):
        @pl.when(first)
        def _():
            if a == 1:
                returned_deltas(final)
            weight_term(a, REST, side)

        pl.when(jnp.logical_not(first))(lambda: weight_term(a, 0, side, True))

    def arrival_at(piece, stage, slot, side_at):
        size = lines[pieces[piece][3][stage]]
        after = plan.slots(piece, stage) // size
        if size == 2:
            return lax.rem(slot, after)
        own = lax.div(slot, after) == coords[pieces[piece][3][stage]]
        return jnp.where(jnp.logical_and(own, side_at == 1), size * after + lax.rem(slot, after), slot)

    def line_copy(piece, stage, slot, dest, final=False):
        keeper, _, size, order = pieces[piece]
        line = order[stage]
        right = dest > coords[line]
        side_at = jnp.where(right, 0, 1)
        to = me + jnp.where(right, strides[line], -strides[line])
        if final:
            to = to - core + keeper
            at = 0 if lines[line] == 2 else side_at
            target, sem = last_in[piece].at[at, core], last_recv[piece].at[at]
        else:
            there = dest == coords[line] + jnp.where(right, 1, -1)
            after = plan.slots(piece, stage) // lines[line]
            if lines[line] == 2:
                at = lax.rem(slot, after)
            else:
                second = jnp.logical_and(there, jnp.logical_not(right))
                at = jnp.where(second, lines[line] * after + lax.rem(slot, after), slot)
            target, sem = in_bufs[piece][stage].at[at], line_recv[piece][stage].at[at]
        return pltpu.make_async_remote_copy(
            src_ref=out_bufs[piece][stage].at[slot], dst_ref=target,
            send_sem=line_send[piece].at[stage], recv_sem=sem, device_id=(sec, to), device_id_type=MESH)

    def arrival(piece, stage, slot, side_at):
        at = arrival_at(piece, stage, slot, side_at)
        pltpu.make_async_remote_copy(
            src_ref=out_bufs[piece][stage].at[slot], dst_ref=in_bufs[piece][stage].at[at],
            send_sem=line_send[piece].at[stage], recv_sem=line_recv[piece][stage].at[at],
            device_id=twin, device_id_type=MESH).wait_recv()
        return in_bufs[piece][stage][at].astype(F32)

    def last_arrival(piece, side_at):
        at = 0 if lines[pieces[piece][3][levels - 1]] == 2 else side_at
        both = last_in[piece].at[at]
        pltpu.make_async_copy(both, both, last_recv[piece].at[at]).wait()
        return last_in[piece][at].astype(F32)

    def send_on(piece, stage, slot, dest):
        line = pieces[piece][3][stage]
        if stage < levels - 1:
            line_copy(piece, stage, slot, dest).start()
            return
        next_to = jnp.abs(dest - coords[line]) == 1

        @pl.when(next_to)
        def _():
            line_copy(piece, stage, slot, dest, True).start()

        @pl.when(jnp.logical_not(next_to))
        def _():
            line_copy(piece, stage, slot, dest).start()

    def leaf(piece, slot):
        keeper, begin, size, order = pieces[piece]
        left, chip = slot, 0
        for line in reversed(order):
            chip = chip + lax.rem(left, lines[line]) * (strides[line] // 2)
            left = lax.div(left, lines[line])
        at = chip * plan.rows + keeper * plan.mine + begin
        return grad[pl.ds(pl.multiple_of(at, 8), size), :]

    def dest_slot(piece, stage, rest_slot, step):
        line = pieces[piece][3][stage]
        dest = dest_at(coords[line], step, lines[line])
        after = plan.slots(piece, stage) // lines[line]
        return dest, dest * after + rest_slot

    def is_early(piece, stage):
        return stage == 0 and lines[pieces[piece][3][0]] == 2

    def own_copy(piece, slot):
        keeper, _, _, order = pieces[piece]
        line = order[0]
        to = me + jnp.where(coords[line] == 0, strides[line], -strides[line]) - core + keeper
        return pltpu.make_async_remote_copy(
            src_ref=out_bufs[piece][0].at[slot], dst_ref=own_in[piece].at[core],
            send_sem=line_send[piece].at[0], recv_sem=own_recv.at[piece], device_id=(sec, to), device_id_type=MESH)

    def is_direct(piece):
        return levels == 2 and is_early(piece, 0)

    def early_send(piece, rest_slot, own_block=False):
        dest, slot = dest_slot(piece, 0, rest_slot, 0)
        out_bufs[piece][0][slot] = leaf(piece, slot).astype(plan.wire)
        if own_block:
            own_copy(piece, slot).start()
        else:
            send_on(piece, 0, slot, dest)

    def line_step(piece, stage, rest_slot, step):
        line = pieces[piece][3][stage]
        size, own = lines[line], coords[line]
        if step < size - 1 and is_early(piece, stage):
            return
        dest, slot = dest_slot(piece, stage, rest_slot, step)
        if stage == 0:
            value = leaf(piece, slot)
        elif step == size - 1 and is_direct(piece):
            value = leaf(piece, dest_slot(piece, 0, slot, 1)[1])
        else:
            value = summed(piece, stage - 1, slot)
        total = sums[piece][stage]
        if step < size - 1:
            right = dest > own
            upstream = jnp.logical_or(jnp.logical_and(right, own > 0), jnp.logical_and(jnp.logical_not(right), own < size - 1))

            @pl.when(upstream)
            def _():
                both = value + arrival(piece, stage, slot, jnp.where(right, 0, 1))
                out_bufs[piece][stage][slot] = both.astype(plan.wire)

            @pl.when(jnp.logical_not(upstream))
            def _():
                out_bufs[piece][stage][slot] = value.astype(plan.wire)

            send_on(piece, stage, slot, dest)
        else:
            total[...] = value
            if stage < levels - 1:
                @pl.when(own > 0)
                def _():
                    total[...] += arrival(piece, stage, slot, 0)

                @pl.when(own < size - 1)
                def _():
                    total[...] += arrival(piece, stage, slot, 1)

    pending = set()

    def summed(piece, stage, rest_slot):
        if (piece, stage) not in pending:
            for step in range(lines[pieces[piece][3][stage]]):
                line_step(piece, stage, rest_slot, step)
        return sums[piece][stage][...]

    def keep_copy(piece):
        keeper, begin, size, _ = pieces[piece]
        return pltpu.make_async_remote_copy(
            src_ref=sums[piece][levels - 1],
            dst_ref=wout.at[0, begin : begin + size, half * (1 - keeper) : half * (2 - keeper)],
            send_sem=keep_send.at[0], recv_sem=keep_recv.at[piece % (len(pieces) // 2)], device_id=twin, device_id_type=MESH)

    def keep(piece):
        keeper, begin, size, _ = pieces[piece]

        @pl.when(core == keeper)
        def _():
            wout[0, begin : begin + size, half * keeper : half * (keeper + 1)] = sums[piece][levels - 1][...]

        @pl.when(core != keeper)
        def _():
            keep_copy(piece).start()

    def finish(piece):
        keeper, begin, size, order = pieces[piece]
        line = order[levels - 1]
        own = coords[line]

        @pl.when(core == keeper)
        def _():
            keep_copy(piece).wait_recv()

            def add(side_at):
                both = last_arrival(piece, side_at)
                for columns in range(2):
                    wout[0, begin : begin + size, half * columns : half * (columns + 1)] += both[columns]

            pl.when(own > 0)(lambda: add(0))
            pl.when(own < lines[line] - 1)(lambda: add(1))
            if is_direct(piece):
                pltpu.make_async_copy(own_in[piece], own_in[piece], own_recv.at[piece]).wait()
                for columns in range(2):
                    arrived_part = own_in[piece][columns].astype(F32)
                    wout[0, begin : begin + size, half * columns : half * (columns + 1)] += arrived_part

    def bias_copy(line, right):
        way = 0 if right else 1
        return pltpu.make_async_remote_copy(
            src_ref=bias_in.at[line, 1 + way], dst_ref=bias_in.at[line, 3 + way],
            send_sem=bias_send.at[line, way], recv_sem=bias_recv.at[line, way],
            device_id=(sec, me + strides[line] * (1 if right else -1)), device_id_type=MESH)

    def bias_step(line, step):
        own, size = coords[line], lines[line]
        for right in (True, False):
            way = 0 if right else 1

            @pl.when(own == (step if right else size - 1 - step))
            def _():
                if step > 0:
                    bias_copy(line, right).wait_recv()
                    bias_in[line, 1 + way] = bias_in[line, 0] + bias_in[line, 3 + way]
                else:
                    bias_in[line, 1 + way] = bias_in[line, 0]
                bias_copy(line, right).start()

    def bias_end(line):
        own, size = coords[line], lines[line]
        total = bias_in.at[line + 1, 0]
        total[...] = bias_in[line, 0]
        for right in (True, False):
            way = 0 if right else 1
            exists = own > 0 if right else own < size - 1
            waited = jnp.logical_and(own > 0, own < size - 1)

            @pl.when(exists)
            def _():
                pl.when(jnp.logical_not(waited))(lambda: bias_copy(line, right).wait_recv())
                total[...] += bias_in[line, 3 + way]

        if line == levels - 1:
            bias_swap().start()

    def bias_swap():
        return pltpu.make_async_remote_copy(
            src_ref=bias_in.at[levels, 0], dst_ref=bias_in.at[levels, 1],
            send_sem=bias_send.at[levels, 0], recv_sem=bias_recv.at[levels, 0],
            device_id=twin, device_id_type=MESH)

    bias_work = []
    for line in range(levels):
        for step in range(lines[line] - 1):
            bias_work.append(functools.partial(bias_step, line, step))
        bias_work.append(functools.partial(bias_end, line))

    def some_bias(count=1):
        for work in bias_work[:count]:
            work()
        del bias_work[:count]

    straight = [p for p, piece in enumerate(pieces) if piece[3][0] == levels - 1]
    turned = [p for p in range(len(pieces)) if p not in straight]
    top = levels - 1
    steps = lines[pieces[0][3][top]]

    def early(step):
        def down(piece, stage, slot):
            if stage == 0:
                if is_early(piece, 0):
                    early_send(piece, slot, is_direct(piece) and step == steps - 1)
                return
            for inner in range(lines[pieces[piece][3][stage]]):
                down(piece, stage - 1, dest_slot(piece, stage, slot, inner)[1])

        for piece in straight:
            if levels == 1:
                if step == 0:
                    down(piece, 0, 0)
            else:
                down(piece, top - 1, dest_slot(piece, top, 0, step)[1])

    def turn(step):
        for piece in turned:
            order = pieces[piece][3]
            for outer in range(lines[order[1]]):
                dest, rest_slot = dest_slot(piece, 1, 0, outer)
                line_step(piece, 0, rest_slot, step)
                if step == lines[order[0]] - 1:
                    pending.add((piece, 0))
                    line_step(piece, 1, 0, outer)
                    pending.discard((piece, 0))
            if step == lines[order[0]] - 1:
                keep(piece)

    def go(step):
        for piece in straight:
            line_step(piece, top, 0, step)
            if step == steps - 1:
                keep(piece)

    direct = all(is_direct(piece) for piece in straight)
    turns = lines[pieces[turned[0]][3][0]] if turned else 0
    def late(k):
        pl.when(first)(lambda: input_grad(*LATE[k]))

    staged = levels > 1 and lines[0] >= 4
    ends = jnp.logical_or(coords[0] == 0, coords[0] == lines[0] - 1)
    if staged:
        early(0)
        if turned:
            pl.when(ends)(lambda: turn(0))
    rest_of_gradient(1)
    bias_in[0, 0] = bsum[...]
    some_bias()
    if staged:
        early(1)
    rest_of_gradient(0)
    for step in range(2 if staged else 0, steps - 1):
        early(step)
    if turned:
        if staged:
            pl.when(jnp.logical_not(ends))(lambda: turn(0))
        else:
            turn(0)
    some_bias()

    for step in range(max(steps, turns - 1)):
        if 1 <= step + 1 < turns:
            turn(step + 1)
        some_bias((1, 2)[step] if step < 2 else 0)
        if step == min(1, steps - 2):
            early(steps - 1)
            if direct:
                go(steps - 1)
        if step < steps - direct:
            go(step)
        if step == steps - 2:
            for k in range(len(LATE)):
                late(k)

    for n, piece in enumerate(turned + straight):
        if n == len(pieces) // 2:
            some_bias(len(bias_work))
        finish(piece)

    bias_swap().wait_recv()
    share = ch // plan.dp_count
    place = me * share
    own_half = (place >= half) == (core == 1)
    bias_row = jnp.where(own_half, bias_in[levels, 0], bias_in[levels, 1])
    bout[...] = pltpu.roll(bias_row, lax.rem(half - lax.rem(place, half), half), 1)[0:1, 0:share]

    def sent_all(ref, sem):
        pltpu.make_async_copy(ref, ref, sem).wait()

    bias_swap().wait_send()
    for line, size in enumerate(lines):
        pl.when(coords[line] < size - 1)(lambda: bias_copy(line, True).wait_send())
        pl.when(coords[line] > 0)(lambda: bias_copy(line, False).wait_send())
    sent_all(wout.at[0, :, 0:half], keep_send.at[0])
    for piece, (_, _, _, order) in enumerate(pieces):
        for stage in range(levels):
            count = plan.slots(piece, stage)
            count -= count // lines[order[stage]]
            sent_all(out_bufs[piece][stage].at[pl.ds(0, count)], line_send[piece].at[stage])
    sent_all(xc.at[:, 0], xc_send.at[0])
    sent_all(do, do_send.at[0])
    pl.when(first)(lambda: share_pre().wait_send())
    pl.when(first)(lambda: sent_all(sent, ahead_send.at[0]))
    pl.when(jnp.logical_not(first))(lambda: sent_all(sent, back_send.at[0]))


def body(boundary, weights, biases, frame_video, video_clips):
    boundary = jnp.transpose(boundary, (0, 2, 3, 1, 4))
    _, side, _, frames, ch = boundary.shape
    dp_count = lax.axis_size("dp")
    plan = Plan(frames, side, ch, dp_count)
    half, group = plan.half, plan.group
    vmem = lambda *shape, dtype=BF16: pltpu.VMEM(shape, dtype)
    dma = pltpu.SemaphoreType.DMA
    scratch = [
        vmem(9 * ch, ch),
        vmem(9 * ch, ch),
        vmem(side, side, frames, ch),
        vmem(side + 2, group, 3 * ch),
        vmem(side + 2, group, 3 * ch),
        vmem(side, 2, group, 3 * half),
        vmem(ch, (side + 2) * 2 * group),
        vmem(side, 2, group, ch),
        vmem(side, group, half),
        vmem(9 * ch, half, dtype=F32),
        vmem(side * group, ch, dtype=F32),
        vmem(side * group, half, dtype=F32),
        vmem(side * group, ch, dtype=F32),
        vmem(side, side, frames, ch),
        vmem(side, side, frames, ch),
        vmem(2, side, side, frames, half),
        vmem(8, half, dtype=F32),
        vmem(group, ch, dtype=F32),
        vmem(1, ch, dtype=F32),
        pltpu.SMEM(frame_video.shape, jnp.int32),
        pltpu.SMEM(video_clips.shape, jnp.int32),
        vmem(len(plan.lines) + 1, 5, 8, half, dtype=F32),
    ]
    levels = len(plan.lines)
    wire = plan.wire
    every = [(p, stage) for p in range(len(plan.pieces)) for stage in range(levels)]
    height = lambda p: plan.pieces[p][2]
    scratch += [vmem(plan.slots(p, stage), height(p), half, dtype=wire) for p, stage in every]
    scratch += [vmem(plan.arrivals(p, stage), height(p), half, dtype=wire) for p, stage in every]
    scratch += [vmem(height(p), half, dtype=F32) for p, _ in every]
    ends = [1 if plan.lines[order[-1]] == 2 else 2 for _, _, _, order in plan.pieces]
    scratch += [vmem(end, 2, height(p), half, dtype=wire) for p, end in enumerate(ends)]
    scratch += [vmem(2, height(p), half, dtype=wire) for p in range(len(plan.pieces))]
    scratch += [dma((levels,)) for _ in plan.pieces]
    scratch += [dma((plan.arrivals(p, stage),)) for p, stage in every]
    scratch += [dma((end,)) for end in ends]
    steps, backs = len(AHEAD) - 1, len(BACK) - 1
    most = max(steps, backs)
    keeps = len(plan.pieces) // 2
    shapes = [(2,), (2, 3), (3,), (1,), (steps,), (1,), (backs,), (1,), (steps,), (1,), (most,), (2,), (1,), (keeps,)]
    scratch += [dma(shape) for shape in shapes]
    scratch += [dma((levels + 1, 2)) for _ in range(2)]
    scratch += [dma((len(plan.pieces),))]
    whole = pl.BlockSpec(memory_space=pltpu.VMEM)
    share = 9 * ch // dp_count
    operands = [
        pltpu.with_memory_space_constraint(operand, pltpu.HBM)
        for operand in (boundary, weights, biases, frame_video, video_clips)
    ]
    results, kernel_grad, bias_grad = pl.pallas_call(
        functools.partial(kernel, plan),
        out_shape=(
            pltpu.VMEM(boundary.shape, BF16),
            pltpu.VMEM((1, share, ch), F32),
            pltpu.VMEM((1, ch // dp_count), F32),
        ),
        in_specs=[pl.BlockSpec(memory_space=pltpu.HBM)] * 5,
        out_specs=(whole, whole, whole),
        scratch_shapes=scratch,
        compiler_params=pltpu.CompilerParams(
            collective_id=0, has_side_effects=True, vmem_limit_bytes=VMEM_LIMIT
        ),
    )(*operands)
    return jnp.transpose(results, (0, 3, 1, 2, 4)), kernel_grad, bias_grad


def solution(mesh):
    return jax.shard_map(
        body,
        mesh=mesh,
        in_specs=(
            P("section", "dp", None, None, None),
            P("section", None, None),
            P("section", None),
            P("dp"),
            P(),
        ),
        out_specs=(
            P("section", "dp", None, None, None),
            P("section", "dp", None),
            P("section", "dp"),
        ),
        check_vma=False,
    )
```

```python
import functools

import jax
import jax.numpy as jnp
from jax import lax
from jax.experimental import pallas as pl
from jax.experimental.pallas import tpu as pltpu
from jax.sharding import PartitionSpec as P

VMEM_LIMIT = 54 * 1024 * 1024
MESH = pl.DeviceIdType.MESH
F32 = jnp.float32
BF16 = jnp.bfloat16
SLOTS = 16
AHEAD = (0, 2, 4, 6, 8, 10, 12, 13)
BACK = (0, 2, 4, 6, 8, 10, 12, 13)
TERMS = {1: (0, 4), 3: (4, 8), 4: (8, 10)}
REST = 10
EARLY = {2: (0, 3, (0, 1))}
LATE = ((3, 8, (2, 3, 4)), (8, 13, (5, 6)))


def line_sizes(chips):
    sizes = []
    while chips > 1:
        size = 4 if chips % 4 == 0 else 2 if chips % 2 == 0 else chips
        sizes.append(size)
        chips //= size
    return tuple(sizes)


def dest_at(own, step, size):
    rights = size - 1 - own
    low = jnp.where(step < rights, size - 1 - step, step - rights)
    high = jnp.where(step < own, step, size - 1 - (step - own))
    return jnp.where(own < (size + 1) // 2, low, high)


class Plan:
    def __init__(self, frames, side, channels, dp_count):
        self.frames, self.side, self.channels, self.dp_count = frames, side, channels, dp_count
        self.group = SLOTS * frames
        self.cells = side * frames
        self.half = channels // 2
        self.chips = dp_count // 2
        self.lines = line_sizes(self.chips)
        self.rows = 9 * channels // self.chips
        self.mine = self.rows // 2
        levels = len(self.lines)
        inner_first = tuple(reversed(range(levels)))
        outer_first = tuple(range(levels))
        self.pieces = []
        for keeper in range(2):
            if self.mine % 96 == 0 and self.lines == (4, 2):
                sixteenths = self.mine // 16
                turned = sixteenths // 6
                part = (sixteenths - turned) // 2
                cuts = [(part, inner_first), (sixteenths - turned - part, inner_first), (turned, outer_first)]
                begin = 0
                for size, order in cuts:
                    self.pieces.append((keeper, begin, 16 * size, order))
                    begin += 16 * size
            else:
                self.pieces.append((keeper, 0, self.mine, inner_first))
        self.wire = BF16 if all(size % 16 == 0 and begin % 16 == 0 for _, begin, size, _ in self.pieces) else F32

    def slots(self, piece, stage):
        order = self.pieces[piece][3]
        count = 1
        for line in order[stage:]:
            count *= self.lines[line]
        return count

    def arrivals(self, piece, stage):
        size = self.lines[self.pieces[piece][3][stage]]
        after = self.slots(piece, stage) // size
        return after if size == 2 else (size + 1) * after


def kernel(plan, *refs):
    (x_hbm, w_hbm, bias_hbm, video_hbm, clips_hbm, res, wout, bout,
     w, wt, xin, xs, ds, wd, xt, xc, do, grad, pre, other_pre, pad,
     sent, arrived, returned, bsum, scale, bias_ref, video_ref, clips_ref, bias_in) = refs[:30]
    rest = list(refs[30:])
    lines, pieces = plan.lines, plan.pieces
    levels = len(lines)

    def take(count):
        taken = rest[:count]
        del rest[:count]
        return taken

    out_bufs = [take(levels) for _ in pieces]
    in_bufs = [take(levels) for _ in pieces]
    sums = [take(levels) for _ in pieces]
    last_in = take(len(pieces))
    own_in = take(len(pieces))
    line_send = take(len(pieces))
    line_recv = [take(levels) for _ in pieces]
    last_recv = take(len(pieces))
    (load_sem, wload_sem, small_sem, ahead_send, ahead_recv, back_send, back_recv, xc_send, xc_recv, do_send, do_recv,
     pre_sem,
     keep_send, keep_recv, bias_send, bias_recv, own_recv) = rest

    frames, side, ch, half = plan.frames, plan.side, plan.channels, plan.half
    group, cells = plan.group, plan.cells
    sec = lax.axis_index("section")
    me = lax.axis_index("dp")
    core = lax.rem(me, 2)
    coords, strides = [], []
    stride = plan.dp_count
    for size in lines:
        stride //= size
        strides.append(stride)
        coords.append(lax.rem(lax.div(me, stride), size))
    first = sec == 0
    across = (1 - sec, me)
    twin = (sec, me + 1 - 2 * core)
    aslant = (1 - sec, me + 1 - 2 * core)

    upside = coords[0] >= (lines[0] + 1) // 2

    def row(i):
        return jnp.where(upside, side - 1 - i, i)

    def tap(a):
        return jnp.where(upside, 2 - a, a)

    first_rows = 3

    def load_row(i):
        return pltpu.make_async_copy(x_hbm.at[0, row(i)], xin.at[i], load_sem.at[0 if i < first_rows else 1])

    def wait_rows(k):
        rows = xin.at[0:first_rows] if k == 0 else xin.at[first_rows:side]
        pltpu.make_async_copy(rows, rows, load_sem.at[k]).wait()

    def load_w(n, a):
        part = pl.ds(pl.multiple_of(3 * ch * tap(a), 3 * ch), 3 * ch)
        columns = slice(half * n, half * (n + 1))
        return pltpu.make_async_copy(
            w_hbm.at[0, part, columns], w.at[3 * ch * a : 3 * ch * (a + 1), columns], wload_sem.at[n, a])

    def load_small(k):
        source, to = ((bias_hbm, bias_ref), (video_hbm, video_ref), (clips_hbm, clips_ref))[k]
        return pltpu.make_async_copy(source, to, small_sem.at[k])

    for k in range(3):
        load_small(k).start()
    for i in range(first_rows):
        load_row(i).start()
    for n in range(2):
        for a in range(3):
            load_w(n, a).start()
    for i in range(first_rows, side):
        load_row(i).start()

    barrier = pltpu.get_barrier_semaphore()
    for device in (across, aslant, twin):
        pl.semaphore_signal(barrier, inc=1, device_id=device, device_id_type=MESH)
    greeted = 3
    for own, size, stride in zip(coords, lines, strides):
        for there, exists in ((me - stride, own > 0), (me + stride, own < size - 1)):
            @pl.when(exists)
            def _():
                for device in (there, there + 1 - 2 * core):
                    pl.semaphore_signal(barrier, inc=1, device_id=(sec, device), device_id_type=MESH)

            greeted = greeted + 2 * exists.astype(jnp.int32)

    for ref in (xs, ds):
        for i in (0, side + 1):
            ref[i] = jnp.zeros((group, 3 * ch), BF16)
    xt[:, 0 : 2 * group] = jnp.zeros((ch, 2 * group), BF16)
    xt[:, (side + 1) * 2 * group : (side + 2) * 2 * group] = jnp.zeros((ch, 2 * group), BF16)
    pad[...] = jnp.zeros_like(pad)
    bsum[...] = jnp.zeros_like(bsum)

    def spread(ref, begin, end, lane=0):
        lanes = slice(lane, lane + ref.shape[-1])
        for i in range(begin, end):
            pad[i * group : i * group + cells, lanes] = ref[i].astype(F32).reshape(cells, ref.shape[-1])
        return pad[begin * group : end * group, lanes]

    def gather(ref, begin, end, value, order=lambda i: i, columns=slice(0, ch)):
        for i in range(begin, end):
            at = (i - begin) * group
            part = value[at : at + cells, :].reshape(side, frames, value.shape[1])
            ref[order(i), :, :, columns] = part.astype(BF16)

    def rounded(v):
        ids = lax.broadcasted_iota(jnp.int32, v.shape, 0)
        return jnp.where(lax.rem(ids, group) < cells, v, 0.0).astype(BF16).astype(F32)

    def moved(v, slots):
        if slots:
            v = pltpu.roll(v, slots * frames % v.shape[0], 0)
        return v.astype(BF16).reshape(v.shape[0] // group, group, v.shape[1])

    def put_inputs(begin, end, v):
        for b in range(3):
            xs[begin + 1 : end + 1, :, b * ch : (b + 1) * ch] = moved(v, 1 - b)
        xc[begin:end, 0] = moved(v, 0)

    def put_deltas(begin, end, v, lane=0):
        for b in range(3):
            at = pl.multiple_of(b * ch + lane, 128)
            ds[begin + 1 : end + 1, :, pl.ds(at, v.shape[1])] = moved(v, b - 1)

    def put_halves(begin, end, which, v):
        for b in range(3):
            wd[begin:end, which, :, half * b : half * (b + 1)] = moved(v, b - 1)
        bsum[0:1, :] += jnp.sum(v, axis=0, keepdims=True)

    def product(source, factor, begin, end, sign, columns=slice(0, ch), ready=lambda a: None):
        count = (end - begin) * group
        total = jnp.zeros((count, columns.stop - columns.start), F32)
        for a in range(3):
            ready(a)
            at = begin + 1 + sign * (a - 1)
            total += jnp.dot(source[at : at + end - begin].reshape(count, 3 * ch), factor[3 * ch * a : 3 * ch * (a + 1), columns],
                             preferred_element_type=F32)
        return total

    def conv(begin, end, columns=slice(0, ch), ready=lambda a: None):
        return product(xs, w, begin, end, 1, columns, ready) + bias_ref[:, columns]

    def conv_back(begin, end):
        return product(ds, wt, begin, end, -1)

    def transpose_w(a):
        for k in range(3 * a, 3 * a + 3):
            at = slice(ch * k, ch * (k + 1))
            wt[at, :] = w[at, :].T

    def ahead(k, columns=slice(0, ch)):
        rows = pl.ds(AHEAD[k], AHEAD[k + 1] - AHEAD[k])
        return pltpu.make_async_remote_copy(
            src_ref=sent.at[rows, :, :, columns], dst_ref=arrived.at[rows, :, :, columns],
            send_sem=ahead_send.at[0], recv_sem=ahead_recv.at[k], device_id=across, device_id_type=MESH)

    def back(k, which):
        rows = pl.ds(BACK[k], BACK[k + 1] - BACK[k])
        lane = pl.multiple_of(half * (core if which == 0 else 1 - core), 128)
        return pltpu.make_async_remote_copy(
            src_ref=sent.at[rows, :, :, pl.ds(lane, half)], dst_ref=returned.at[which, rows],
            send_sem=back_send.at[0], recv_sem=back_recv.at[k],
            device_id=(across, aslant)[which], device_id_type=MESH)

    def share_inputs(k):
        rows = pl.ds(AHEAD[k], AHEAD[k + 1] - AHEAD[k])
        return pltpu.make_async_remote_copy(
            src_ref=xc.at[rows, 0], dst_ref=xc.at[rows, 1], send_sem=xc_send.at[0], recv_sem=xc_recv.at[k],
            device_id=twin, device_id_type=MESH)

    def share_pre():
        lane = pl.multiple_of(half * (1 - core), 128)
        return pltpu.make_async_remote_copy(
            src_ref=pre.at[:, pl.ds(lane, half)], dst_ref=other_pre, send_sem=pre_sem.at[0], recv_sem=pre_sem.at[1],
            device_id=twin, device_id_type=MESH)

    def share_deltas(k, begin, end, source):
        return pltpu.make_async_remote_copy(
            src_ref=source, dst_ref=do.at[begin:end],
            send_sem=do_send.at[0], recv_sem=do_recv.at[k], device_id=twin, device_id_type=MESH)

    def other_deltas(k, begin, end):
        share_deltas(k, begin, end, do.at[begin:end]).wait_recv()
        return do[begin:end].reshape((end - begin) * group, half).astype(F32)

    def transpose_inputs():
        for k in range(len(AHEAD) - 1):
            share_inputs(k).wait_recv()
        for begin in range(0, side, 2):
            end = min(begin + 2, side)
            part = xc[begin:end].reshape((end - begin) * 2 * group, ch)
            xt[:, (begin + 1) * 2 * group : (end + 1) * 2 * group] = part.T

    def weight_term(a, begin, end, fresh=False):
        wide = 2 * group
        term = jnp.dot(xt[:, (begin + a) * wide : (end + a) * wide], wd[begin:end].reshape((end - begin) * wide, 3 * half),
                       preferred_element_type=F32)
        for b in range(3):
            at = pl.ds(pl.multiple_of(ch * (3 * tap(a) + b), ch), ch)
            part = term[:, half * b : half * (b + 1)]
            grad[at, :] = part if fresh else grad[at, :] + part

    def sigmoid(v):
        return 1.0 / (1.0 + jnp.exp(-v))

    for k in range(3):
        load_small(k).wait()

    def ahead_rows(k, columns=slice(0, ch), ready=lambda a: None):
        begin, end = AHEAD[k], AHEAD[k + 1]
        v = conv(begin, end, columns, ready)
        s = sigmoid(v)
        gather(sent, begin, end, v * s, columns=columns)
        pre[begin * group : end * group, columns] = s * (1.0 + v * (1.0 - s))

    @pl.when(first)
    def _():
        wait_rows(0)
        put_inputs(0, first_rows, spread(xin, 0, first_rows))
        ahead_rows(0, slice(0, half), lambda a: load_w(0, a).wait())

    @pl.when(jnp.logical_not(first))
    def _():
        ids = lax.rem(lax.broadcasted_iota(jnp.int32, (group, ch), 0), frames)
        per_row = jnp.zeros((group, ch), F32)
        for f in range(frames):
            clip = clips_ref[video_ref[f]].astype(F32)
            per_row = jnp.where(ids == f, 1.0 / jnp.full((1, ch), clip, F32), per_row)
        scale[...] = per_row
        wait_rows(0)

    pl.semaphore_wait(barrier, greeted)

    back_rows = list(zip(BACK, BACK[1:]))
    final = len(back_rows) - 1

    def returned_deltas(k):
        begin, end = back_rows[k]
        rows = slice(begin * group, end * group)
        both = returned.at[:, begin:end]
        pltpu.make_async_copy(both, both, back_recv.at[k]).wait()
        for which in range(2):
            if which == 0:
                factor = pre[rows, pl.ds(pl.multiple_of(half * core, 128), half)]
            else:
                factor = other_pre[rows, :]
            d = rounded(spread(returned.at[which], begin, end, half * which) * factor)
            put_halves(begin, end, which, d)
        share_deltas(k, begin, end, wd.at[begin:end, 1, :, half : 2 * half]).start()

    def own_deltas(k):
        begin, end = back_rows[k]
        own = wd[begin:end, 0, :, half : 2 * half].reshape((end - begin) * group, half)
        put_deltas(begin, end, own.astype(F32), half * core)

    def input_grad(begin, end, chunks):
        for k in chunks:
            own_deltas(k)
            put_deltas(*back_rows[k], other_deltas(k, *back_rows[k]), half * (1 - core))
        gather(res.at[0], begin, end, conv_back(begin, end), row)

    @pl.when(first)
    def _():
        ahead(0, slice(0, half)).start()
        ahead_rows(0, slice(half, ch), lambda a: load_w(1, a).wait())
        ahead(0, slice(half, ch)).start()
        wait_rows(1)
        share_inputs(0).start()
        low = first_rows
        for k in range(1, len(AHEAD) - 1):
            high = min(AHEAD[k + 1] + 1, side)
            if high > low:
                put_inputs(low, high, spread(xin, low, high))
                low = high
            ahead_rows(k)
            ahead(k).start()
            share_inputs(k).start()
        share_pre().start()
        for a in range(3):
            transpose_w(a)
        transpose_inputs()
        share_pre().wait_recv()

        for k in range(final):
            returned_deltas(k)
            if k in TERMS:
                for a in range(3):
                    weight_term(a, *TERMS[k], TERMS[k][0] == 0)
            if k in EARLY:
                input_grad(*EARLY[k])
        weight_term(2, REST, BACK[final])

    @pl.when(jnp.logical_not(first))
    def _():
        for a in range(3):
            load_w(0, a).wait()
            load_w(1, a).wait()
            transpose_w(a)
        wait_rows(1)
        rows_of = []
        done, next_back = 0, 0
        for k, (begin, end) in enumerate(zip(AHEAD, AHEAD[1:])):
            ahead(k).wait_recv()
            put_inputs(begin, end, spread(arrived, begin, end))
            share_inputs(k).start()
            top = side if end == side else end - 1
            v = conv(done, top)
            s = sigmoid(v)
            g = spread(xin, done, top).reshape(top - done, group, ch) * scale[...]
            d = rounded(g.reshape((top - done) * group, ch) * (s * (1.0 + v * (1.0 - s))))
            put_deltas(done, top, d)
            rows_of.append((done, top))
            begin, done = done, top
            while next_back < len(BACK) - 1 and (BACK[next_back + 1] < done or done == side):
                low, high = BACK[next_back], BACK[next_back + 1]
                gather(sent, low, high, conv_back(low, high))
                for which in range(2):
                    back(next_back, which).start()
                next_back += 1
            lane = pl.multiple_of(ch + half * (1 - core), 128)
            share_deltas(k, begin, done, ds.at[begin + 1 : done + 1, :, pl.ds(lane, half)]).start()
            lane = pl.multiple_of(ch + half * core, 128)
            own = ds[begin + 1 : done + 1, :, pl.ds(lane, half)]
            put_halves(begin, done, 0, own.reshape((done - begin) * group, half).astype(F32))
            gather(res.at[0], begin, done, v * s, row)
        transpose_inputs()
        for k, (begin, end) in enumerate(rows_of):
            put_halves(begin, end, 1, other_deltas(k, begin, end))
        weight_term(2, 0, side, True)

    def rest_of_gradient(a):
        @pl.when(first)
        def _():
            if a == 1:
                returned_deltas(final)
            weight_term(a, REST, side)

        pl.when(jnp.logical_not(first))(lambda: weight_term(a, 0, side, True))

    def arrival_at(piece, stage, slot, side_at):
        size = lines[pieces[piece][3][stage]]
        after = plan.slots(piece, stage) // size
        if size == 2:
            return lax.rem(slot, after)
        own = lax.div(slot, after) == coords[pieces[piece][3][stage]]
        return jnp.where(jnp.logical_and(own, side_at == 1), size * after + lax.rem(slot, after), slot)

    def line_copy(piece, stage, slot, dest, final=False):
        keeper, _, size, order = pieces[piece]
        line = order[stage]
        right = dest > coords[line]
        side_at = jnp.where(right, 0, 1)
        to = me + jnp.where(right, strides[line], -strides[line])
        if final:
            to = to - core + keeper
            at = 0 if lines[line] == 2 else side_at
            target, sem = last_in[piece].at[at, core], last_recv[piece].at[at]
        else:
            there = dest == coords[line] + jnp.where(right, 1, -1)
            after = plan.slots(piece, stage) // lines[line]
            if lines[line] == 2:
                at = lax.rem(slot, after)
            else:
                second = jnp.logical_and(there, jnp.logical_not(right))
                at = jnp.where(second, lines[line] * after + lax.rem(slot, after), slot)
            target, sem = in_bufs[piece][stage].at[at], line_recv[piece][stage].at[at]
        return pltpu.make_async_remote_copy(
            src_ref=out_bufs[piece][stage].at[slot], dst_ref=target,
            send_sem=line_send[piece].at[stage], recv_sem=sem, device_id=(sec, to), device_id_type=MESH)

    def arrival(piece, stage, slot, side_at):
        at = arrival_at(piece, stage, slot, side_at)
        pltpu.make_async_remote_copy(
            src_ref=out_bufs[piece][stage].at[slot], dst_ref=in_bufs[piece][stage].at[at],
            send_sem=line_send[piece].at[stage], recv_sem=line_recv[piece][stage].at[at],
            device_id=twin, device_id_type=MESH).wait_recv()
        return in_bufs[piece][stage][at].astype(F32)

    def last_arrival(piece, side_at):
        at = 0 if lines[pieces[piece][3][levels - 1]] == 2 else side_at
        both = last_in[piece].at[at]
        pltpu.make_async_copy(both, both, last_recv[piece].at[at]).wait()
        return last_in[piece][at].astype(F32)

    def send_on(piece, stage, slot, dest):
        line = pieces[piece][3][stage]
        if stage < levels - 1:
            line_copy(piece, stage, slot, dest).start()
            return
        next_to = jnp.abs(dest - coords[line]) == 1

        @pl.when(next_to)
        def _():
            line_copy(piece, stage, slot, dest, True).start()

        @pl.when(jnp.logical_not(next_to))
        def _():
            line_copy(piece, stage, slot, dest).start()

    def leaf(piece, slot):
        keeper, begin, size, order = pieces[piece]
        left, chip = slot, 0
        for line in reversed(order):
            chip = chip + lax.rem(left, lines[line]) * (strides[line] // 2)
            left = lax.div(left, lines[line])
        at = chip * plan.rows + keeper * plan.mine + begin
        return grad[pl.ds(pl.multiple_of(at, 8), size), :]

    def dest_slot(piece, stage, rest_slot, step):
        line = pieces[piece][3][stage]
        dest = dest_at(coords[line], step, lines[line])
        after = plan.slots(piece, stage) // lines[line]
        return dest, dest * after + rest_slot

    def is_early(piece, stage):
        return stage == 0 and lines[pieces[piece][3][0]] == 2

    def own_copy(piece, slot):
        keeper, _, _, order = pieces[piece]
        line = order[0]
        to = me + jnp.where(coords[line] == 0, strides[line], -strides[line]) - core + keeper
        return pltpu.make_async_remote_copy(
            src_ref=out_bufs[piece][0].at[slot], dst_ref=own_in[piece].at[core],
            send_sem=line_send[piece].at[0], recv_sem=own_recv.at[piece], device_id=(sec, to), device_id_type=MESH)

    def is_direct(piece):
        return levels == 2 and is_early(piece, 0)

    def early_send(piece, rest_slot, own_block=False):
        dest, slot = dest_slot(piece, 0, rest_slot, 0)
        out_bufs[piece][0][slot] = leaf(piece, slot).astype(plan.wire)
        if own_block:
            own_copy(piece, slot).start()
        else:
            send_on(piece, 0, slot, dest)

    def line_step(piece, stage, rest_slot, step):
        line = pieces[piece][3][stage]
        size, own = lines[line], coords[line]
        if step < size - 1 and is_early(piece, stage):
            return
        dest, slot = dest_slot(piece, stage, rest_slot, step)
        if stage == 0:
            value = leaf(piece, slot)
        elif step == size - 1 and is_direct(piece):
            value = leaf(piece, dest_slot(piece, 0, slot, 1)[1])
        else:
            value = summed(piece, stage - 1, slot)
        total = sums[piece][stage]
        if step < size - 1:
            right = dest > own
            upstream = jnp.logical_or(jnp.logical_and(right, own > 0), jnp.logical_and(jnp.logical_not(right), own < size - 1))

            @pl.when(upstream)
            def _():
                both = value + arrival(piece, stage, slot, jnp.where(right, 0, 1))
                out_bufs[piece][stage][slot] = both.astype(plan.wire)

            @pl.when(jnp.logical_not(upstream))
            def _():
                out_bufs[piece][stage][slot] = value.astype(plan.wire)

            send_on(piece, stage, slot, dest)
        else:
            total[...] = value
            if stage < levels - 1:
                @pl.when(own > 0)
                def _():
                    total[...] += arrival(piece, stage, slot, 0)

                @pl.when(own < size - 1)
                def _():
                    total[...] += arrival(piece, stage, slot, 1)

    pending = set()

    def summed(piece, stage, rest_slot):
        if (piece, stage) not in pending:
            for step in range(lines[pieces[piece][3][stage]]):
                line_step(piece, stage, rest_slot, step)
        return sums[piece][stage][...]

    def keep_copy(piece):
        keeper, begin, size, _ = pieces[piece]
        return pltpu.make_async_remote_copy(
            src_ref=sums[piece][levels - 1],
            dst_ref=wout.at[0, begin : begin + size, half * (1 - keeper) : half * (2 - keeper)],
            send_sem=keep_send.at[0], recv_sem=keep_recv.at[piece % (len(pieces) // 2)], device_id=twin, device_id_type=MESH)

    def keep(piece):
        keeper, begin, size, _ = pieces[piece]

        @pl.when(core == keeper)
        def _():
            wout[0, begin : begin + size, half * keeper : half * (keeper + 1)] = sums[piece][levels - 1][...]

        @pl.when(core != keeper)
        def _():
            keep_copy(piece).start()

    def finish(piece):
        keeper, begin, size, order = pieces[piece]
        line = order[levels - 1]
        own = coords[line]

        @pl.when(core == keeper)
        def _():
            keep_copy(piece).wait_recv()

            def add(side_at):
                both = last_arrival(piece, side_at)
                for columns in range(2):
                    wout[0, begin : begin + size, half * columns : half * (columns + 1)] += both[columns]

            pl.when(own > 0)(lambda: add(0))
            pl.when(own < lines[line] - 1)(lambda: add(1))
            if is_direct(piece):
                pltpu.make_async_copy(own_in[piece], own_in[piece], own_recv.at[piece]).wait()
                for columns in range(2):
                    arrived_part = own_in[piece][columns].astype(F32)
                    wout[0, begin : begin + size, half * columns : half * (columns + 1)] += arrived_part

    def bias_copy(line, right):
        way = 0 if right else 1
        return pltpu.make_async_remote_copy(
            src_ref=bias_in.at[line, 1 + way], dst_ref=bias_in.at[line, 3 + way],
            send_sem=bias_send.at[line, way], recv_sem=bias_recv.at[line, way],
            device_id=(sec, me + strides[line] * (1 if right else -1)), device_id_type=MESH)

    def bias_step(line, step):
        own, size = coords[line], lines[line]
        for right in (True, False):
            way = 0 if right else 1

            @pl.when(own == (step if right else size - 1 - step))
            def _():
                if step > 0:
                    bias_copy(line, right).wait_recv()
                    bias_in[line, 1 + way] = bias_in[line, 0] + bias_in[line, 3 + way]
                else:
                    bias_in[line, 1 + way] = bias_in[line, 0]
                bias_copy(line, right).start()

    def bias_end(line):
        own, size = coords[line], lines[line]
        total = bias_in.at[line + 1, 0]
        total[...] = bias_in[line, 0]
        for right in (True, False):
            way = 0 if right else 1
            exists = own > 0 if right else own < size - 1
            waited = jnp.logical_and(own > 0, own < size - 1)

            @pl.when(exists)
            def _():
                pl.when(jnp.logical_not(waited))(lambda: bias_copy(line, right).wait_recv())
                total[...] += bias_in[line, 3 + way]

        if line == levels - 1:
            bias_swap().start()

    def bias_swap():
        return pltpu.make_async_remote_copy(
            src_ref=bias_in.at[levels, 0], dst_ref=bias_in.at[levels, 1],
            send_sem=bias_send.at[levels, 0], recv_sem=bias_recv.at[levels, 0],
            device_id=twin, device_id_type=MESH)

    bias_work = []
    for line in range(levels):
        for step in range(lines[line] - 1):
            bias_work.append(functools.partial(bias_step, line, step))
        bias_work.append(functools.partial(bias_end, line))

    def some_bias(count=1):
        for work in bias_work[:count]:
            work()
        del bias_work[:count]

    straight = [p for p, piece in enumerate(pieces) if piece[3][0] == levels - 1]
    turned = [p for p in range(len(pieces)) if p not in straight]
    top = levels - 1
    steps = lines[pieces[0][3][top]]

    def early(step):
        def down(piece, stage, slot):
            if stage == 0:
                if is_early(piece, 0):
                    early_send(piece, slot, is_direct(piece) and step == steps - 1)
                return
            for inner in range(lines[pieces[piece][3][stage]]):
                down(piece, stage - 1, dest_slot(piece, stage, slot, inner)[1])

        for piece in straight:
            if levels == 1:
                if step == 0:
                    down(piece, 0, 0)
            else:
                down(piece, top - 1, dest_slot(piece, top, 0, step)[1])

    def turn(step):
        for piece in turned:
            order = pieces[piece][3]
            for outer in range(lines[order[1]]):
                dest, rest_slot = dest_slot(piece, 1, 0, outer)
                line_step(piece, 0, rest_slot, step)
                if step == lines[order[0]] - 1:
                    pending.add((piece, 0))
                    line_step(piece, 1, 0, outer)
                    pending.discard((piece, 0))
            if step == lines[order[0]] - 1:
                keep(piece)

    def go(step):
        for piece in straight:
            line_step(piece, top, 0, step)
            if step == steps - 1:
                keep(piece)

    direct = all(is_direct(piece) for piece in straight)
    turns = lines[pieces[turned[0]][3][0]] if turned else 0
    def late(k):
        pl.when(first)(lambda: input_grad(*LATE[k]))

    staged = levels > 1 and lines[0] >= 4
    ends = jnp.logical_or(coords[0] == 0, coords[0] == lines[0] - 1)
    if staged:
        early(0)
        if turned:
            pl.when(ends)(lambda: turn(0))
    rest_of_gradient(1)
    bias_in[0, 0] = bsum[...]
    some_bias()
    if staged:
        early(1)
    rest_of_gradient(0)
    for step in range(2 if staged else 0, steps - 1):
        early(step)
    if turned:
        if staged:
            pl.when(jnp.logical_not(ends))(lambda: turn(0))
        else:
            turn(0)
    some_bias()

    for step in range(max(steps, turns - 1)):
        if 1 <= step + 1 < turns:
            turn(step + 1)
        some_bias((1, 2)[step] if step < 2 else 0)
        if step == min(1, steps - 2):
            early(steps - 1)
            if direct:
                go(steps - 1)
        if step < steps - direct:
            go(step)
        if step == steps - 2:
            for k in range(len(LATE)):
                late(k)

    for n, piece in enumerate(turned + straight):
        if n == len(pieces) // 2:
            some_bias(len(bias_work))
        finish(piece)

    bias_swap().wait_recv()
    share = ch // plan.dp_count
    place = me * share
    own_half = (place >= half) == (core == 1)
    bias_row = jnp.where(own_half, bias_in[levels, 0], bias_in[levels, 1])
    bout[...] = pltpu.roll(bias_row, lax.rem(half - lax.rem(place, half), half), 1)[0:1, 0:share]

    def sent_all(ref, sem):
        pltpu.make_async_copy(ref, ref, sem).wait()

    bias_swap().wait_send()
    for line, size in enumerate(lines):
        pl.when(coords[line] < size - 1)(lambda: bias_copy(line, True).wait_send())
        pl.when(coords[line] > 0)(lambda: bias_copy(line, False).wait_send())
    sent_all(wout.at[0, :, 0:half], keep_send.at[0])
    for piece, (_, _, _, order) in enumerate(pieces):
        for stage in range(levels):
            count = plan.slots(piece, stage)
            count -= count // lines[order[stage]]
            sent_all(out_bufs[piece][stage].at[pl.ds(0, count)], line_send[piece].at[stage])
    sent_all(xc.at[:, 0], xc_send.at[0])
    sent_all(do, do_send.at[0])
    pl.when(first)(lambda: share_pre().wait_send())
    pl.when(first)(lambda: sent_all(sent, ahead_send.at[0]))
    pl.when(jnp.logical_not(first))(lambda: sent_all(sent, back_send.at[0]))


def body(boundary, weights, biases, frame_video, video_clips):
    boundary = jnp.transpose(boundary, (0, 2, 3, 1, 4))
    _, side, _, frames, ch = boundary.shape
    dp_count = lax.axis_size("dp")
    plan = Plan(frames, side, ch, dp_count)
    half, group = plan.half, plan.group
    vmem = lambda *shape, dtype=BF16: pltpu.VMEM(shape, dtype)
    dma = pltpu.SemaphoreType.DMA
    scratch = [
        vmem(9 * ch, ch),
        vmem(9 * ch, ch),
        vmem(side, side, frames, ch),
        vmem(side + 2, group, 3 * ch),
        vmem(side + 2, group, 3 * ch),
        vmem(side, 2, group, 3 * half),
        vmem(ch, (side + 2) * 2 * group),
        vmem(side, 2, group, ch),
        vmem(side, group, half),
        vmem(9 * ch, half, dtype=F32),
        vmem(side * group, ch, dtype=F32),
        vmem(side * group, half, dtype=F32),
        vmem(side * group, ch, dtype=F32),
        vmem(side, side, frames, ch),
        vmem(side, side, frames, ch),
        vmem(2, side, side, frames, half),
        vmem(8, half, dtype=F32),
        vmem(group, ch, dtype=F32),
        vmem(1, ch, dtype=F32),
        pltpu.SMEM(frame_video.shape, jnp.int32),
        pltpu.SMEM(video_clips.shape, jnp.int32),
        vmem(len(plan.lines) + 1, 5, 8, half, dtype=F32),
    ]
    levels = len(plan.lines)
    wire = plan.wire
    every = [(p, stage) for p in range(len(plan.pieces)) for stage in range(levels)]
    height = lambda p: plan.pieces[p][2]
    scratch += [vmem(plan.slots(p, stage), height(p), half, dtype=wire) for p, stage in every]
    scratch += [vmem(plan.arrivals(p, stage), height(p), half, dtype=wire) for p, stage in every]
    scratch += [vmem(height(p), half, dtype=F32) for p, _ in every]
    ends = [1 if plan.lines[order[-1]] == 2 else 2 for _, _, _, order in plan.pieces]
    scratch += [vmem(end, 2, height(p), half, dtype=wire) for p, end in enumerate(ends)]
    scratch += [vmem(2, height(p), half, dtype=wire) for p in range(len(plan.pieces))]
    scratch += [dma((levels,)) for _ in plan.pieces]
    scratch += [dma((plan.arrivals(p, stage),)) for p, stage in every]
    scratch += [dma((end,)) for end in ends]
    steps, backs = len(AHEAD) - 1, len(BACK) - 1
    most = max(steps, backs)
    keeps = len(plan.pieces) // 2
    shapes = [(2,), (2, 3), (3,), (1,), (steps,), (1,), (backs,), (1,), (steps,), (1,), (most,), (2,), (1,), (keeps,)]
    scratch += [dma(shape) for shape in shapes]
    scratch += [dma((levels + 1, 2)) for _ in range(2)]
    scratch += [dma((len(plan.pieces),))]
    whole = pl.BlockSpec(memory_space=pltpu.VMEM)
    share = 9 * ch // dp_count
    operands = [
        pltpu.with_memory_space_constraint(operand, pltpu.HBM)
        for operand in (boundary, weights, biases, frame_video, video_clips)
    ]
    results, kernel_grad, bias_grad = pl.pallas_call(
        functools.partial(kernel, plan),
        out_shape=(
            pltpu.VMEM(boundary.shape, BF16),
            pltpu.VMEM((1, share, ch), F32),
            pltpu.VMEM((1, ch // dp_count), F32),
        ),
        in_specs=[pl.BlockSpec(memory_space=pltpu.HBM)] * 5,
        out_specs=(whole, whole, whole),
        scratch_shapes=scratch,
        compiler_params=pltpu.CompilerParams(
            collective_id=0, has_side_effects=True, vmem_limit_bytes=VMEM_LIMIT
        ),
    )(*operands)
    return jnp.transpose(results, (0, 3, 1, 2, 4)), kernel_grad, bias_grad


def solution(mesh):
    return jax.shard_map(
        body,
        mesh=mesh,
        in_specs=(
            P("section", "dp", None, None, None),
            P("section", None, None),
            P("section", None),
            P("dp"),
            P(),
        ),
        out_specs=(
            P("section", "dp", None, None, None),
            P("section", "dp", None),
            P("section", "dp"),
        ),
        check_vma=False,
    )
```

```python
import functools

import jax
import jax.numpy as jnp
from jax import lax
from jax.experimental import pallas as pl
from jax.experimental.pallas import tpu as pltpu
from jax.sharding import PartitionSpec as P

VMEM_LIMIT = 54 * 1024 * 1024
MESH = pl.DeviceIdType.MESH
F32 = jnp.float32
BF16 = jnp.bfloat16
SLOTS = 16
AHEAD = (0, 2, 4, 6, 8, 10, 12, 13)
BACK = (0, 2, 4, 6, 8, 10, 12, 13)
TERMS = {1: (0, 4), 3: (4, 8), 4: (8, 10)}
REST = 10
EARLY = {2: (0, 3, (0, 1))}
LATE = ((3, 8, (2, 3, 4)), (8, 13, (5, 6)))


def line_sizes(chips):
    sizes = []
    while chips > 1:
        size = 4 if chips % 4 == 0 else 2 if chips % 2 == 0 else chips
        sizes.append(size)
        chips //= size
    return tuple(sizes)


def dest_at(own, step, size):
    rights = size - 1 - own
    low = jnp.where(step < rights, size - 1 - step, step - rights)
    high = jnp.where(step < own, step, size - 1 - (step - own))
    return jnp.where(own < (size + 1) // 2, low, high)


class Plan:
    def __init__(self, frames, side, channels, dp_count):
        self.frames, self.side, self.channels, self.dp_count = frames, side, channels, dp_count
        self.group = SLOTS * frames
        self.cells = side * frames
        self.half = channels // 2
        self.chips = dp_count // 2
        self.lines = line_sizes(self.chips)
        self.rows = 9 * channels // self.chips
        self.mine = self.rows // 2
        levels = len(self.lines)
        inner_first = tuple(reversed(range(levels)))
        outer_first = tuple(range(levels))
        self.pieces = []
        for keeper in range(2):
            if self.mine % 96 == 0 and self.lines == (4, 2):
                sixteenths = self.mine // 16
                turned = sixteenths // 6
                part = (sixteenths - turned) // 2
                cuts = [(part, inner_first), (sixteenths - turned - part, inner_first), (turned, outer_first)]
                begin = 0
                for size, order in cuts:
                    self.pieces.append((keeper, begin, 16 * size, order))
                    begin += 16 * size
            else:
                self.pieces.append((keeper, 0, self.mine, inner_first))
        self.wire = BF16 if all(size % 16 == 0 and begin % 16 == 0 for _, begin, size, _ in self.pieces) else F32

    def slots(self, piece, stage):
        order = self.pieces[piece][3]
        count = 1
        for line in order[stage:]:
            count *= self.lines[line]
        return count

    def arrivals(self, piece, stage):
        size = self.lines[self.pieces[piece][3][stage]]
        after = self.slots(piece, stage) // size
        if size == 2:
            return after
        return size * after if stage == len(self.lines) - 1 else (size + 1) * after


def kernel(plan, *refs):
    (x_hbm, w_hbm, bias_hbm, video_hbm, clips_hbm, res, wout, bout,
     w, wt, xin, xs, ds, wd, xt, xc, do, grad, pre, other_pre, pad,
     sent, arrived, returned, bsum, scale, bias_ref, video_ref, clips_ref, bias_in) = refs[:30]
    rest = list(refs[30:])
    lines, pieces = plan.lines, plan.pieces
    levels = len(lines)

    def take(count):
        taken = rest[:count]
        del rest[:count]
        return taken

    out_bufs = [take(levels) for _ in pieces]
    in_bufs = [take(levels) for _ in pieces]
    sums = [take(levels) for _ in pieces]
    last_in = take(len(pieces))
    own_in = take(len(pieces))
    line_send, = take(1)
    line_recv = [take(levels) for _ in pieces]
    last_recv = take(len(pieces))
    (load_sem, wload_sem, small_sem, ahead_send, ahead_recv, back_send, back_recv, xc_send, xc_recv, do_send, do_recv,
     pre_sem,
     keep_send, keep_recv, bias_send, bias_recv, own_recv) = rest

    frames, side, ch, half = plan.frames, plan.side, plan.channels, plan.half
    group, cells = plan.group, plan.cells
    sec = lax.axis_index("section")
    me = lax.axis_index("dp")
    core = lax.rem(me, 2)
    coords, strides = [], []
    stride = plan.dp_count
    for size in lines:
        stride //= size
        strides.append(stride)
        coords.append(lax.rem(lax.div(me, stride), size))
    first = sec == 0
    across = (1 - sec, me)
    twin = (sec, me + 1 - 2 * core)
    aslant = (1 - sec, me + 1 - 2 * core)

    upside = coords[0] >= (lines[0] + 1) // 2

    def row(i):
        return jnp.where(upside, side - 1 - i, i)

    def tap(a):
        return jnp.where(upside, 2 - a, a)

    first_rows = 3

    def load_row(i):
        return pltpu.make_async_copy(x_hbm.at[0, row(i)], xin.at[i], load_sem.at[0 if i < first_rows else 1])

    def wait_rows(k):
        rows = xin.at[0:first_rows] if k == 0 else xin.at[first_rows:side]
        pltpu.make_async_copy(rows, rows, load_sem.at[k]).wait()

    def load_w(n, a):
        part = pl.ds(pl.multiple_of(3 * ch * tap(a), 3 * ch), 3 * ch)
        columns = slice(half * n, half * (n + 1))
        return pltpu.make_async_copy(
            w_hbm.at[0, part, columns], w.at[3 * ch * a : 3 * ch * (a + 1), columns], wload_sem.at[n, a])

    def load_small(k):
        source, to = ((bias_hbm, bias_ref), (video_hbm, video_ref), (clips_hbm, clips_ref))[k]
        return pltpu.make_async_copy(source, to, small_sem.at[k])

    for k in range(3):
        load_small(k).start()
    for i in range(first_rows):
        load_row(i).start()
    for n in range(2):
        for a in range(3):
            load_w(n, a).start()
    for i in range(first_rows, side):
        load_row(i).start()

    barrier = pltpu.get_barrier_semaphore()
    for device in (across, aslant, twin):
        pl.semaphore_signal(barrier, inc=1, device_id=device, device_id_type=MESH)
    greeted = 3
    for own, size, stride in zip(coords, lines, strides):
        for there, exists in ((me - stride, own > 0), (me + stride, own < size - 1)):
            @pl.when(exists)
            def _():
                for device in (there, there + 1 - 2 * core):
                    pl.semaphore_signal(barrier, inc=1, device_id=(sec, device), device_id_type=MESH)

            greeted = greeted + 2 * exists.astype(jnp.int32)

    for ref in (xs, ds):
        for i in (0, side + 1):
            ref[i] = jnp.zeros((group, 3 * ch), BF16)
    xt[:, 0 : 2 * group] = jnp.zeros((ch, 2 * group), BF16)
    xt[:, (side + 1) * 2 * group : (side + 2) * 2 * group] = jnp.zeros((ch, 2 * group), BF16)
    pad[...] = jnp.zeros_like(pad)
    bsum[...] = jnp.zeros_like(bsum)

    def spread(ref, begin, end, lane=0):
        lanes = slice(lane, lane + ref.shape[-1])
        for i in range(begin, end):
            pad[i * group : i * group + cells, lanes] = ref[i].astype(F32).reshape(cells, ref.shape[-1])
        return pad[begin * group : end * group, lanes]

    def gather(ref, begin, end, value, order=lambda i: i, columns=slice(0, ch)):
        for i in range(begin, end):
            at = (i - begin) * group
            part = value[at : at + cells, :].reshape(side, frames, value.shape[1])
            ref[order(i), :, :, columns] = part.astype(BF16)

    def rounded(v):
        ids = lax.broadcasted_iota(jnp.int32, v.shape, 0)
        return jnp.where(lax.rem(ids, group) < cells, v, 0.0).astype(BF16).astype(F32)

    def moved(v, slots):
        if slots:
            v = pltpu.roll(v, slots * frames % v.shape[0], 0)
        return v.astype(BF16).reshape(v.shape[0] // group, group, v.shape[1])

    def put_inputs(begin, end, v):
        for b in range(3):
            xs[begin + 1 : end + 1, :, b * ch : (b + 1) * ch] = moved(v, 1 - b)
        xc[begin:end, 0] = moved(v, 0)

    def put_deltas(begin, end, v, lane=0):
        for b in range(3):
            at = pl.multiple_of(b * ch + lane, 128)
            ds[begin + 1 : end + 1, :, pl.ds(at, v.shape[1])] = moved(v, b - 1)

    def put_halves(begin, end, which, v):
        for b in range(3):
            wd[begin:end, which, :, half * b : half * (b + 1)] = moved(v, b - 1)
        bsum[0:1, :] += jnp.sum(v, axis=0, keepdims=True)

    def product(source, factor, begin, end, sign, columns=slice(0, ch), ready=lambda a: None):
        count = (end - begin) * group
        total = jnp.zeros((count, columns.stop - columns.start), F32)
        for a in range(3):
            ready(a)
            at = begin + 1 + sign * (a - 1)
            total += jnp.dot(source[at : at + end - begin].reshape(count, 3 * ch), factor[3 * ch * a : 3 * ch * (a + 1), columns],
                             preferred_element_type=F32)
        return total

    def conv(begin, end, columns=slice(0, ch), ready=lambda a: None):
        return product(xs, w, begin, end, 1, columns, ready) + bias_ref[:, columns]

    def conv_back(begin, end):
        return product(ds, wt, begin, end, -1)

    def transpose_w(a):
        for k in range(3 * a, 3 * a + 3):
            at = slice(ch * k, ch * (k + 1))
            wt[at, :] = w[at, :].T

    def ahead(k, columns=slice(0, ch)):
        rows = pl.ds(AHEAD[k], AHEAD[k + 1] - AHEAD[k])
        return pltpu.make_async_remote_copy(
            src_ref=sent.at[rows, :, :, columns], dst_ref=arrived.at[rows, :, :, columns],
            send_sem=ahead_send.at[0], recv_sem=ahead_recv.at[k], device_id=across, device_id_type=MESH)

    def back(k, which):
        rows = pl.ds(BACK[k], BACK[k + 1] - BACK[k])
        lane = pl.multiple_of(half * (core if which == 0 else 1 - core), 128)
        return pltpu.make_async_remote_copy(
            src_ref=sent.at[rows, :, :, pl.ds(lane, half)], dst_ref=returned.at[which, rows],
            send_sem=back_send.at[0], recv_sem=back_recv.at[k],
            device_id=(across, aslant)[which], device_id_type=MESH)

    def share_inputs(k):
        rows = pl.ds(AHEAD[k], AHEAD[k + 1] - AHEAD[k])
        return pltpu.make_async_remote_copy(
            src_ref=xc.at[rows, 0], dst_ref=xc.at[rows, 1], send_sem=xc_send.at[0], recv_sem=xc_recv.at[0],
            device_id=twin, device_id_type=MESH)

    def share_pre():
        lane = pl.multiple_of(half * (1 - core), 128)
        return pltpu.make_async_remote_copy(
            src_ref=pre.at[:, pl.ds(lane, half)], dst_ref=other_pre, send_sem=pre_sem.at[0], recv_sem=pre_sem.at[1],
            device_id=twin, device_id_type=MESH)

    def share_deltas(k, begin, end, source):
        return pltpu.make_async_remote_copy(
            src_ref=source, dst_ref=do.at[begin:end],
            send_sem=do_send.at[0], recv_sem=do_recv.at[k], device_id=twin, device_id_type=MESH)

    def wait_deltas(k, begin, end):
        theirs = do.at[begin:end]
        pltpu.make_async_copy(theirs, theirs, do_recv.at[k]).wait()

    def other_deltas(begin, end):
        return do[begin:end].reshape((end - begin) * group, half).astype(F32)

    def transpose_inputs():
        theirs = xc.at[:, 1]
        pltpu.make_async_copy(theirs, theirs, xc_recv.at[0]).wait()
        for begin in range(0, side, 2):
            end = min(begin + 2, side)
            part = xc[begin:end].reshape((end - begin) * 2 * group, ch)
            xt[:, (begin + 1) * 2 * group : (end + 1) * 2 * group] = part.T

    def weight_term(a, begin, end, fresh=False):
        wide = 2 * group
        term = jnp.dot(xt[:, (begin + a) * wide : (end + a) * wide], wd[begin:end].reshape((end - begin) * wide, 3 * half),
                       preferred_element_type=F32)
        for b in range(3):
            at = pl.ds(pl.multiple_of(ch * (3 * tap(a) + b), ch), ch)
            part = term[:, half * b : half * (b + 1)]
            grad[at, :] = part if fresh else grad[at, :] + part

    def sigmoid(v):
        return 1.0 / (1.0 + jnp.exp(-v))

    for k in range(3):
        load_small(k).wait()

    def ahead_rows(k, columns=slice(0, ch), ready=lambda a: None):
        begin, end = AHEAD[k], AHEAD[k + 1]
        v = conv(begin, end, columns, ready)
        s = sigmoid(v)
        gather(sent, begin, end, v * s, columns=columns)
        pre[begin * group : end * group, columns] = s * (1.0 + v * (1.0 - s))

    @pl.when(first)
    def _():
        wait_rows(0)
        put_inputs(0, first_rows, spread(xin, 0, first_rows))
        ahead_rows(0, slice(0, half), lambda a: load_w(0, a).wait())

    @pl.when(jnp.logical_not(first))
    def _():
        ids = lax.rem(lax.broadcasted_iota(jnp.int32, (group, ch), 0), frames)
        per_row = jnp.zeros((group, ch), F32)
        for f in range(frames):
            clip = clips_ref[video_ref[f]].astype(F32)
            per_row = jnp.where(ids == f, 1.0 / jnp.full((1, ch), clip, F32), per_row)
        scale[...] = per_row
        wait_rows(0)

    pl.semaphore_wait(barrier, greeted)

    back_rows = list(zip(BACK, BACK[1:]))
    final = len(back_rows) - 1

    def returned_deltas(k):
        begin, end = back_rows[k]
        rows = slice(begin * group, end * group)
        both = returned.at[:, begin:end]
        pltpu.make_async_copy(both, both, back_recv.at[k]).wait()
        for which in range(2):
            if which == 0:
                factor = pre[rows, pl.ds(pl.multiple_of(half * core, 128), half)]
            else:
                factor = other_pre[rows, :]
            d = rounded(spread(returned.at[which], begin, end, half * which) * factor)
            put_halves(begin, end, which, d)
        use = [k in chunks for chunks in uses].index(True)
        share_deltas(use, begin, end, wd.at[begin:end, 1, :, half : 2 * half]).start()

    def own_deltas(k):
        begin, end = back_rows[k]
        own = wd[begin:end, 0, :, half : 2 * half].reshape((end - begin) * group, half)
        put_deltas(begin, end, own.astype(F32), half * core)

    uses = [part[2] for part in list(EARLY.values()) + list(LATE)]

    def input_grad(begin, end, chunks):
        wait_deltas(uses.index(chunks), back_rows[chunks[0]][0], back_rows[chunks[-1]][1])
        for k in chunks:
            own_deltas(k)
            put_deltas(*back_rows[k], other_deltas(*back_rows[k]), half * (1 - core))
        gather(res.at[0], begin, end, conv_back(begin, end), row)

    @pl.when(first)
    def _():
        ahead(0, slice(0, half)).start()
        ahead_rows(0, slice(half, ch), lambda a: load_w(1, a).wait())
        ahead(0, slice(half, ch)).start()
        wait_rows(1)
        share_inputs(0).start()
        low = first_rows
        for k in range(1, len(AHEAD) - 1):
            high = min(AHEAD[k + 1] + 1, side)
            if high > low:
                put_inputs(low, high, spread(xin, low, high))
                low = high
            ahead_rows(k)
            ahead(k).start()
            share_inputs(k).start()
        share_pre().start()
        for a in range(3):
            transpose_w(a)
        transpose_inputs()
        share_pre().wait_recv()

        for k in range(final):
            returned_deltas(k)
            if k in TERMS:
                for a in range(3):
                    weight_term(a, *TERMS[k], TERMS[k][0] == 0)
            if k in EARLY:
                input_grad(*EARLY[k])
        weight_term(2, REST, BACK[final])

    @pl.when(jnp.logical_not(first))
    def _():
        for a in range(3):
            load_w(0, a).wait()
            load_w(1, a).wait()
            transpose_w(a)
        wait_rows(1)
        rows_of = []
        done, next_back = 0, 0
        for k, (begin, end) in enumerate(zip(AHEAD, AHEAD[1:])):
            ahead(k).wait_recv()
            put_inputs(begin, end, spread(arrived, begin, end))
            share_inputs(k).start()
            top = side if end == side else end - 1
            v = conv(done, top)
            s = sigmoid(v)
            g = spread(xin, done, top).reshape(top - done, group, ch) * scale[...]
            d = rounded(g.reshape((top - done) * group, ch) * (s * (1.0 + v * (1.0 - s))))
            put_deltas(done, top, d)
            rows_of.append((done, top))
            begin, done = done, top
            while next_back < len(BACK) - 1 and (BACK[next_back + 1] < done or done == side):
                low, high = BACK[next_back], BACK[next_back + 1]
                gather(sent, low, high, conv_back(low, high))
                for which in range(2):
                    back(next_back, which).start()
                next_back += 1
            lane = pl.multiple_of(ch + half * (1 - core), 128)
            share_deltas(0, begin, done, ds.at[begin + 1 : done + 1, :, pl.ds(lane, half)]).start()
            lane = pl.multiple_of(ch + half * core, 128)
            own = ds[begin + 1 : done + 1, :, pl.ds(lane, half)]
            put_halves(begin, done, 0, own.reshape((done - begin) * group, half).astype(F32))
            gather(res.at[0], begin, done, v * s, row)
        transpose_inputs()
        wait_deltas(0, 0, side)
        for begin, end in rows_of:
            put_halves(begin, end, 1, other_deltas(begin, end))
        weight_term(2, 0, side, True)

    def rest_of_gradient(a):
        @pl.when(first)
        def _():
            if a == 1:
                returned_deltas(final)
            weight_term(a, REST, side)

        pl.when(jnp.logical_not(first))(lambda: weight_term(a, 0, side, True))

    def arrival_at(piece, stage, slot, side_at):
        size = lines[pieces[piece][3][stage]]
        after = plan.slots(piece, stage) // size
        if size == 2:
            return lax.rem(slot, after)
        own = lax.div(slot, after) == coords[pieces[piece][3][stage]]
        return jnp.where(jnp.logical_and(own, side_at == 1), size * after + lax.rem(slot, after), slot)

    def line_copy(piece, stage, slot, dest, final=False):
        keeper, _, size, order = pieces[piece]
        line = order[stage]
        right = dest > coords[line]
        side_at = jnp.where(right, 0, 1)
        to = me + jnp.where(right, strides[line], -strides[line])
        if final:
            to = to - core + keeper
            at = 0 if lines[line] == 2 else side_at
            target, sem = last_in[piece].at[at, core], last_recv[piece].at[at]
        else:
            there = dest == coords[line] + jnp.where(right, 1, -1)
            after = plan.slots(piece, stage) // lines[line]
            if lines[line] == 2:
                at = lax.rem(slot, after)
            else:
                second = jnp.logical_and(there, jnp.logical_not(right))
                at = jnp.where(second, lines[line] * after + lax.rem(slot, after), slot)
            target, sem = in_bufs[piece][stage].at[at], line_recv[piece][stage].at[at]
        return pltpu.make_async_remote_copy(
            src_ref=out_bufs[piece][stage].at[slot], dst_ref=target,
            send_sem=line_send.at[0], recv_sem=sem, device_id=(sec, to), device_id_type=MESH)

    def arrival(piece, stage, slot, side_at):
        at = arrival_at(piece, stage, slot, side_at)
        pltpu.make_async_remote_copy(
            src_ref=out_bufs[piece][stage].at[slot], dst_ref=in_bufs[piece][stage].at[at],
            send_sem=line_send.at[0], recv_sem=line_recv[piece][stage].at[at],
            device_id=twin, device_id_type=MESH).wait_recv()
        return in_bufs[piece][stage][at].astype(F32)

    def last_arrival(piece, side_at):
        at = 0 if lines[pieces[piece][3][levels - 1]] == 2 else side_at
        both = last_in[piece].at[at]
        pltpu.make_async_copy(both, both, last_recv[piece].at[at]).wait()
        return last_in[piece][at].astype(F32)

    def send_on(piece, stage, slot, dest):
        line = pieces[piece][3][stage]
        if stage < levels - 1:
            line_copy(piece, stage, slot, dest).start()
            return
        next_to = jnp.abs(dest - coords[line]) == 1

        @pl.when(next_to)
        def _():
            line_copy(piece, stage, slot, dest, True).start()

        @pl.when(jnp.logical_not(next_to))
        def _():
            line_copy(piece, stage, slot, dest).start()

    def leaf(piece, slot):
        keeper, begin, size, order = pieces[piece]
        left, chip = slot, 0
        for line in reversed(order):
            chip = chip + lax.rem(left, lines[line]) * (strides[line] // 2)
            left = lax.div(left, lines[line])
        at = chip * plan.rows + keeper * plan.mine + begin
        return grad[pl.ds(pl.multiple_of(at, 8), size), :]

    def dest_slot(piece, stage, rest_slot, step):
        line = pieces[piece][3][stage]
        dest = dest_at(coords[line], step, lines[line])
        after = plan.slots(piece, stage) // lines[line]
        return dest, dest * after + rest_slot

    def is_early(piece, stage):
        return stage == 0 and lines[pieces[piece][3][0]] == 2

    def own_copy(piece, slot):
        keeper, _, _, order = pieces[piece]
        line = order[0]
        to = me + jnp.where(coords[line] == 0, strides[line], -strides[line]) - core + keeper
        return pltpu.make_async_remote_copy(
            src_ref=out_bufs[piece][0].at[slot], dst_ref=own_in[piece].at[core],
            send_sem=line_send.at[0], recv_sem=own_recv.at[straight.index(piece)], device_id=(sec, to), device_id_type=MESH)

    def is_direct(piece):
        return levels == 2 and is_early(piece, 0)

    def early_send(piece, rest_slot, own_block=False):
        dest, slot = dest_slot(piece, 0, rest_slot, 0)
        out_bufs[piece][0][slot] = leaf(piece, slot).astype(plan.wire)
        if own_block:
            own_copy(piece, slot).start()
        else:
            send_on(piece, 0, slot, dest)

    def line_step(piece, stage, rest_slot, step):
        line = pieces[piece][3][stage]
        size, own = lines[line], coords[line]
        if step < size - 1 and is_early(piece, stage):
            return
        dest, slot = dest_slot(piece, stage, rest_slot, step)
        if stage == 0:
            value = leaf(piece, slot)
        elif step == size - 1 and is_direct(piece):
            value = leaf(piece, dest_slot(piece, 0, slot, 1)[1])
        else:
            value = summed(piece, stage - 1, slot)
        total = sums[piece][stage]
        if step < size - 1:
            right = dest > own
            upstream = jnp.logical_or(jnp.logical_and(right, own > 0), jnp.logical_and(jnp.logical_not(right), own < size - 1))

            @pl.when(upstream)
            def _():
                both = value + arrival(piece, stage, slot, jnp.where(right, 0, 1))
                out_bufs[piece][stage][slot] = both.astype(plan.wire)

            @pl.when(jnp.logical_not(upstream))
            def _():
                out_bufs[piece][stage][slot] = value.astype(plan.wire)

            send_on(piece, stage, slot, dest)
        else:
            total[...] = value
            if stage < levels - 1:
                @pl.when(own > 0)
                def _():
                    total[...] += arrival(piece, stage, slot, 0)

                @pl.when(own < size - 1)
                def _():
                    total[...] += arrival(piece, stage, slot, 1)

    pending = set()

    def summed(piece, stage, rest_slot):
        if (piece, stage) not in pending:
            for step in range(lines[pieces[piece][3][stage]]):
                line_step(piece, stage, rest_slot, step)
        return sums[piece][stage][...]

    def keep_copy(piece):
        keeper, begin, size, _ = pieces[piece]
        return pltpu.make_async_remote_copy(
            src_ref=sums[piece][levels - 1],
            dst_ref=wout.at[0, begin : begin + size, half * (1 - keeper) : half * (2 - keeper)],
            send_sem=keep_send.at[0], recv_sem=keep_recv.at[piece % (len(pieces) // 2)], device_id=twin, device_id_type=MESH)

    def keep(piece):
        keeper, begin, size, _ = pieces[piece]

        @pl.when(core == keeper)
        def _():
            wout[0, begin : begin + size, half * keeper : half * (keeper + 1)] = sums[piece][levels - 1][...]

        @pl.when(core != keeper)
        def _():
            keep_copy(piece).start()

    def finish(piece):
        keeper, begin, size, order = pieces[piece]
        line = order[levels - 1]
        own = coords[line]

        @pl.when(core == keeper)
        def _():
            keep_copy(piece).wait_recv()

            def add(side_at):
                both = last_arrival(piece, side_at)
                for columns in range(2):
                    wout[0, begin : begin + size, half * columns : half * (columns + 1)] += both[columns]

            pl.when(own > 0)(lambda: add(0))
            pl.when(own < lines[line] - 1)(lambda: add(1))
            if is_direct(piece):
                pltpu.make_async_copy(own_in[piece], own_in[piece], own_recv.at[straight.index(piece)]).wait()
                for columns in range(2):
                    arrived_part = own_in[piece][columns].astype(F32)
                    wout[0, begin : begin + size, half * columns : half * (columns + 1)] += arrived_part

    def bias_copy(line, right):
        way = 0 if right else 1
        return pltpu.make_async_remote_copy(
            src_ref=bias_in.at[line, 1 + way], dst_ref=bias_in.at[line, 3 + way],
            send_sem=bias_send.at[line, way], recv_sem=bias_recv.at[line, way],
            device_id=(sec, me + strides[line] * (1 if right else -1)), device_id_type=MESH)

    def bias_step(line, step):
        own, size = coords[line], lines[line]
        for right in (True, False):
            way = 0 if right else 1

            @pl.when(own == (step if right else size - 1 - step))
            def _():
                if step > 0:
                    bias_copy(line, right).wait_recv()
                    bias_in[line, 1 + way] = bias_in[line, 0] + bias_in[line, 3 + way]
                else:
                    bias_in[line, 1 + way] = bias_in[line, 0]
                bias_copy(line, right).start()

    def bias_end(line):
        own, size = coords[line], lines[line]
        total = bias_in.at[line + 1, 0]
        total[...] = bias_in[line, 0]
        for right in (True, False):
            way = 0 if right else 1
            exists = own > 0 if right else own < size - 1
            waited = jnp.logical_and(own > 0, own < size - 1)

            @pl.when(exists)
            def _():
                pl.when(jnp.logical_not(waited))(lambda: bias_copy(line, right).wait_recv())
                total[...] += bias_in[line, 3 + way]

        if line == levels - 1:
            bias_swap().start()

    def bias_swap():
        return pltpu.make_async_remote_copy(
            src_ref=bias_in.at[levels, 0], dst_ref=bias_in.at[levels, 1],
            send_sem=bias_send.at[levels, 0], recv_sem=bias_recv.at[levels, 0],
            device_id=twin, device_id_type=MESH)

    bias_work = []
    for line in range(levels):
        for step in range(lines[line] - 1):
            bias_work.append(functools.partial(bias_step, line, step))
        bias_work.append(functools.partial(bias_end, line))

    def some_bias(count=1):
        for work in bias_work[:count]:
            work()
        del bias_work[:count]

    straight = [p for p, piece in enumerate(pieces) if piece[3][0] == levels - 1]
    turned = [p for p in range(len(pieces)) if p not in straight]
    top = levels - 1
    steps = lines[pieces[0][3][top]]

    def early(step):
        def down(piece, stage, slot):
            if stage == 0:
                if is_early(piece, 0):
                    early_send(piece, slot, is_direct(piece) and step == steps - 1)
                return
            for inner in range(lines[pieces[piece][3][stage]]):
                down(piece, stage - 1, dest_slot(piece, stage, slot, inner)[1])

        for piece in straight:
            if levels == 1:
                if step == 0:
                    down(piece, 0, 0)
            else:
                down(piece, top - 1, dest_slot(piece, top, 0, step)[1])

    def turn(step):
        for piece in turned:
            order = pieces[piece][3]
            for outer in range(lines[order[1]]):
                dest, rest_slot = dest_slot(piece, 1, 0, outer)
                line_step(piece, 0, rest_slot, step)
                if step == lines[order[0]] - 1:
                    pending.add((piece, 0))
                    line_step(piece, 1, 0, outer)
                    pending.discard((piece, 0))
            if step == lines[order[0]] - 1:
                keep(piece)

    def go(step):
        for piece in straight:
            line_step(piece, top, 0, step)
            if step == steps - 1:
                keep(piece)

    direct = all(is_direct(piece) for piece in straight)
    turns = lines[pieces[turned[0]][3][0]] if turned else 0
    def late(k):
        pl.when(first)(lambda: input_grad(*LATE[k]))

    staged = levels > 1 and lines[0] >= 4
    ends = jnp.logical_or(coords[0] == 0, coords[0] == lines[0] - 1)
    if staged:
        early(0)
        if turned:
            pl.when(ends)(lambda: turn(0))
    rest_of_gradient(1)
    bias_in[0, 0] = bsum[...]
    some_bias()
    if staged:
        early(1)
    rest_of_gradient(0)
    for step in range(2 if staged else 0, steps - 1):
        early(step)
    if turned:
        if staged:
            pl.when(jnp.logical_not(ends))(lambda: turn(0))
        else:
            turn(0)
    some_bias()

    for step in range(max(steps, turns - 1)):
        if 1 <= step + 1 < turns:
            turn(step + 1)
        some_bias((1, 2)[step] if step < 2 else 0)
        if step == min(1, steps - 2):
            early(steps - 1)
            if direct:
                go(steps - 1)
        if step < steps - direct:
            go(step)
        if step == steps - 2:
            for k in range(len(LATE)):
                late(k)

    for n, piece in enumerate(turned + straight):
        if n == len(pieces) // 2:
            some_bias(len(bias_work))
        finish(piece)

    bias_swap().wait_recv()
    share = ch // plan.dp_count
    place = me * share
    own_half = (place >= half) == (core == 1)
    bias_row = jnp.where(own_half, bias_in[levels, 0], bias_in[levels, 1])
    bout[...] = pltpu.roll(bias_row, lax.rem(half - lax.rem(place, half), half), 1)[0:1, 0:share]

    def sent_all(ref, sem):
        pltpu.make_async_copy(ref, ref, sem).wait()

    bias_swap().wait_send()
    for line, size in enumerate(lines):
        pl.when(coords[line] < size - 1)(lambda: bias_copy(line, True).wait_send())
        pl.when(coords[line] > 0)(lambda: bias_copy(line, False).wait_send())
    sent_all(wout.at[0, :, 0:half], keep_send.at[0])
    total = 0
    for piece, (_, _, size, order) in enumerate(pieces):
        for stage in range(levels):
            count = plan.slots(piece, stage)
            total += (count - count // lines[order[stage]]) * size
    sent_all(grad.at[0 : total * jnp.dtype(plan.wire).itemsize // 4], line_send.at[0])
    sent_all(xc.at[:, 0], xc_send.at[0])
    sent_all(do, do_send.at[0])
    pl.when(first)(lambda: share_pre().wait_send())
    pl.when(first)(lambda: sent_all(sent, ahead_send.at[0]))
    pl.when(jnp.logical_not(first))(lambda: sent_all(sent, back_send.at[0]))


def body(boundary, weights, biases, frame_video, video_clips):
    boundary = jnp.transpose(boundary, (0, 2, 3, 1, 4))
    _, side, _, frames, ch = boundary.shape
    dp_count = lax.axis_size("dp")
    plan = Plan(frames, side, ch, dp_count)
    half, group = plan.half, plan.group
    vmem = lambda *shape, dtype=BF16: pltpu.VMEM(shape, dtype)
    dma = pltpu.SemaphoreType.DMA
    scratch = [
        vmem(9 * ch, ch),
        vmem(9 * ch, ch),
        vmem(side, side, frames, ch),
        vmem(side + 2, group, 3 * ch),
        vmem(side + 2, group, 3 * ch),
        vmem(side, 2, group, 3 * half),
        vmem(ch, (side + 2) * 2 * group),
        vmem(side, 2, group, ch),
        vmem(side, group, half),
        vmem(9 * ch, half, dtype=F32),
        vmem(side * group, ch, dtype=F32),
        vmem(side * group, half, dtype=F32),
        vmem(side * group, ch, dtype=F32),
        vmem(side, side, frames, ch),
        vmem(side, side, frames, ch),
        vmem(2, side, side, frames, half),
        vmem(8, half, dtype=F32),
        vmem(group, ch, dtype=F32),
        vmem(1, ch, dtype=F32),
        pltpu.SMEM(frame_video.shape, jnp.int32),
        pltpu.SMEM(video_clips.shape, jnp.int32),
        vmem(len(plan.lines) + 1, 5, 8, half, dtype=F32),
    ]
    levels = len(plan.lines)
    wire = plan.wire
    every = [(p, stage) for p in range(len(plan.pieces)) for stage in range(levels)]
    height = lambda p: plan.pieces[p][2]
    scratch += [vmem(plan.slots(p, stage), height(p), half, dtype=wire) for p, stage in every]
    scratch += [vmem(plan.arrivals(p, stage), height(p), half, dtype=wire) for p, stage in every]
    scratch += [vmem(height(p), half, dtype=F32) for p, _ in every]
    ends = [1 if plan.lines[order[-1]] == 2 else 2 for _, _, _, order in plan.pieces]
    scratch += [vmem(end, 2, height(p), half, dtype=wire) for p, end in enumerate(ends)]
    scratch += [vmem(2, height(p), half, dtype=wire) for p in range(len(plan.pieces))]
    scratch += [dma((1,))]
    scratch += [dma((plan.arrivals(p, stage),)) for p, stage in every]
    scratch += [dma((end,)) for end in ends]
    steps, backs = len(AHEAD) - 1, len(BACK) - 1
    keeps = len(plan.pieces) // 2
    shapes = [(2,), (2, 3), (3,), (1,), (steps,), (1,), (backs,), (1,), (1,), (1,), (len(EARLY) + len(LATE),), (2,), (1,), (keeps,)]
    scratch += [dma(shape) for shape in shapes]
    scratch += [dma((levels + 1, 2)) for _ in range(2)]
    scratch += [dma((len(plan.pieces),))]
    whole = pl.BlockSpec(memory_space=pltpu.VMEM)
    share = 9 * ch // dp_count
    operands = [
        pltpu.with_memory_space_constraint(operand, pltpu.HBM)
        for operand in (boundary, weights, biases, frame_video, video_clips)
    ]
    results, kernel_grad, bias_grad = pl.pallas_call(
        functools.partial(kernel, plan),
        out_shape=(
            pltpu.VMEM(boundary.shape, BF16),
            pltpu.VMEM((1, share, ch), F32),
            pltpu.VMEM((1, ch // dp_count), F32),
        ),
        in_specs=[pl.BlockSpec(memory_space=pltpu.HBM)] * 5,
        out_specs=(whole, whole, whole),
        scratch_shapes=scratch,
        compiler_params=pltpu.CompilerParams(
            collective_id=0, has_side_effects=True, vmem_limit_bytes=VMEM_LIMIT
        ),
    )(*operands)
    return jnp.transpose(results, (0, 3, 1, 2, 4)), kernel_grad, bias_grad


def solution(mesh):
    return jax.shard_map(
        body,
        mesh=mesh,
        in_specs=(
            P("section", "dp", None, None, None),
            P("section", None, None),
            P("section", None),
            P("dp"),
            P(),
        ),
        out_specs=(
            P("section", "dp", None, None, None),
            P("section", "dp", None),
            P("section", "dp"),
        ),
        check_vma=False,
    )
```

```python
import functools

import jax
import jax.numpy as jnp
from jax import lax
from jax.experimental import pallas as pl
from jax.experimental.pallas import tpu as pltpu
from jax.sharding import PartitionSpec as P

VMEM_LIMIT = 54 * 1024 * 1024
MESH = pl.DeviceIdType.MESH
F32 = jnp.float32
BF16 = jnp.bfloat16
SLOTS = 16
AHEAD = (0, 2, 4, 6, 8, 10, 12, 13)
BACK = (0, 2, 4, 6, 8, 10, 12, 13)
TERMS = {1: (0, 4), 3: (4, 8), 4: (8, 10)}
REST = 10
EARLY = {2: (0, 3, (0, 1))}
LATE = ((3, 8, (2, 3, 4)), (8, 13, (5, 6)))


def line_sizes(chips):
    sizes = []
    while chips > 1:
        size = 4 if chips % 4 == 0 else 2 if chips % 2 == 0 else chips
        sizes.append(size)
        chips //= size
    return tuple(sizes)


def dest_at(own, step, size):
    rights = size - 1 - own
    low = jnp.where(step < rights, size - 1 - step, step - rights)
    high = jnp.where(step < own, step, size - 1 - (step - own))
    return jnp.where(own < (size + 1) // 2, low, high)


class Plan:
    def __init__(self, frames, side, channels, dp_count):
        self.frames, self.side, self.channels, self.dp_count = frames, side, channels, dp_count
        self.group = SLOTS * frames
        self.cells = side * frames
        self.half = channels // 2
        self.chips = dp_count // 2
        self.lines = line_sizes(self.chips)
        self.rows = 9 * channels // self.chips
        self.mine = self.rows // 2
        levels = len(self.lines)
        inner_first = tuple(reversed(range(levels)))
        outer_first = tuple(range(levels))
        self.pieces = []
        for keeper in range(2):
            if self.mine % 96 == 0 and self.lines == (4, 2):
                sixteenths = self.mine // 16
                turned = sixteenths // 6
                part = (sixteenths - turned) // 2
                cuts = [(part, inner_first), (sixteenths - turned - part, inner_first), (turned, outer_first)]
                begin = 0
                for size, order in cuts:
                    self.pieces.append((keeper, begin, 16 * size, order))
                    begin += 16 * size
            else:
                self.pieces.append((keeper, 0, self.mine, inner_first))
        self.wire = BF16 if all(size % 16 == 0 and begin % 16 == 0 for _, begin, size, _ in self.pieces) else F32

    def slots(self, piece, stage):
        order = self.pieces[piece][3]
        count = 1
        for line in order[stage:]:
            count *= self.lines[line]
        return count

    def arrivals(self, piece, stage):
        size = self.lines[self.pieces[piece][3][stage]]
        after = self.slots(piece, stage) // size
        if size == 2:
            return after
        return size * after if stage == len(self.lines) - 1 else (size + 1) * after


def kernel(plan, *refs):
    (x_hbm, w_hbm, bias_hbm, video_hbm, clips_hbm, res, wout, bout,
     w, wt, xin, xs, ds, wd, xt, xc, do, grad, pre, other_pre, pad,
     sent, arrived, returned, bsum, scale, bias_ref, video_ref, clips_ref, bias_in) = refs[:30]
    rest = list(refs[30:])
    lines, pieces = plan.lines, plan.pieces
    levels = len(lines)

    def take(count):
        taken = rest[:count]
        del rest[:count]
        return taken

    out_bufs = [take(levels) for _ in pieces]
    in_bufs = [take(levels) for _ in pieces]
    sums = [take(levels) for _ in pieces]
    last_in = take(len(pieces))
    own_in = take(len(pieces))
    line_send, = take(1)
    line_recv = [take(levels) for _ in pieces]
    last_recv = take(len(pieces))
    (load_sem, wload_sem, small_sem, ahead_send, ahead_recv, back_send, back_recv, xc_send, xc_recv, do_send, do_recv,
     pre_sem,
     keep_send, keep_recv, bias_send, bias_recv, own_recv) = rest

    frames, side, ch, half = plan.frames, plan.side, plan.channels, plan.half
    group, cells = plan.group, plan.cells
    sec = lax.axis_index("section")
    me = lax.axis_index("dp")
    core = lax.rem(me, 2)
    coords, strides = [], []
    stride = plan.dp_count
    for size in lines:
        stride //= size
        strides.append(stride)
        coords.append(lax.rem(lax.div(me, stride), size))
    first = sec == 0
    across = (1 - sec, me)
    twin = (sec, me + 1 - 2 * core)
    aslant = (1 - sec, me + 1 - 2 * core)

    upside = coords[0] >= (lines[0] + 1) // 2

    def row(i):
        return jnp.where(upside, side - 1 - i, i)

    def tap(a):
        return jnp.where(upside, 2 - a, a)

    first_rows = 3

    def load_row(i):
        return pltpu.make_async_copy(x_hbm.at[0, row(i)], xin.at[i], load_sem.at[0 if i < first_rows else 1])

    def wait_rows(k):
        rows = xin.at[0:first_rows] if k == 0 else xin.at[first_rows:side]
        pltpu.make_async_copy(rows, rows, load_sem.at[k]).wait()

    def load_w(n, a):
        part = pl.ds(pl.multiple_of(3 * ch * tap(a), 3 * ch), 3 * ch)
        columns = slice(half * n, half * (n + 1))
        return pltpu.make_async_copy(
            w_hbm.at[0, part, columns], w.at[3 * ch * a : 3 * ch * (a + 1), columns], wload_sem.at[n, a])

    def load_small(k):
        source, to = ((bias_hbm, bias_ref), (video_hbm, video_ref), (clips_hbm, clips_ref))[k]
        return pltpu.make_async_copy(source, to, small_sem.at[k])

    for k in range(3):
        load_small(k).start()
    for i in range(first_rows):
        load_row(i).start()
    for n in range(2):
        for a in range(3):
            load_w(n, a).start()
    for i in range(first_rows, side):
        load_row(i).start()

    barrier = pltpu.get_barrier_semaphore()
    for device in (across, aslant, twin):
        pl.semaphore_signal(barrier, inc=1, device_id=device, device_id_type=MESH)
    greeted = 3
    for own, size, stride in zip(coords, lines, strides):
        for there, exists in ((me - stride, own > 0), (me + stride, own < size - 1)):
            @pl.when(exists)
            def _():
                for device in (there, there + 1 - 2 * core):
                    pl.semaphore_signal(barrier, inc=1, device_id=(sec, device), device_id_type=MESH)

            greeted = greeted + 2 * exists.astype(jnp.int32)

    for ref in (xs, ds):
        for i in (0, side + 1):
            ref[i] = jnp.zeros((group, 3 * ch), BF16)
    xt[:, 0 : 2 * group] = jnp.zeros((ch, 2 * group), BF16)
    xt[:, (side + 1) * 2 * group : (side + 2) * 2 * group] = jnp.zeros((ch, 2 * group), BF16)
    pad[...] = jnp.zeros_like(pad)
    bsum[...] = jnp.zeros_like(bsum)

    def spread(ref, begin, end, lane=0):
        lanes = slice(lane, lane + ref.shape[-1])
        for i in range(begin, end):
            pad[i * group : i * group + cells, lanes] = ref[i].astype(F32).reshape(cells, ref.shape[-1])
        return pad[begin * group : end * group, lanes]

    def gather(ref, begin, end, value, order=lambda i: i, columns=slice(0, ch)):
        for i in range(begin, end):
            at = (i - begin) * group
            part = value[at : at + cells, :].reshape(side, frames, value.shape[1])
            ref[order(i), :, :, columns] = part.astype(BF16)

    def rounded(v):
        ids = lax.broadcasted_iota(jnp.int32, v.shape, 0)
        return jnp.where(lax.rem(ids, group) < cells, v, 0.0).astype(BF16).astype(F32)

    def moved(v, slots):
        if slots:
            v = pltpu.roll(v, slots * frames % v.shape[0], 0)
        return v.astype(BF16).reshape(v.shape[0] // group, group, v.shape[1])

    def put_inputs(begin, end, v):
        for b in range(3):
            xs[begin + 1 : end + 1, :, b * ch : (b + 1) * ch] = moved(v, 1 - b)
        xc[begin:end, 0] = moved(v, 0)

    def put_deltas(begin, end, v, lane=0):
        for b in range(3):
            at = pl.multiple_of(b * ch + lane, 128)
            ds[begin + 1 : end + 1, :, pl.ds(at, v.shape[1])] = moved(v, b - 1)

    def put_halves(begin, end, which, v):
        for b in range(3):
            wd[begin:end, which, :, half * b : half * (b + 1)] = moved(v, b - 1)
        bsum[0:1, :] += jnp.sum(v, axis=0, keepdims=True)

    def product(source, factor, begin, end, sign, columns=slice(0, ch), ready=lambda a: None):
        count = (end - begin) * group
        total = jnp.zeros((count, columns.stop - columns.start), F32)
        for a in range(3):
            ready(a)
            at = begin + 1 + sign * (a - 1)
            total += jnp.dot(source[at : at + end - begin].reshape(count, 3 * ch), factor[3 * ch * a : 3 * ch * (a + 1), columns],
                             preferred_element_type=F32)
        return total

    def conv(begin, end, columns=slice(0, ch), ready=lambda a: None):
        return product(xs, w, begin, end, 1, columns, ready) + bias_ref[:, columns]

    def conv_back(begin, end):
        return product(ds, wt, begin, end, -1)

    def transpose_w(a):
        for k in range(3 * a, 3 * a + 3):
            at = slice(ch * k, ch * (k + 1))
            wt[at, :] = w[at, :].T

    def ahead(k, columns=slice(0, ch)):
        rows = pl.ds(AHEAD[k], AHEAD[k + 1] - AHEAD[k])
        return pltpu.make_async_remote_copy(
            src_ref=sent.at[rows, :, :, columns], dst_ref=arrived.at[rows, :, :, columns],
            send_sem=ahead_send.at[0], recv_sem=ahead_recv.at[k], device_id=across, device_id_type=MESH)

    def back(k, which):
        rows = pl.ds(BACK[k], BACK[k + 1] - BACK[k])
        lane = pl.multiple_of(half * (core if which == 0 else 1 - core), 128)
        return pltpu.make_async_remote_copy(
            src_ref=sent.at[rows, :, :, pl.ds(lane, half)], dst_ref=returned.at[which, rows],
            send_sem=back_send.at[0], recv_sem=back_recv.at[k],
            device_id=(across, aslant)[which], device_id_type=MESH)

    def share_inputs(k):
        rows = pl.ds(AHEAD[k], AHEAD[k + 1] - AHEAD[k])
        return pltpu.make_async_remote_copy(
            src_ref=xc.at[rows, 0], dst_ref=xc.at[rows, 1], send_sem=xc_send.at[0], recv_sem=xc_recv.at[0],
            device_id=twin, device_id_type=MESH)

    def share_pre():
        lane = pl.multiple_of(half * (1 - core), 128)
        return pltpu.make_async_remote_copy(
            src_ref=pre.at[:, pl.ds(lane, half)], dst_ref=other_pre, send_sem=pre_sem.at[0], recv_sem=pre_sem.at[1],
            device_id=twin, device_id_type=MESH)

    def share_deltas(k, begin, end, source):
        return pltpu.make_async_remote_copy(
            src_ref=source, dst_ref=do.at[begin:end],
            send_sem=do_send.at[0], recv_sem=do_recv.at[k], device_id=twin, device_id_type=MESH)

    def wait_deltas(k, begin, end):
        theirs = do.at[begin:end]
        pltpu.make_async_copy(theirs, theirs, do_recv.at[k]).wait()

    def other_deltas(begin, end):
        return do[begin:end].reshape((end - begin) * group, half).astype(F32)

    def transpose_inputs():
        theirs = xc.at[:, 1]
        pltpu.make_async_copy(theirs, theirs, xc_recv.at[0]).wait()
        for begin in range(0, side, 2):
            end = min(begin + 2, side)
            part = xc[begin:end].reshape((end - begin) * 2 * group, ch)
            xt[:, (begin + 1) * 2 * group : (end + 1) * 2 * group] = part.T

    def weight_term(a, begin, end, fresh=False):
        wide = 2 * group
        term = jnp.dot(xt[:, (begin + a) * wide : (end + a) * wide], wd[begin:end].reshape((end - begin) * wide, 3 * half),
                       preferred_element_type=F32)
        for b in range(3):
            at = pl.ds(pl.multiple_of(ch * (3 * tap(a) + b), ch), ch)
            part = term[:, half * b : half * (b + 1)]
            grad[at, :] = part if fresh else grad[at, :] + part

    def sigmoid(v):
        return 1.0 / (1.0 + jnp.exp(-v))

    for k in range(3):
        load_small(k).wait()

    def ahead_rows(k, columns=slice(0, ch), ready=lambda a: None):
        begin, end = AHEAD[k], AHEAD[k + 1]
        v = conv(begin, end, columns, ready)
        s = sigmoid(v)
        gather(sent, begin, end, v * s, columns=columns)
        pre[begin * group : end * group, columns] = s * (1.0 + v * (1.0 - s))

    @pl.when(first)
    def _():
        wait_rows(0)
        put_inputs(0, first_rows, spread(xin, 0, first_rows))
        ahead_rows(0, slice(0, half), lambda a: load_w(0, a).wait())

    @pl.when(jnp.logical_not(first))
    def _():
        ids = lax.rem(lax.broadcasted_iota(jnp.int32, (group, ch), 0), frames)
        per_row = jnp.zeros((group, ch), F32)
        for f in range(frames):
            clip = clips_ref[video_ref[f]].astype(F32)
            per_row = jnp.where(ids == f, 1.0 / jnp.full((1, ch), clip, F32), per_row)
        scale[...] = per_row
        wait_rows(0)

    pl.semaphore_wait(barrier, greeted)

    back_rows = list(zip(BACK, BACK[1:]))
    final = len(back_rows) - 1

    def returned_deltas(k):
        begin, end = back_rows[k]
        rows = slice(begin * group, end * group)
        both = returned.at[:, begin:end]
        pltpu.make_async_copy(both, both, back_recv.at[k]).wait()
        for which in range(2):
            if which == 0:
                factor = pre[rows, pl.ds(pl.multiple_of(half * core, 128), half)]
            else:
                factor = other_pre[rows, :]
            d = rounded(spread(returned.at[which], begin, end, half * which) * factor)
            put_halves(begin, end, which, d)
        use = [k in chunks for chunks in uses].index(True)
        share_deltas(use, begin, end, wd.at[begin:end, 1, :, half : 2 * half]).start()

    def own_deltas(k):
        begin, end = back_rows[k]
        own = wd[begin:end, 0, :, half : 2 * half].reshape((end - begin) * group, half)
        put_deltas(begin, end, own.astype(F32), half * core)

    uses = [part[2] for part in list(EARLY.values()) + list(LATE)]

    def input_grad(begin, end, chunks):
        wait_deltas(uses.index(chunks), back_rows[chunks[0]][0], back_rows[chunks[-1]][1])
        for k in chunks:
            own_deltas(k)
            put_deltas(*back_rows[k], other_deltas(*back_rows[k]), half * (1 - core))
        gather(res.at[0], begin, end, conv_back(begin, end), row)

    @pl.when(first)
    def _():
        ahead(0, slice(0, half)).start()
        ahead_rows(0, slice(half, ch), lambda a: load_w(1, a).wait())
        ahead(0, slice(half, ch)).start()
        wait_rows(1)
        share_inputs(0).start()
        low = first_rows
        for k in range(1, len(AHEAD) - 1):
            high = min(AHEAD[k + 1] + 1, side)
            if high > low:
                put_inputs(low, high, spread(xin, low, high))
                low = high
            ahead_rows(k)
            ahead(k).start()
            share_inputs(k).start()
        share_pre().start()
        for a in range(3):
            transpose_w(a)
        transpose_inputs()
        share_pre().wait_recv()

        for k in range(final):
            returned_deltas(k)
            if k in TERMS:
                for a in range(3):
                    weight_term(a, *TERMS[k], TERMS[k][0] == 0)
            if k in EARLY:
                input_grad(*EARLY[k])
        weight_term(2, REST, BACK[final])

    @pl.when(jnp.logical_not(first))
    def _():
        for a in range(3):
            load_w(0, a).wait()
            load_w(1, a).wait()
            transpose_w(a)
        wait_rows(1)
        rows_of = []
        done, next_back = 0, 0
        for k, (begin, end) in enumerate(zip(AHEAD, AHEAD[1:])):
            ahead(k).wait_recv()
            put_inputs(begin, end, spread(arrived, begin, end))
            share_inputs(k).start()
            top = side if end == side else end - 1
            v = conv(done, top)
            s = sigmoid(v)
            g = spread(xin, done, top).reshape(top - done, group, ch) * scale[...]
            d = rounded(g.reshape((top - done) * group, ch) * (s * (1.0 + v * (1.0 - s))))
            put_deltas(done, top, d)
            rows_of.append((done, top))
            begin, done = done, top
            while next_back < len(BACK) - 1 and (BACK[next_back + 1] < done or done == side):
                low, high = BACK[next_back], BACK[next_back + 1]
                gather(sent, low, high, conv_back(low, high))
                for which in (1, 0):
                    back(next_back, which).start()
                next_back += 1
            lane = pl.multiple_of(ch + half * (1 - core), 128)
            share_deltas(0, begin, done, ds.at[begin + 1 : done + 1, :, pl.ds(lane, half)]).start()
            lane = pl.multiple_of(ch + half * core, 128)
            own = ds[begin + 1 : done + 1, :, pl.ds(lane, half)]
            put_halves(begin, done, 0, own.reshape((done - begin) * group, half).astype(F32))
            gather(res.at[0], begin, done, v * s, row)
        transpose_inputs()
        wait_deltas(0, 0, side)
        for begin, end in rows_of:
            put_halves(begin, end, 1, other_deltas(begin, end))
        weight_term(2, 0, side, True)

    def rest_of_gradient(a):
        @pl.when(first)
        def _():
            if a == 1:
                returned_deltas(final)
            weight_term(a, REST, side)

        pl.when(jnp.logical_not(first))(lambda: weight_term(a, 0, side, True))

    def arrival_at(piece, stage, slot, side_at):
        size = lines[pieces[piece][3][stage]]
        after = plan.slots(piece, stage) // size
        if size == 2:
            return lax.rem(slot, after)
        own = lax.div(slot, after) == coords[pieces[piece][3][stage]]
        return jnp.where(jnp.logical_and(own, side_at == 1), size * after + lax.rem(slot, after), slot)

    def line_copy(piece, stage, slot, dest, final=False):
        keeper, _, size, order = pieces[piece]
        line = order[stage]
        right = dest > coords[line]
        side_at = jnp.where(right, 0, 1)
        to = me + jnp.where(right, strides[line], -strides[line])
        if final:
            to = to - core + keeper
            at = 0 if lines[line] == 2 else side_at
            target, sem = last_in[piece].at[at, core], last_recv[piece].at[at]
        else:
            there = dest == coords[line] + jnp.where(right, 1, -1)
            after = plan.slots(piece, stage) // lines[line]
            if lines[line] == 2:
                at = lax.rem(slot, after)
            else:
                second = jnp.logical_and(there, jnp.logical_not(right))
                at = jnp.where(second, lines[line] * after + lax.rem(slot, after), slot)
            target, sem = in_bufs[piece][stage].at[at], line_recv[piece][stage].at[at]
        return pltpu.make_async_remote_copy(
            src_ref=out_bufs[piece][stage].at[slot], dst_ref=target,
            send_sem=line_send.at[0], recv_sem=sem, device_id=(sec, to), device_id_type=MESH)

    def arrival(piece, stage, slot, side_at):
        at = arrival_at(piece, stage, slot, side_at)
        pltpu.make_async_remote_copy(
            src_ref=out_bufs[piece][stage].at[slot], dst_ref=in_bufs[piece][stage].at[at],
            send_sem=line_send.at[0], recv_sem=line_recv[piece][stage].at[at],
            device_id=twin, device_id_type=MESH).wait_recv()
        return in_bufs[piece][stage][at].astype(F32)

    def last_arrival(piece, side_at):
        at = 0 if lines[pieces[piece][3][levels - 1]] == 2 else side_at
        both = last_in[piece].at[at]
        pltpu.make_async_copy(both, both, last_recv[piece].at[at]).wait()
        return last_in[piece][at].astype(F32)

    def send_on(piece, stage, slot, dest):
        line = pieces[piece][3][stage]
        if stage < levels - 1:
            line_copy(piece, stage, slot, dest).start()
            return
        next_to = jnp.abs(dest - coords[line]) == 1

        @pl.when(next_to)
        def _():
            line_copy(piece, stage, slot, dest, True).start()

        @pl.when(jnp.logical_not(next_to))
        def _():
            line_copy(piece, stage, slot, dest).start()

    def leaf(piece, slot):
        keeper, begin, size, order = pieces[piece]
        left, chip = slot, 0
        for line in reversed(order):
            chip = chip + lax.rem(left, lines[line]) * (strides[line] // 2)
            left = lax.div(left, lines[line])
        at = chip * plan.rows + keeper * plan.mine + begin
        return grad[pl.ds(pl.multiple_of(at, 8), size), :]

    def dest_slot(piece, stage, rest_slot, step):
        line = pieces[piece][3][stage]
        dest = dest_at(coords[line], step, lines[line])
        after = plan.slots(piece, stage) // lines[line]
        return dest, dest * after + rest_slot

    def is_early(piece, stage):
        return stage == 0 and lines[pieces[piece][3][0]] == 2

    def own_copy(piece, slot):
        keeper, _, _, order = pieces[piece]
        line = order[0]
        to = me + jnp.where(coords[line] == 0, strides[line], -strides[line]) - core + keeper
        return pltpu.make_async_remote_copy(
            src_ref=out_bufs[piece][0].at[slot], dst_ref=own_in[piece].at[core],
            send_sem=line_send.at[0], recv_sem=own_recv.at[straight.index(piece)], device_id=(sec, to), device_id_type=MESH)

    def is_direct(piece):
        return levels == 2 and is_early(piece, 0)

    def early_send(piece, rest_slot, own_block=False):
        dest, slot = dest_slot(piece, 0, rest_slot, 0)
        out_bufs[piece][0][slot] = leaf(piece, slot).astype(plan.wire)
        if own_block:
            own_copy(piece, slot).start()
        else:
            send_on(piece, 0, slot, dest)

    def line_step(piece, stage, rest_slot, step):
        line = pieces[piece][3][stage]
        size, own = lines[line], coords[line]
        if step < size - 1 and is_early(piece, stage):
            return
        dest, slot = dest_slot(piece, stage, rest_slot, step)
        if stage == 0:
            value = leaf(piece, slot)
        elif step == size - 1 and is_direct(piece):
            value = leaf(piece, dest_slot(piece, 0, slot, 1)[1])
        else:
            value = summed(piece, stage - 1, slot)
        total = sums[piece][stage]
        if step < size - 1:
            right = dest > own
            upstream = jnp.logical_or(jnp.logical_and(right, own > 0), jnp.logical_and(jnp.logical_not(right), own < size - 1))

            @pl.when(upstream)
            def _():
                both = value + arrival(piece, stage, slot, jnp.where(right, 0, 1))
                out_bufs[piece][stage][slot] = both.astype(plan.wire)

            @pl.when(jnp.logical_not(upstream))
            def _():
                out_bufs[piece][stage][slot] = value.astype(plan.wire)

            send_on(piece, stage, slot, dest)
        else:
            total[...] = value
            if stage < levels - 1:
                @pl.when(own > 0)
                def _():
                    total[...] += arrival(piece, stage, slot, 0)

                @pl.when(own < size - 1)
                def _():
                    total[...] += arrival(piece, stage, slot, 1)

    pending = set()

    def summed(piece, stage, rest_slot):
        if (piece, stage) not in pending:
            for step in range(lines[pieces[piece][3][stage]]):
                line_step(piece, stage, rest_slot, step)
        return sums[piece][stage][...]

    def keep_copy(piece):
        keeper, begin, size, _ = pieces[piece]
        return pltpu.make_async_remote_copy(
            src_ref=sums[piece][levels - 1],
            dst_ref=wout.at[0, begin : begin + size, half * (1 - keeper) : half * (2 - keeper)],
            send_sem=keep_send.at[0], recv_sem=keep_recv.at[piece % (len(pieces) // 2)], device_id=twin, device_id_type=MESH)

    def keep(piece):
        keeper, begin, size, _ = pieces[piece]

        @pl.when(core == keeper)
        def _():
            wout[0, begin : begin + size, half * keeper : half * (keeper + 1)] = sums[piece][levels - 1][...]

        @pl.when(core != keeper)
        def _():
            keep_copy(piece).start()

    def finish(piece):
        keeper, begin, size, order = pieces[piece]
        line = order[levels - 1]
        own = coords[line]

        @pl.when(core == keeper)
        def _():
            keep_copy(piece).wait_recv()

            def add(side_at):
                both = last_arrival(piece, side_at)
                for columns in range(2):
                    wout[0, begin : begin + size, half * columns : half * (columns + 1)] += both[columns]

            pl.when(own > 0)(lambda: add(0))
            pl.when(own < lines[line] - 1)(lambda: add(1))
            if is_direct(piece):
                pltpu.make_async_copy(own_in[piece], own_in[piece], own_recv.at[straight.index(piece)]).wait()
                for columns in range(2):
                    arrived_part = own_in[piece][columns].astype(F32)
                    wout[0, begin : begin + size, half * columns : half * (columns + 1)] += arrived_part

    def bias_copy(line, right):
        way = 0 if right else 1
        return pltpu.make_async_remote_copy(
            src_ref=bias_in.at[line, 1 + way], dst_ref=bias_in.at[line, 3 + way],
            send_sem=bias_send.at[line, way], recv_sem=bias_recv.at[line, way],
            device_id=(sec, me + strides[line] * (1 if right else -1)), device_id_type=MESH)

    def bias_step(line, step):
        own, size = coords[line], lines[line]
        for right in (True, False):
            way = 0 if right else 1

            @pl.when(own == (step if right else size - 1 - step))
            def _():
                if step > 0:
                    bias_copy(line, right).wait_recv()
                    bias_in[line, 1 + way] = bias_in[line, 0] + bias_in[line, 3 + way]
                else:
                    bias_in[line, 1 + way] = bias_in[line, 0]
                bias_copy(line, right).start()

    def bias_end(line):
        own, size = coords[line], lines[line]
        total = bias_in.at[line + 1, 0]
        total[...] = bias_in[line, 0]
        for right in (True, False):
            way = 0 if right else 1
            exists = own > 0 if right else own < size - 1
            waited = jnp.logical_and(own > 0, own < size - 1)

            @pl.when(exists)
            def _():
                pl.when(jnp.logical_not(waited))(lambda: bias_copy(line, right).wait_recv())
                total[...] += bias_in[line, 3 + way]

        if line == levels - 1:
            bias_swap().start()

    def bias_swap():
        return pltpu.make_async_remote_copy(
            src_ref=bias_in.at[levels, 0], dst_ref=bias_in.at[levels, 1],
            send_sem=bias_send.at[levels, 0], recv_sem=bias_recv.at[levels, 0],
            device_id=twin, device_id_type=MESH)

    bias_work = []
    for line in range(levels):
        for step in range(lines[line] - 1):
            bias_work.append(functools.partial(bias_step, line, step))
        bias_work.append(functools.partial(bias_end, line))

    def some_bias(count=1):
        for work in bias_work[:count]:
            work()
        del bias_work[:count]

    straight = [p for p, piece in enumerate(pieces) if piece[3][0] == levels - 1]
    turned = [p for p in range(len(pieces)) if p not in straight]
    top = levels - 1
    steps = lines[pieces[0][3][top]]

    def early(step):
        def down(piece, stage, slot):
            if stage == 0:
                if is_early(piece, 0):
                    early_send(piece, slot, is_direct(piece) and step == steps - 1)
                return
            for inner in range(lines[pieces[piece][3][stage]]):
                down(piece, stage - 1, dest_slot(piece, stage, slot, inner)[1])

        for piece in straight:
            if levels == 1:
                if step == 0:
                    down(piece, 0, 0)
            else:
                down(piece, top - 1, dest_slot(piece, top, 0, step)[1])

    def turn(step):
        for piece in turned:
            order = pieces[piece][3]
            for outer in range(lines[order[1]]):
                dest, rest_slot = dest_slot(piece, 1, 0, outer)
                line_step(piece, 0, rest_slot, step)
                if step == lines[order[0]] - 1:
                    pending.add((piece, 0))
                    line_step(piece, 1, 0, outer)
                    pending.discard((piece, 0))
            if step == lines[order[0]] - 1:
                keep(piece)

    def go(step):
        for piece in straight:
            line_step(piece, top, 0, step)
            if step == steps - 1:
                keep(piece)

    direct = all(is_direct(piece) for piece in straight)
    turns = lines[pieces[turned[0]][3][0]] if turned else 0
    def late(k):
        pl.when(first)(lambda: input_grad(*LATE[k]))

    staged = levels > 1 and lines[0] >= 4
    ends = jnp.logical_or(coords[0] == 0, coords[0] == lines[0] - 1)
    if staged:
        early(0)
        if turned:
            pl.when(ends)(lambda: turn(0))
    rest_of_gradient(1)
    bias_in[0, 0] = bsum[...]
    some_bias()
    if staged:
        early(1)
    rest_of_gradient(0)
    for step in range(2 if staged else 0, steps - 1):
        early(step)
    if turned:
        if staged:
            pl.when(jnp.logical_not(ends))(lambda: turn(0))
        else:
            turn(0)
    some_bias()

    for step in range(max(steps, turns - 1)):
        if 1 <= step + 1 < turns:
            turn(step + 1)
        some_bias((1, 2)[step] if step < 2 else 0)
        if step == min(1, steps - 2):
            early(steps - 1)
            if direct:
                go(steps - 1)
        if step < steps - direct:
            go(step)
        if step == steps - 2:
            for k in range(len(LATE)):
                late(k)

    for n, piece in enumerate(turned + straight):
        if n == len(pieces) // 2:
            some_bias(len(bias_work))
        finish(piece)

    bias_swap().wait_recv()
    share = ch // plan.dp_count
    place = me * share
    own_half = (place >= half) == (core == 1)
    bias_row = jnp.where(own_half, bias_in[levels, 0], bias_in[levels, 1])
    bout[...] = pltpu.roll(bias_row, lax.rem(half - lax.rem(place, half), half), 1)[0:1, 0:share]

    def sent_all(ref, sem):
        pltpu.make_async_copy(ref, ref, sem).wait()

    bias_swap().wait_send()
    for line, size in enumerate(lines):
        pl.when(coords[line] < size - 1)(lambda: bias_copy(line, True).wait_send())
        pl.when(coords[line] > 0)(lambda: bias_copy(line, False).wait_send())
    sent_all(wout.at[0, :, 0:half], keep_send.at[0])
    total = 0
    for piece, (_, _, size, order) in enumerate(pieces):
        for stage in range(levels):
            count = plan.slots(piece, stage)
            total += (count - count // lines[order[stage]]) * size
    sent_all(grad.at[0 : total * jnp.dtype(plan.wire).itemsize // 4], line_send.at[0])
    sent_all(xc.at[:, 0], xc_send.at[0])
    sent_all(do, do_send.at[0])
    pl.when(first)(lambda: share_pre().wait_send())
    pl.when(first)(lambda: sent_all(sent, ahead_send.at[0]))
    pl.when(jnp.logical_not(first))(lambda: sent_all(sent, back_send.at[0]))


def body(boundary, weights, biases, frame_video, video_clips):
    boundary = jnp.transpose(boundary, (0, 2, 3, 1, 4))
    _, side, _, frames, ch = boundary.shape
    dp_count = lax.axis_size("dp")
    plan = Plan(frames, side, ch, dp_count)
    half, group = plan.half, plan.group
    vmem = lambda *shape, dtype=BF16: pltpu.VMEM(shape, dtype)
    dma = pltpu.SemaphoreType.DMA
    scratch = [
        vmem(9 * ch, ch),
        vmem(9 * ch, ch),
        vmem(side, side, frames, ch),
        vmem(side + 2, group, 3 * ch),
        vmem(side + 2, group, 3 * ch),
        vmem(side, 2, group, 3 * half),
        vmem(ch, (side + 2) * 2 * group),
        vmem(side, 2, group, ch),
        vmem(side, group, half),
        vmem(9 * ch, half, dtype=F32),
        vmem(side * group, ch, dtype=F32),
        vmem(side * group, half, dtype=F32),
        vmem(side * group, ch, dtype=F32),
        vmem(side, side, frames, ch),
        vmem(side, side, frames, ch),
        vmem(2, side, side, frames, half),
        vmem(8, half, dtype=F32),
        vmem(group, ch, dtype=F32),
        vmem(1, ch, dtype=F32),
        pltpu.SMEM(frame_video.shape, jnp.int32),
        pltpu.SMEM(video_clips.shape, jnp.int32),
        vmem(len(plan.lines) + 1, 5, 8, half, dtype=F32),
    ]
    levels = len(plan.lines)
    wire = plan.wire
    every = [(p, stage) for p in range(len(plan.pieces)) for stage in range(levels)]
    height = lambda p: plan.pieces[p][2]
    scratch += [vmem(plan.slots(p, stage), height(p), half, dtype=wire) for p, stage in every]
    scratch += [vmem(plan.arrivals(p, stage), height(p), half, dtype=wire) for p, stage in every]
    scratch += [vmem(height(p), half, dtype=F32) for p, _ in every]
    ends = [1 if plan.lines[order[-1]] == 2 else 2 for _, _, _, order in plan.pieces]
    scratch += [vmem(end, 2, height(p), half, dtype=wire) for p, end in enumerate(ends)]
    scratch += [vmem(2, height(p), half, dtype=wire) for p in range(len(plan.pieces))]
    scratch += [dma((1,))]
    scratch += [dma((plan.arrivals(p, stage),)) for p, stage in every]
    scratch += [dma((end,)) for end in ends]
    steps, backs = len(AHEAD) - 1, len(BACK) - 1
    keeps = len(plan.pieces) // 2
    shapes = [(2,), (2, 3), (3,), (1,), (steps,), (1,), (backs,), (1,), (1,), (1,), (len(EARLY) + len(LATE),), (2,), (1,), (keeps,)]
    scratch += [dma(shape) for shape in shapes]
    scratch += [dma((levels + 1, 2)) for _ in range(2)]
    scratch += [dma((len(plan.pieces),))]
    whole = pl.BlockSpec(memory_space=pltpu.VMEM)
    share = 9 * ch // dp_count
    operands = [
        pltpu.with_memory_space_constraint(operand, pltpu.HBM)
        for operand in (boundary, weights, biases, frame_video, video_clips)
    ]
    results, kernel_grad, bias_grad = pl.pallas_call(
        functools.partial(kernel, plan),
        out_shape=(
            pltpu.VMEM(boundary.shape, BF16),
            pltpu.VMEM((1, share, ch), F32),
            pltpu.VMEM((1, ch // dp_count), F32),
        ),
        in_specs=[pl.BlockSpec(memory_space=pltpu.HBM)] * 5,
        out_specs=(whole, whole, whole),
        scratch_shapes=scratch,
        compiler_params=pltpu.CompilerParams(
            collective_id=0, has_side_effects=True, vmem_limit_bytes=VMEM_LIMIT
        ),
    )(*operands)
    return jnp.transpose(results, (0, 3, 1, 2, 4)), kernel_grad, bias_grad


def solution(mesh):
    return jax.shard_map(
        body,
        mesh=mesh,
        in_specs=(
            P("section", "dp", None, None, None),
            P("section", None, None),
            P("section", None),
            P("dp"),
            P(),
        ),
        out_specs=(
            P("section", "dp", None, None, None),
            P("section", "dp", None),
            P("section", "dp"),
        ),
        check_vma=False,
    )
```
